32 devices in a mesh: seq: 4 (over z), head: 8 (over y, x, core).
Axes of the slice: x: 2, y: 2, z: 4, core: 2. Of those that a mesh axis runs over, the one named last changes fastest.
Arguments:
- tokens: bfloat16 [128, 3, 2048], P('seq', None, 'head'), may hold values from -6 to 6
- states: float32 [128, 32, 128, 128], P('seq', 'head'), may hold values from -4 to 4
- router_ids: int32 [128, 3, 10], P('seq'), may hold values from 0 to 31, all different within a row; in each aligned block of 96 rows (0 to 95, 96 to 191, ..., all dimensions but the last counted through in order) at most 92 rows name the same one
- router_weights: float32 [128, 3, 10], P('seq'), may hold values from 0.02 to 0.3
- input_gain: float32 [2048], replicated, may hold values from 0.25 to 1.75
- w_query: bfloat16 [2048, 2048], P(None, 'head'), may hold values from -0.125 to 0.125
- w_key: bfloat16 [2048, 2048], P(None, 'head'), may hold values from -0.125 to 0.125
- w_value: bfloat16 [2048, 4096], P(None, 'head'), may hold values from -0.125 to 0.125
- w_zgate: bfloat16 [2048, 4096], P(None, 'head'), may hold values from -0.125 to 0.125
- w_beta: bfloat16 [2048, 32], P(None, 'head'), may hold values from -0.125 to 0.125
- w_alpha: bfloat16 [2048, 32], P(None, 'head'), may hold values from -0.125 to 0.125
- decay_scale: float32 [32], P('head'), may hold values from 0.05 to 2
- dt_bias: float32 [32], P('head'), may hold values from -2 to 1
- gated_gain: float32 [128], replicated, may hold values from 0.25 to 1.75
- w_out: bfloat16 [4096, 2048], P('head'), may hold values from -0.09375 to 0.09375
- post_gain: float32 [2048], replicated, may hold values from 0.25 to 1.75
- w_shared_in: bfloat16 [2048, 1024], P('head'), may hold values from -0.125 to 0.125
- w_shared_out: bfloat16 [512, 2048], P(None, 'head'), may hold values from -0.25 to 0.25
- w_expert_in: bfloat16 [32, 2048, 1024], P(('seq', 'head')), may hold values from -0.125 to 0.125
- w_expert_out: bfloat16 [32, 512, 2048], P(('seq', 'head')), may hold values from -0.25 to 0.25
Outputs:
- layer_out: bfloat16 [128, 3, 2048], P('seq', None, 'head')
- states_out: float32 [128, 32, 128, 128], P('seq', 'head')
The draws below stay inside these ranges and needn't reach their ends.
Inputs may be any that keep to these rules, and one draw needn't show every extreme that they name: `router_ids`: each row names 10 different experts; among the 96 rows of one device (sequence-major order), no expert is named by more than 92 rows, and some expert reaches 92 in some blocks.
All inputs are finite; a program needn't handle non-finite values.
Results may differ from the reference program's by a relative error of at most 0.0061.
Values may be sent and summed in bfloat16 or wider, within the bound.
No kernel may reach another device: no remote copies, remote signals or barrier semaphores. Data moves between devices by JAX's collectives and lax.ppermute only.
A program may use at most 128 MiB of HBM per device.

```python
import math
import jax
import jax.numpy as jnp
import numpy as np
from jax import lax

D = 2048
KH = 16
HV = 32
DK = 128
DV = 128
FE = 512
FS = 512
TOP = 10
S_DEV = 32
STEPS = 3
SEQS = 128
EXPERTS = 32
CAP = 92
N_SEQ = 4


def level_of(key, shape, split, least, high):
    factor_of, own = 1.0, jax.random.fold_in(key, 6)
    for position, blocks in split:
        heights = jnp.exp(jax.random.uniform(jax.random.fold_in(own, position), (blocks,), jnp.float32, least / len(split), high / len(split)))
        factor_of = factor_of * jnp.repeat(heights, shape[position] // blocks).reshape([-1 if axis == position else 1 for axis in range(len(shape))])
    return factor_of


def shared_out(key, own, number, rows, number_of, top, bound, skew):
    ranking = jax.random.permutation(key, number_of)
    packed, ordinary = portions_of(number_of, rows * top, bound, skew, True), portions_of(number_of, rows * top, bound, skew, False)
    places = jnp.arange(number_of)

    def named(tallies, rotation):
        used = int((tallies > 0).sum())
        fixed = max(1, used // 4)
        shifted = fixed + (places - fixed + rotation * (used - fixed)) % max(1, number_of - fixed)
        return jnp.zeros((number_of,), jnp.int32).at[ranking[jnp.where(places < fixed, places, shifted)]].set(jnp.asarray(tallies, jnp.int32))

    tallies = jnp.where(number % 4 == 0, named(packed, number // 4), named(ordinary, number - number // 4 - 1))
    mixed = jax.random.permutation(jax.random.fold_in(own, 3), number_of)
    donor, receiver = mixed[0:number_of // 2 * 2:2], mixed[1:number_of // 2 * 2:2]
    margin = jnp.minimum(tallies[donor] - 1, bound - tallies[receiver]) // 2
    margin = jnp.where((donor == ranking[0]) | (receiver == ranking[0]) | (tallies[receiver] == 0), 0, jnp.maximum(margin, 0))
    shifted = jax.random.randint(jax.random.fold_in(own, 4), (number_of // 2,), 0, 1 << 20) % (margin + 1)
    tallies = tallies.at[donor].add(-shifted).at[receiver].add(shifted)
    members = jnp.searchsorted(jnp.cumsum(tallies), jnp.arange(rows * top), side="right").astype(jnp.int32)
    table = members.reshape(top, rows).T
    table = table[jax.random.permutation(jax.random.fold_in(own, 1), rows)]
    rotation = jax.random.randint(jax.random.fold_in(own, 2), (rows, 1), 0, top)
    return jnp.take_along_axis(table, (jnp.arange(top)[None, :] + rotation) % top, axis=1)


def portions_of(count, total, bound, lean, full):
    weights = [(1 << 20) // math.isqrt(rank ** lean) + 1 for rank in range(1, count + 1)]
    largest = bound if full else min(bound, max(-(-total // count), total * weights[0] // sum(weights)))
    least = 1 if total - largest >= count - 1 else 0
    given, surplus = [largest] + [least] * (count - 1), total - largest - least * (count - 1)
    while surplus > 0:
        movable = [i for i in range(1, count) if given[i] < largest] or [i for i in range(1, count) if given[i] < bound]
        whole, left = sum([weights[i] for i in movable]), surplus
        for i in movable:
            more = min(bound - given[i], max(1, left * weights[i] // whole), surplus)
            given[i] = given[i] + more
            surplus = surplus - more
    return np.array(given)


def normal_values(rng, dims, scale, reach, split=(), kind=jnp.bfloat16):
    level = level_of(rng, dims, split, -0.22, 0.18) if split else 1.0
    array = jax.random.normal(rng, dims, jnp.float32) * scale * level
    return jnp.minimum(jnp.maximum(array, -reach), reach).astype(kind)


def setup_inputs(seed: int = 0) -> dict:
    arg_keys = jax.random.split(jax.random.key(seed), 21)
    tokens = normal_values(arg_keys[0], (SEQS, STEPS, D), 1.0, 6.0, ((0, 4), (2, 8)))
    states = normal_values(arg_keys[1], (SEQS, HV, DK, DV), 0.5, 4.0, ((0, 4), (1, 8)), jnp.float32)
    router_ids_keys = jax.random.split(jax.random.fold_in(arg_keys[2], 1), SEQS * STEPS // (S_DEV * STEPS))
    router_ids_turns = jax.random.permutation(jax.random.fold_in(arg_keys[2], 3), SEQS * STEPS // (S_DEV * STEPS))
    router_ids = jax.vmap(lambda own, number: shared_out(jax.random.fold_in(arg_keys[2], 2), own, number, S_DEV * STEPS, EXPERTS, TOP, CAP, 2))(router_ids_keys, router_ids_turns).reshape((SEQS, STEPS, TOP))
    router_weights = jnp.clip(jnp.exp(math.log(0.3) - 2.7080503 * jax.random.uniform(arg_keys[3], (SEQS, STEPS, TOP), jnp.float32) ** level_of(arg_keys[3], (SEQS, STEPS, TOP), ((0, 4),), -0.2, 0.2)), 0.02, 0.3)
    input_gain = jnp.clip(1.0 + 0.15 * jax.random.normal(arg_keys[4], (D,), jnp.float32), 0.25, 1.75)
    w_query = normal_values(arg_keys[5], (D, KH * DK), D ** -0.5, 0.125, ((1, 8),))
    w_key = normal_values(arg_keys[6], (D, KH * DK), D ** -0.5, 0.125, ((1, 8),))
    w_value = normal_values(arg_keys[7], (D, HV * DV), D ** -0.5, 0.125, ((1, 8),))
    w_zgate = normal_values(arg_keys[8], (D, HV * DV), D ** -0.5, 0.125, ((1, 8),))
    w_beta = normal_values(arg_keys[9], (D, HV), D ** -0.5, 0.125, ((1, 8),))
    w_alpha = normal_values(arg_keys[10], (D, HV), D ** -0.5, 0.125, ((1, 8),))
    decay_scale = jnp.clip(jnp.exp(math.log(2.0) - 3.6888794 * jax.random.uniform(arg_keys[11], (HV,), jnp.float32) ** level_of(arg_keys[11], (HV,), ((0, 8),), -0.2, 0.2)), 0.05, 2.0)
    dt_bias = jnp.clip(-2.0 + 3.0 * jax.random.uniform(arg_keys[12], (HV,), jnp.float32) ** level_of(arg_keys[12], (HV,), ((0, 8),), -0.2, 0.2), -2.0, 1.0)
    gated_gain = jnp.clip(1.0 + 0.15 * jax.random.normal(arg_keys[13], (DV,), jnp.float32), 0.25, 1.75)
    w_out = normal_values(arg_keys[14], (HV * DV, D), (HV * DV) ** -0.5, 0.09375, ((0, 8),))
    post_gain = jnp.clip(1.0 + 0.15 * jax.random.normal(arg_keys[15], (D,), jnp.float32), 0.25, 1.75)
    w_shared_in = normal_values(arg_keys[16], (D, 2 * FS), D ** -0.5, 0.125, ((0, 8),))
    w_shared_out = normal_values(arg_keys[17], (FS, D), FS ** -0.5, 0.25, ((1, 8),))
    w_expert_in = normal_values(arg_keys[18], (EXPERTS, D, 2 * FE), D ** -0.5, 0.125, ((0, 32),))
    w_expert_out = normal_values(arg_keys[19], (EXPERTS, FE, D), FE ** -0.5, 0.25, ((0, 32),))
    return dict(tokens=tokens, states=states, router_ids=router_ids, router_weights=router_weights, input_gain=input_gain, w_query=w_query, w_key=w_key, w_value=w_value, w_zgate=w_zgate, w_beta=w_beta, w_alpha=w_alpha, decay_scale=decay_scale, dt_bias=dt_bias, gated_gain=gated_gain, w_out=w_out, post_gain=post_gain, w_shared_in=w_shared_in, w_shared_out=w_shared_out, w_expert_in=w_expert_in, w_expert_out=w_expert_out)


epsilon = 1e-06

def rms_norm(values):
    return values * lax.rsqrt(lax.optimization_barrier(jnp.mean(values * values, axis=-1, keepdims=True)) + epsilon)

def unit_norm(values):
    return values * lax.rsqrt(lax.optimization_barrier(jnp.sum(values * values, axis=-1, keepdims=True)) + epsilon)

def reference(tokens, states, router_ids, router_weights, input_gain, w_query, w_key, w_value, w_zgate, w_beta, w_alpha, decay_scale, dt_bias, gated_gain, w_out, post_gain, w_shared_in, w_shared_out, w_expert_in, w_expert_out):
    row_total = SEQS * STEPS
    rows_wide = tokens.reshape(row_total, D).astype(jnp.float32)
    normed = (rms_norm(rows_wide) * input_gain).astype(jnp.bfloat16)
    queries = jax.nn.silu(jnp.dot(normed, w_query, preferred_element_type=jnp.float32))
    keys_all = jax.nn.silu(jnp.dot(normed, w_key, preferred_element_type=jnp.float32))
    values_all = jax.nn.silu(jnp.dot(normed, w_value, preferred_element_type=jnp.float32))
    zgates = jnp.dot(normed, w_zgate, preferred_element_type=jnp.float32)
    betas = jax.nn.sigmoid(jnp.dot(normed, w_beta, preferred_element_type=jnp.float32))
    alphas = jnp.dot(normed, w_alpha, preferred_element_type=jnp.float32)
    decays = jnp.exp(-decay_scale * jax.nn.softplus(alphas + dt_bias))
    group = HV // KH
    queries = jnp.repeat(unit_norm(queries.reshape(SEQS, STEPS, KH, DK)) * DK ** (-0.5), group, axis=2)
    keys_all = jnp.repeat(unit_norm(keys_all.reshape(SEQS, STEPS, KH, DK)), group, axis=2)
    values_all = values_all.reshape(SEQS, STEPS, HV, DV)
    betas = betas.reshape(SEQS, STEPS, HV)
    decays = decays.reshape(SEQS, STEPS, HV)
    current = states
    outputs = []
    for step_index in range(STEPS):
        current = current * decays[:, step_index, :, None, None]
        key_now = keys_all[:, step_index]
        recall = jnp.einsum('shk,shkv->shv', key_now, current, precision=lax.Precision.HIGHEST)
        delta = betas[:, step_index, :, None] * (values_all[:, step_index] - recall)
        current = current + key_now[:, :, :, None] * delta[:, :, None, :]
        outputs.append(jnp.einsum('shk,shkv->shv', queries[:, step_index], current, precision=lax.Precision.HIGHEST))
    mixed = jnp.stack(outputs, axis=1)
    gated = (rms_norm(mixed) * gated_gain * jax.nn.silu(zgates.reshape(SEQS, STEPS, HV, DV))).astype(jnp.bfloat16)
    attention = jnp.dot(gated.reshape(row_total, HV * DV), w_out, preferred_element_type=jnp.float32)
    resid = rows_wide + attention
    post = (rms_norm(resid) * post_gain).astype(jnp.bfloat16)
    shared_pre = jnp.dot(post, w_shared_in, preferred_element_type=jnp.float32)
    shared_hidden = (jax.nn.silu(shared_pre[:, :FS]) * shared_pre[:, FS:]).astype(jnp.bfloat16)
    shared = jnp.dot(shared_hidden, w_shared_out, preferred_element_type=jnp.float32)
    expert_ids = router_ids.reshape(row_total, TOP)
    gate_values = router_weights.reshape(row_total, TOP)
    slot_total = N_SEQ * CAP
    slot_range = jnp.arange(slot_total, dtype=jnp.int32)

    def add_expert(routed, inputs):
        expert_index, weight_in, weight_out = inputs
        matched = expert_ids == expert_index
        row_weight = lax.optimization_barrier(jnp.sum(jnp.where(matched, gate_values, jnp.zeros_like(gate_values)), axis=-1))
        used = jnp.any(matched, axis=-1)
        picked = jnp.nonzero(used, size=slot_total, fill_value=0)[0].astype(jnp.int32)
        valid = slot_range < jnp.sum(used.astype(jnp.int32))
        chosen = post[picked]
        pre_act = jnp.dot(chosen, weight_in, preferred_element_type=jnp.float32)
        hidden = (jax.nn.silu(pre_act[:, :FE]) * pre_act[:, FE:]).astype(jnp.bfloat16)
        result = jnp.dot(hidden, weight_out, preferred_element_type=jnp.float32).astype(jnp.bfloat16)
        picked_weight = row_weight[picked]
        scale = jnp.where(valid, picked_weight, jnp.zeros_like(picked_weight))
        return (routed.at[picked].add(scale[:, None] * result.astype(routed.dtype)), None)
    routed, unused = lax.scan(add_expert, jnp.zeros((row_total, D), jnp.float32), (jnp.arange(EXPERTS, dtype=jnp.int32), w_expert_in, w_expert_out))
    layer_out = (resid + shared + routed).astype(jnp.bfloat16).reshape(SEQS, STEPS, D)
    return (layer_out, current)
```

```python
import functools

import jax
import jax.numpy as jnp
from jax import lax
from jax.experimental import pallas as pl
from jax.experimental.pallas import tpu as pltpu
from jax.sharding import PartitionSpec as P

DK = 128
DV = 128
EPS = 1e-06
SLOTS = 16
F32 = jnp.float32
BF16 = jnp.bfloat16
VMEM_LIMIT = 56 * 1024 * 1024


def dot(a, b):
    return jnp.dot(a, b, preferred_element_type=F32)


def silu(v):
    return v / (1.0 + jnp.exp(-v))


def split(v):
    high = v.astype(BF16)
    low = (v - high.astype(F32)).astype(BF16)
    return high, low


def exchange(x, axis, bit):
    size = lax.axis_size(axis)
    return lax.ppermute(x, axis, [(i, i ^ bit) for i in range(size)])


def front_kernel(
    steps,
    head_count,
    me_ref,
    x_ref,
    gain_ref,
    small_ref,
    scale_ref,
    bias_ref,
    ggain_ref,
    wq_hbm,
    wk_hbm,
    wv_hbm,
    wz_hbm,
    wo_hbm,
    states_hbm,
    own_ref,
    sib_ref,
    keys_ref,
    delta_ref,
    total_ref,
    wq,
    wk,
    wv,
    wz,
    wo,
    states,
    left,
    recalls,
    sems,
    state_sems,
):
    me = me_ref[0]
    rows = x_ref.shape[1]
    width = x_ref.shape[2]
    seqs = rows // steps
    key_heads = wq.shape[1] // DK
    value_heads = wv.shape[1] // DV
    group = value_heads // key_heads
    pair = group * DV
    copies = []
    for n, (src, dst) in enumerate(((wq_hbm, wq), (wk_hbm, wk), (wv_hbm, wv), (wz_hbm, wz))):
        copies.append(pltpu.make_async_copy(src, dst, sems.at[n]))
        copies[-1].start()
    parts = state_sems.shape[0]
    part = seqs // parts
    state_copies = []
    for n in range(parts):
        span = pl.ds(n * part, part)
        state_copies.append(
            pltpu.make_async_copy(states_hbm.at[span], states.at[span], state_sems.at[n])
        )
        state_copies[-1].start()
    out_copy = pltpu.make_async_copy(wo_hbm, wo, sems.at[4])
    out_copy.start()

    squares = jnp.zeros((rows, 1), F32)
    for j in range(head_count):
        xj = x_ref[j].astype(F32)
        squares = squares + jnp.sum(xj * xj, axis=1, keepdims=True)
    inverse = lax.rsqrt(squares / (head_count * width) + EPS)
    normed = []
    spans = []
    for j in range(head_count):
        block = me ^ j
        normed.append((x_ref[j].astype(F32) * inverse * gain_ref[block]).astype(BF16))
        spans.append(pl.ds(pl.multiple_of(block * width, width), width))

    def project(w_ref):
        total = None
        for j in range(head_count):
            term = dot(normed[j], w_ref[spans[j], :])
            total = term if total is None else total + term
        return total

    small = None
    for j in range(head_count):
        term = lax.dot_general(
            normed[j],
            small_ref[me ^ j],
            (((1,), (1,)), ((), ())),
            preferred_element_type=F32,
        )
        small = term if small is None else small + term
    betas = 1.0 / (1.0 + jnp.exp(-small[:, :value_heads]))
    alphas = small[:, value_heads : 2 * value_heads] + bias_ref[...]
    softplus = jnp.maximum(alphas, 0.0) + jnp.log1p(jnp.exp(-jnp.abs(alphas)))
    decays = jnp.exp(-scale_ref[...] * softplus)

    def units(v):
        return v * lax.rsqrt(jnp.sum(v * v, axis=1, keepdims=True) + EPS)

    copies[0].wait()
    queries_all = silu(project(wq))
    copies[1].wait()
    keys_all = silu(project(wk))
    keys, queries = [], []
    for i in range(key_heads):
        k = units(keys_all[:, i * DK : (i + 1) * DK])
        q = units(queries_all[:, i * DK : (i + 1) * DK]) * DK ** (-0.5)
        keys_ref[i] = k
        keys.append([k[t * seqs : (t + 1) * seqs] for t in range(steps)])
        queries.append([q[t * seqs : (t + 1) * seqs] for t in range(steps)])
        for t in range(steps):
            for at, v in ((t, keys[i][t]), (steps + t, queries[i][t])):
                high = v.astype(BF16).astype(F32)
                left[i, pl.ds(at, seqs, stride=SLOTS), :] = high
                left[i, pl.ds(2 * steps + at, seqs, stride=SLOTS), :] = v - high
        for at in range(4 * steps, SLOTS):
            left[i, pl.ds(at, seqs, stride=SLOTS), :] = jnp.zeros((seqs, DK), F32)
    copies[2].wait()
    values_all = silu(project(wv))
    copies[3].wait()
    gates = silu(project(wz))

    for n in range(parts):
        state_copies[n].wait()

        def one(s, carry):
            base = pl.multiple_of(s * SLOTS, SLOTS)
            for i in range(key_heads):
                lhs = left[i, pl.ds(base, SLOTS), :].astype(BF16)
                rhs = jnp.concatenate([states[s, i * group + u] for u in range(group)], axis=1)
                high, low = split(rhs)
                answer = dot(
                    jnp.concatenate([lhs, lhs], axis=1), jnp.concatenate([high, low], axis=0)
                )
                for u in range(group):
                    recalls[i * group + u, pl.ds(base, SLOTS), :] = answer[:, u * DV : (u + 1) * DV]
            return carry

        lax.fori_loop(n * part, (n + 1) * part, one, 0, unroll=2)

    def wide(columns, t, i):
        return jnp.concatenate(
            [
                jnp.broadcast_to(
                    columns[t * seqs : (t + 1) * seqs, i * group + u : i * group + u + 1],
                    (seqs, DV),
                )
                for u in range(group)
            ],
            axis=1,
        )

    mixed_rows = [[] for _ in range(steps)]
    for i in range(key_heads):
        decay = [wide(decays, t, i) for t in range(steps)]
        beta = [wide(betas, t, i) for t in range(steps)]

        def read(at):
            return jnp.concatenate(
                [
                    recalls[i * group + u, pl.ds(at, seqs, stride=SLOTS), :]
                    + recalls[i * group + u, pl.ds(2 * steps + at, seqs, stride=SLOTS), :]
                    for u in range(group)
                ],
                axis=1,
            )

        deltas = []
        running = None
        for t in range(steps):
            running = decay[t] if running is None else running * decay[t]
            recall = running * read(t)
            answer = running * read(steps + t)
            deltas = [d * decay[t] for d in deltas]
            for u, d in enumerate(deltas):
                recall = recall + d * jnp.sum(keys[i][t] * keys[i][u], axis=1, keepdims=True)
                answer = answer + d * jnp.sum(queries[i][t] * keys[i][u], axis=1, keepdims=True)
            value = values_all[t * seqs : (t + 1) * seqs, i * pair : (i + 1) * pair]
            delta = beta[t] * (value - recall)
            answer = answer + delta * jnp.sum(queries[i][t] * keys[i][t], axis=1, keepdims=True)
            deltas.append(delta)
            mixed_rows[t].append(answer)
        for t in range(steps):
            delta_ref[i, t] = deltas[t]
        total_ref[i] = running
    mixed = jnp.concatenate([jnp.concatenate(m, axis=1) for m in mixed_rows], axis=0)
    gated = []
    for h in range(value_heads):
        m = mixed[:, h * DV : (h + 1) * DV]
        m = m * lax.rsqrt(jnp.mean(m * m, axis=1, keepdims=True) + EPS)
        gated.append((m * ggain_ref[...] * gates[:, h * DV : (h + 1) * DV]).astype(BF16))
    gated = jnp.concatenate(gated, axis=1)
    out_copy.wait()
    for c in range(head_count):
        piece = dot(gated, wo[:, c * width : (c + 1) * width]).astype(BF16)
        away = me ^ c

        @pl.when(away % 2 == 0)
        def _():
            own_ref[away // 2] = piece

        @pl.when(away % 2 == 1)
        def _():
            sib_ref[away // 2] = piece


def front(me, x, gain, small, scale, bias, ggain, wq, wk, wv, wz, wo, states, steps):
    head_count, rows, width = x.shape
    seqs = rows // steps
    key_heads = wq.shape[1] // DK
    value_heads = wv.shape[1] // DV
    pair = value_heads // key_heads * DV
    vmem = pl.BlockSpec(memory_space=pltpu.VMEM)
    any_ = pl.BlockSpec(memory_space=pl.ANY)
    parts = 4
    return pl.pallas_call(
        functools.partial(front_kernel, steps, head_count),
        out_shape=(
            jax.ShapeDtypeStruct((head_count // 2, rows, width), BF16),
            jax.ShapeDtypeStruct((head_count // 2, rows, width), BF16),
            jax.ShapeDtypeStruct((key_heads, rows, DK), F32),
            jax.ShapeDtypeStruct((key_heads, steps, seqs, pair), F32),
            jax.ShapeDtypeStruct((key_heads, seqs, pair), F32),
        ),
        in_specs=[pl.BlockSpec(memory_space=pltpu.SMEM)] + [vmem] * 6 + [any_] * 6,
        out_specs=(vmem,) * 5,
        scratch_shapes=[
            pltpu.VMEM(wq.shape, BF16),
            pltpu.VMEM(wk.shape, BF16),
            pltpu.VMEM(wv.shape, BF16),
            pltpu.VMEM(wz.shape, BF16),
            pltpu.VMEM(wo.shape, BF16),
            pltpu.VMEM(states.shape, F32),
            pltpu.VMEM((key_heads, seqs * SLOTS, DK), F32),
            pltpu.VMEM((value_heads, seqs * SLOTS, DV), F32),
            pltpu.SemaphoreType.DMA((5,)),
            pltpu.SemaphoreType.DMA((parts,)),
        ],
        compiler_params=pltpu.CompilerParams(vmem_limit_bytes=VMEM_LIMIT),
        name="front",
    )(me, x, gain, small, scale, bias, ggain, wq, wk, wv, wz, wo, states)


def update_kernel(steps, keys_ref, delta_ref, total_ref, states_ref, out_ref, left, right):
    key_heads, rows, _ = keys_ref.shape
    seqs = rows // steps
    block = states_ref.shape[0]
    group = states_ref.shape[1] // key_heads
    at_block = pl.program_id(0)

    @pl.when(at_block == 0)
    def _():
        for i in range(key_heads):
            for at in range(SLOTS):
                rows_at = pl.ds(at, seqs, stride=SLOTS)
                t = at % steps
                k = keys_ref[i, t * seqs : (t + 1) * seqs, :]
                k_high = k.astype(BF16).astype(F32)
                k = k - k_high if at >= 2 * steps else k_high
                left[i, rows_at, :] = k if at < 3 * steps else jnp.zeros_like(k)
                for u in range(group):
                    d = delta_ref[i, t, :, u * DV : (u + 1) * DV]
                    d_high = d.astype(BF16).astype(F32)
                    d = d - d_high if steps <= at < 2 * steps else d_high
                    right[i * group + u, rows_at, :] = d if at < 3 * steps else jnp.zeros_like(d)

    def one(s, carry):
        here = at_block * block + s
        base = pl.multiple_of(here * SLOTS, SLOTS)
        for i in range(key_heads):
            lhs = left[i, pl.ds(base, SLOTS), :].astype(BF16)
            rhs = jnp.concatenate(
                [right[i * group + u, pl.ds(base, SLOTS), :] for u in range(group)], axis=1
            ).astype(BF16)
            change = lax.dot_general(
                lhs, rhs, (((0,), (0,)), ((), ())), preferred_element_type=F32
            )
            total = total_ref[i, pl.ds(here, 1), :]
            for u in range(group):
                columns = slice(u * DV, (u + 1) * DV)
                h = i * group + u
                out_ref[s, h] = states_ref[s, h] * total[:, columns] + change[:, columns]
        return carry

    lax.fori_loop(0, block, one, 0, unroll=2)


def update(keys, deltas, totals, states):
    key_heads, steps, seqs, pair = deltas.shape
    blocks = 8
    block = seqs // blocks
    vmem = pl.BlockSpec(memory_space=pltpu.VMEM)
    spec = pl.BlockSpec((block, *states.shape[1:]), lambda n: (n, 0, 0, 0))
    return pl.pallas_call(
        functools.partial(update_kernel, steps),
        out_shape=jax.ShapeDtypeStruct(states.shape, F32),
        grid=(blocks,),
        in_specs=[vmem, vmem, vmem, spec],
        out_specs=spec,
        scratch_shapes=[
            pltpu.VMEM((key_heads, seqs * SLOTS, DK), F32),
            pltpu.VMEM((states.shape[1], seqs * SLOTS, DV), F32),
        ],
        compiler_params=pltpu.CompilerParams(vmem_limit_bytes=VMEM_LIMIT),
        name="update",
    )(keys, deltas, totals, states)


def expert_in_kernel(orders, odd, first, me_ref, *refs):
    a_ref, b_ref, gain_inv_ref, w_ref = refs[:4]
    if first:
        pre_ref, sq_ref = refs[4:]
    else:
        pre_in, sq_in, pre_ref, sq_ref = refs[4:]
    me = me_ref[0]
    start = 0
    for ref, order in zip((a_ref, b_ref), orders):
        count, zs, rows, width = ref.shape
        total, squares = None, None
        for n in range(count):
            block = me ^ (2 * order[n] + odd)
            x = ref[n].reshape(zs * rows, width)
            term = dot(x, w_ref[0, pl.ds(pl.multiple_of(block * width, width), width), :])
            plain = x.astype(F32) * gain_inv_ref[block]
            sq = jnp.sum(plain * plain, axis=1, keepdims=True)
            total = term if total is None else total + term
            squares = sq if squares is None else squares + sq
        span = slice(start, start + zs * rows)
        start += zs * rows
        if not first:
            total = total + pre_in[span, :]
            squares = squares + sq_in[span, :]
        pre_ref[span, :] = total
        sq_ref[span, :] = squares


def expert_in(me, a, b, gain_inv, w, orders, odd, before=None):
    count, zs, rows, width = a.shape
    total = (zs + b.shape[1]) * rows
    vmem = pl.BlockSpec(memory_space=pltpu.VMEM)
    args = (me, a, b, gain_inv, w) + (() if before is None else tuple(before))
    return pl.pallas_call(
        functools.partial(expert_in_kernel, orders, odd, before is None),
        out_shape=(
            jax.ShapeDtypeStruct((total, w.shape[2]), F32),
            jax.ShapeDtypeStruct((total, 1), F32),
        ),
        in_specs=[pl.BlockSpec(memory_space=pltpu.SMEM)] + [vmem] * (len(args) - 1),
        out_specs=(vmem, vmem),
        compiler_params=pltpu.CompilerParams(vmem_limit_bytes=VMEM_LIMIT),
        name="expert_in",
    )(*args)


def expert_out_kernel(orders, me_ref, pre_ref, sq_ref, weight_ref, w_ref, *outs):
    a_own, a_sib, b_own, b_sib = outs
    me = me_ref[0]
    count, zs, rows, width = a_own.shape
    features = w_ref.shape[2]
    hidden_width = w_ref.shape[1]
    start = 0
    for own, sib, order in ((a_own, a_sib, orders[0]), (b_own, b_sib, orders[1])):
        zs = own.shape[1]
        span = slice(start, start + zs * rows)
        start += zs * rows
        inverse = lax.rsqrt(sq_ref[span, :] / features + EPS)
        gate = pre_ref[span, :hidden_width] * inverse
        up = pre_ref[span, hidden_width:] * inverse
        hidden = (silu(gate) * up).astype(BF16)
        weight = weight_ref[span, :]
        for odd, ref in ((1, sib), (0, own)):
            for n in range(count):
                block = me ^ (2 * order[n] + odd)
                columns = pl.ds(pl.multiple_of(block * width, width), width)
                result = dot(hidden, w_ref[0, :, columns]) * weight
                ref[n] = result.astype(BF16).reshape(zs, rows, width)


def expert_out(me, pre, sq, weight, w, orders, shapes):
    vmem = pl.BlockSpec(memory_space=pltpu.VMEM)
    return pl.pallas_call(
        functools.partial(expert_out_kernel, orders),
        out_shape=tuple(jax.ShapeDtypeStruct(s, BF16) for s in shapes),
        in_specs=[pl.BlockSpec(memory_space=pltpu.SMEM)] + [vmem] * 4,
        out_specs=(vmem,) * len(shapes),
        compiler_params=pltpu.CompilerParams(vmem_limit_bytes=VMEM_LIMIT),
        name="expert_out",
    )(me, pre, sq, weight, w)


def bit_reversed(count):
    bits = count.bit_length() - 1
    return [int(format(n, "b").zfill(bits)[::-1], 2) if bits else 0 for n in range(count)]


def add(a, b):
    return (a.astype(F32) + b.astype(F32)).astype(BF16)


def on_device(
    tokens,
    states,
    router_ids,
    router_weights,
    input_gain,
    w_query,
    w_key,
    w_value,
    w_zgate,
    w_beta,
    w_alpha,
    decay_scale,
    dt_bias,
    gated_gain,
    w_out,
    post_gain,
    w_shared_in,
    w_shared_out,
    w_expert_in,
    w_expert_out,
):
    seq_count = lax.axis_size("seq")
    head_count = lax.axis_size("head")
    head_index = lax.axis_index("head")
    seq_index = lax.axis_index("seq")
    me = head_index.astype(jnp.int32).reshape(1)
    seqs, steps, width = tokens.shape
    rows = seqs * steps
    features = head_count * width
    pairs = head_count // 2
    axes = [1 << n for n in range(1, head_count.bit_length() - 1)]

    mine = jnp.transpose(tokens, (1, 0, 2)).reshape(rows, width)

    both = jnp.stack([mine, exchange(mine, "head", 1)])
    gathered = jnp.concatenate(
        [both] + [exchange(both, "head", 2 * p) for p in range(1, pairs)], axis=0
    )

    ids = jnp.transpose(router_ids, (1, 0, 2)).reshape(rows, -1)
    chosen = jnp.transpose(router_weights, (1, 0, 2)).reshape(rows, -1)
    row_weights = []
    for z in range(seq_count):
        target = (seq_index ^ z) * head_count + head_index
        weight = jnp.sum(jnp.where(ids == target, chosen, 0.0), axis=1).reshape(1, rows)
        row_weights.append(exchange(weight, "seq", z) if z else weight)
    row_weight = jnp.concatenate(row_weights, axis=1).reshape(seq_count * rows, 1)

    value_heads = w_beta.shape[1]
    small = jnp.concatenate([w_beta, w_alpha], axis=1)
    small = jnp.transpose(small.reshape(head_count, width, 2 * value_heads), (0, 2, 1))
    small = jnp.pad(small, ((0, 0), (0, -2 * value_heads % 16), (0, 0)))

    own, sib, keys, deltas, totals = front(
        me,
        gathered,
        input_gain.reshape(head_count, 1, width),
        small,
        decay_scale.reshape(1, value_heads),
        dt_bias.reshape(1, value_heads),
        gated_gain.reshape(1, DV),
        w_query,
        w_key,
        w_value,
        w_zgate,
        w_out,
        states,
        steps,
    )

    merged = add(own, exchange(sib, "head", 1))
    resid = mine.astype(F32) + merged[0].astype(F32)
    for p in range(1, pairs):
        resid = resid + exchange(merged[p], "head", 2 * p).astype(F32)
    gain_mine = lax.dynamic_slice_in_dim(post_gain, head_index * width, width, 0)
    x = (resid * gain_mine).astype(BF16)

    half = seq_count // 2
    slabs = [x] + [exchange(x, "seq", z) for z in range(1, seq_count)]
    sides = []
    for slab, bits in ((slabs[:half], axes), (slabs[half:], axes[::-1])):
        side = jnp.stack(slab)[None]
        for bit in bits:
            side = jnp.concatenate([side, exchange(side, "head", bit)], axis=0)
        sides.append(side)
    natural, reverse = list(range(pairs)), bit_reversed(pairs)
    siblings = [exchange(side, "head", 1) for side in sides]

    states_out = update(keys, deltas, totals, states)

    gain_inv = (1.0 / post_gain).reshape(head_count, 1, width)
    orders = (natural, reverse)
    pre = expert_in(me, *sides, gain_inv, w_expert_in, orders, 0)
    pre, squares = expert_in(me, *siblings, gain_inv, w_expert_in, orders, 1, pre)
    shape = (pairs, half, rows, width)
    a_own, a_sib, b_own, b_sib = expert_out(
        me, pre, squares, row_weight, w_expert_out, (reverse, natural), (shape,) * 4
    )
    sums = []
    for own, sib, bits in ((a_own, a_sib, axes), (b_own, b_sib, axes[::-1])):
        total = add(own, exchange(sib, "head", 1))
        for bit in bits:
            middle = total.shape[0] // 2
            total = add(total[:middle], exchange(total[middle:], "head", bit))
        sums.append(total[0])

    shared_pre = dot(x, w_shared_in)
    for bit in [1] + axes:
        sent = shared_pre.astype(BF16)
        shared_pre = sent.astype(F32) + exchange(sent, "head", bit).astype(F32)
    shared_pre = shared_pre * lax.rsqrt(squares[:rows] / features + EPS)
    half_shared = shared_pre.shape[1] // 2
    hidden = (silu(shared_pre[:, :half_shared]) * shared_pre[:, half_shared:]).astype(BF16)
    result = resid + dot(hidden, w_shared_out)

    for z in range(seq_count):
        part = sums[z // half][z % half]
        result = result + (exchange(part, "seq", z) if z else part).astype(F32)
    layer_out = jnp.transpose(result.astype(BF16).reshape(steps, seqs, width), (1, 0, 2))
    return (layer_out, states_out)


def solution(mesh):
    in_specs = (
        P("seq", None, "head"),
        P("seq", "head", None, None),
        P("seq", None, None),
        P("seq", None, None),
        P(),
        P(None, "head"),
        P(None, "head"),
        P(None, "head"),
        P(None, "head"),
        P(None, "head"),
        P(None, "head"),
        P("head"),
        P("head"),
        P(),
        P("head", None),
        P(),
        P("head", None),
        P(None, "head"),
        P(("seq", "head"), None, None),
        P(("seq", "head"), None, None),
    )
    out_specs = (P("seq", None, "head"), P("seq", "head", None, None))
    return jax.shard_map(
        on_device, mesh=mesh, in_specs=in_specs, out_specs=out_specs, check_vma=False
    )
```

```python
import functools

import jax
import jax.numpy as jnp
from jax import lax
from jax.experimental import pallas as pl
from jax.experimental.pallas import tpu as pltpu
from jax.sharding import PartitionSpec as P

DK = 128
DV = 128
EPS = 1e-06
SLOTS = 16
F32 = jnp.float32
BF16 = jnp.bfloat16
VMEM_LIMIT = 16 * 1024 * 1024


def dot(a, b):
    return jnp.dot(a, b, preferred_element_type=F32)


def silu(v):
    return v / (1.0 + jnp.exp(-v))


def split(v):
    high = v.astype(BF16)
    low = (v - high.astype(F32)).astype(BF16)
    return high, low


def pin(x):
    return pltpu.with_memory_space_constraint(x, pltpu.VMEM)


VMEM_SPEC = pl.BlockSpec(memory_space=pltpu.VMEM)
SMEM_SPEC = pl.BlockSpec(memory_space=pltpu.SMEM)
ANY_SPEC = pl.BlockSpec(memory_space=pl.ANY)


def call(body, name, out_shapes, smem, pinned, loose=(), scratch=(), aliases=None, outs=None):
    return pl.pallas_call(
        body,
        out_shape=tuple(out_shapes),
        in_specs=[SMEM_SPEC] * len(smem) + [VMEM_SPEC] * len(pinned) + [ANY_SPEC] * len(loose),
        out_specs=tuple(outs or [VMEM_SPEC] * len(out_shapes)),
        scratch_shapes=list(scratch),
        input_output_aliases=aliases or {},
        compiler_params=pltpu.CompilerParams(vmem_limit_bytes=VMEM_LIMIT),
        name=name,
    )(*smem, *(pin(x) for x in pinned), *loose)


def exchange(x, axis, bit):
    size = lax.axis_size(axis)
    return lax.ppermute(x, axis, [(i, i ^ bit) for i in range(size)])


def stack_kernel(a_ref, b_ref, out_ref):
    out_ref[0] = a_ref[...]
    out_ref[1] = b_ref[...]


def stack(a, b):
    [out] = call(stack_kernel, "stack", [pltpu.VMEM((2, *a.shape), a.dtype)], (), (a, b))
    return out


def front_kernel(
    steps,
    head_count,
    me_ref,
    *refs,
):
    x_refs = refs[: head_count // 2]
    (
        gain_ref,
        small_ref,
        scale_ref,
        bias_ref,
        ggain_ref,
        wq,
        wk,
        wv,
        wz,
        wo,
        states,
        _,
        own_ref,
        sib_ref,
        keys_ref,
        delta_ref,
        total_ref,
        left,
        recalls,
    ) = refs[head_count // 2 :]
    me = me_ref[0]
    _, rows, width = x_refs[0].shape
    seqs = rows // steps
    key_heads = wq.shape[1] // DK
    value_heads = wv.shape[1] // DV
    group = value_heads // key_heads
    pair = group * DV

    squares = jnp.zeros((rows, 1), F32)
    for j in range(head_count):
        xj = x_refs[j // 2][j % 2].astype(F32)
        squares = squares + jnp.sum(xj * xj, axis=1, keepdims=True)
    inverse = lax.rsqrt(squares / (head_count * width) + EPS)
    normed = []
    spans = []
    for j in range(head_count):
        block = me ^ j
        normed.append((x_refs[j // 2][j % 2].astype(F32) * inverse * gain_ref[block]).astype(BF16))
        spans.append(pl.ds(pl.multiple_of(block * width, width), width))

    def project(w_ref):
        total = None
        for j in range(head_count):
            term = dot(normed[j], w_ref[spans[j], :])
            total = term if total is None else total + term
        return total

    small = None
    for j in range(head_count):
        term = lax.dot_general(
            normed[j],
            small_ref[me ^ j],
            (((1,), (1,)), ((), ())),
            preferred_element_type=F32,
        )
        small = term if small is None else small + term
    betas = 1.0 / (1.0 + jnp.exp(-small[:, :value_heads]))
    alphas = small[:, value_heads : 2 * value_heads] + bias_ref[...]
    softplus = jnp.maximum(alphas, 0.0) + jnp.log1p(jnp.exp(-jnp.abs(alphas)))
    decays = jnp.exp(-scale_ref[...] * softplus)

    def units(v):
        return v * lax.rsqrt(jnp.sum(v * v, axis=1, keepdims=True) + EPS)

    queries_all = silu(project(wq))
    keys_all = silu(project(wk))
    keys, queries = [], []
    for i in range(key_heads):
        k = units(keys_all[:, i * DK : (i + 1) * DK])
        q = units(queries_all[:, i * DK : (i + 1) * DK]) * DK ** (-0.5)
        keys_ref[i] = k
        keys.append([k[t * seqs : (t + 1) * seqs] for t in range(steps)])
        queries.append([q[t * seqs : (t + 1) * seqs] for t in range(steps)])
        for t in range(steps):
            for at, v in ((t, keys[i][t]), (steps + t, queries[i][t])):
                high = v.astype(BF16).astype(F32)
                left[i, pl.ds(at, seqs, stride=SLOTS), :] = high
                left[i, pl.ds(2 * steps + at, seqs, stride=SLOTS), :] = v - high
        for at in range(4 * steps, SLOTS):
            left[i, pl.ds(at, seqs, stride=SLOTS), :] = jnp.zeros((seqs, DK), F32)
    values_all = silu(project(wv))
    gates = silu(project(wz))

    def one(s, carry):
        base = pl.multiple_of(s * SLOTS, SLOTS)
        for i in range(key_heads):
            lhs = left[i, pl.ds(base, SLOTS), :].astype(BF16)
            rhs = jnp.concatenate([states[s, i * group + u] for u in range(group)], axis=1)
            high, low = split(rhs)
            answer = dot(jnp.concatenate([lhs, lhs], axis=1), jnp.concatenate([high, low], axis=0))
            for u in range(group):
                recalls[i * group + u, pl.ds(base, SLOTS), :] = answer[:, u * DV : (u + 1) * DV]
        return carry

    lax.fori_loop(0, seqs, one, 0, unroll=4)

    def wide(columns, t, i):
        return jnp.concatenate(
            [
                jnp.broadcast_to(
                    columns[t * seqs : (t + 1) * seqs, i * group + u : i * group + u + 1],
                    (seqs, DV),
                )
                for u in range(group)
            ],
            axis=1,
        )

    mixed_rows = [[] for _ in range(steps)]
    for i in range(key_heads):
        decay = [wide(decays, t, i) for t in range(steps)]
        beta = [wide(betas, t, i) for t in range(steps)]

        def read(at):
            return jnp.concatenate(
                [
                    recalls[i * group + u, pl.ds(at, seqs, stride=SLOTS), :]
                    + recalls[i * group + u, pl.ds(2 * steps + at, seqs, stride=SLOTS), :]
                    for u in range(group)
                ],
                axis=1,
            )

        deltas = []
        running = None
        for t in range(steps):
            running = decay[t] if running is None else running * decay[t]
            recall = running * read(t)
            answer = running * read(steps + t)
            deltas = [d * decay[t] for d in deltas]
            for u, d in enumerate(deltas):
                recall = recall + d * jnp.sum(keys[i][t] * keys[i][u], axis=1, keepdims=True)
                answer = answer + d * jnp.sum(queries[i][t] * keys[i][u], axis=1, keepdims=True)
            value = values_all[t * seqs : (t + 1) * seqs, i * pair : (i + 1) * pair]
            delta = beta[t] * (value - recall)
            answer = answer + delta * jnp.sum(queries[i][t] * keys[i][t], axis=1, keepdims=True)
            deltas.append(delta)
            mixed_rows[t].append(answer)
        for t in range(steps):
            delta_ref[i, t] = deltas[t]
        total_ref[i] = running
    mixed = jnp.concatenate([jnp.concatenate(m, axis=1) for m in mixed_rows], axis=0)
    gated = []
    for h in range(value_heads):
        m = mixed[:, h * DV : (h + 1) * DV]
        m = m * lax.rsqrt(jnp.mean(m * m, axis=1, keepdims=True) + EPS)
        gated.append((m * ggain_ref[...] * gates[:, h * DV : (h + 1) * DV]).astype(BF16))
    gated = jnp.concatenate(gated, axis=1)
    for c in range(head_count):
        piece = dot(gated, wo[:, c * width : (c + 1) * width]).astype(BF16)
        away = me ^ c

        @pl.when(away % 2 == 0)
        def _():
            own_ref[away // 2] = piece

        @pl.when(away % 2 == 1)
        def _():
            sib_ref[away // 2] = piece


def front(me, xs, gain, small, scale, bias, ggain, wq, wk, wv, wz, wo, states, after, steps):
    _, rows, width = xs[0].shape
    head_count = 2 * len(xs)
    seqs = rows // steps
    key_heads = wq.shape[1] // DK
    value_heads = wv.shape[1] // DV
    pair = value_heads // key_heads * DV
    return call(
        functools.partial(front_kernel, steps, head_count),
        "front",
        [
            pltpu.VMEM((head_count // 2, rows, width), BF16),
            pltpu.VMEM((head_count // 2, rows, width), BF16),
            pltpu.VMEM((key_heads, rows, DK), F32),
            pltpu.VMEM((key_heads, steps, seqs, pair), F32),
            pltpu.VMEM((key_heads, seqs, pair), F32),
        ],
        (me,),
        (*xs, gain, small, scale, bias, ggain, wq, wk, wv, wz, wo, states),
        (after,),
        [
            pltpu.VMEM((key_heads, seqs * SLOTS, DK), F32),
            pltpu.VMEM((value_heads, seqs * SLOTS, DV), F32),
        ],
    )


PER_BLOCK = DK // SLOTS


def update_kernel(steps, blocks, aliased, keys_ref, delta_ref, total_ref, states_ref, *refs):
    if aliased:
        refs = refs[1:]
    _, out_ref, done_ref, left, right, buffers, sems = refs
    key_heads, rows, _ = keys_ref.shape
    seqs = rows // steps
    group = states_ref.shape[1] // key_heads
    first, count = blocks[0] * PER_BLOCK, len(blocks) * PER_BLOCK
    for i in range(key_heads):
        for at in range(SLOTS):
            rows_at = pl.ds(at, count, stride=SLOTS)
            t = at % steps
            k = keys_ref[i, t * seqs + first : t * seqs + first + count, :]
            k_high = k.astype(BF16).astype(F32)
            k = k - k_high if at >= 2 * steps else k_high
            left[i, rows_at, :] = k if at < 3 * steps else jnp.zeros_like(k)
            for u in range(group):
                d = delta_ref[i, t, first : first + count, u * DV : (u + 1) * DV]
                d_high = d.astype(BF16).astype(F32)
                d = d - d_high if steps <= at < 2 * steps else d_high
                right[i * group + u, rows_at, :] = d if at < 3 * steps else jnp.zeros_like(d)
    slot_of = lax.broadcasted_iota(jnp.int32, (DK, DK), 1) // SLOTS
    copies = []
    for n, block in enumerate(blocks):
        if n >= 2:
            copies[n - 2].wait()
        buffer = buffers.at[n % 2]
        span = slice(n * DK, (n + 1) * DK)
        for i in range(key_heads):
            lhs = jnp.transpose(left[i, span, :])
            rhs = jnp.concatenate([right[i * group + u, span, :] for u in range(group)], axis=1)
            rhs = rhs.astype(BF16)
            for m in range(PER_BLOCK):
                s = block * PER_BLOCK + m
                masked = jnp.where(slot_of == m, lhs, 0.0).astype(BF16)
                change = dot(masked, rhs)
                for u in range(group):
                    columns = slice(u * DV, (u + 1) * DV)
                    h = i * group + u
                    total = total_ref[i, s : s + 1, columns]
                    buffer[m, h] = states_ref[s, h] * total + change[:, columns]
        span = pl.ds(block * PER_BLOCK, PER_BLOCK)
        copies.append(pltpu.make_async_copy(buffer, out_ref.at[span], sems.at[n % 2]))
        copies[-1].start()
    for copy in copies[-2:]:
        copy.wait()
    done_ref[...] = jnp.zeros_like(done_ref)


def update(keys, deltas, totals, states, blocks, after, before=None):
    key_heads, steps, seqs, pair = deltas.shape
    rows = len(blocks) * DK
    value_heads = states.shape[1]
    loose = (after,) if before is None else (before, after)
    return call(
        functools.partial(update_kernel, steps, blocks, before is not None),
        "update",
        [jax.ShapeDtypeStruct(states.shape, F32), jax.ShapeDtypeStruct((8, 128), F32)],
        (),
        (keys, deltas, totals, states),
        loose,
        [
            pltpu.VMEM((key_heads, rows, DK), F32),
            pltpu.VMEM((value_heads, rows, DV), F32),
            pltpu.VMEM((2, PER_BLOCK, *states.shape[1:]), F32),
            pltpu.SemaphoreType.DMA((2,)),
        ],
        None if before is None else {4: 0},
        [ANY_SPEC, VMEM_SPEC],
    )


def expert_in_kernel(orders, odd, first, me_ref, *refs):
    pieces = refs[: sum(map(len, orders))]
    refs = refs[len(pieces) :]
    gain_inv_ref, w_ref = refs[:2]
    if first:
        pre_ref, sq_ref = refs[-2:]
    else:
        pre_in, sq_in = refs[2:4]
        pre_ref, sq_ref = refs[-2:]
    me = me_ref[0]
    start, at = 0, 0
    for order in orders:
        blocks, xs = [], []
        for part in order:
            ref = pieces[at]
            at += 1
            _, zs, rows, width = ref.shape
            for n, place in enumerate(part):
                xs.append(ref[n].reshape(zs * rows, width))
                blocks.append(me ^ (2 * place + odd))
        spans = [pl.ds(pl.multiple_of(b * width, width), width) for b in blocks]
        span = slice(start, start + zs * rows)
        start += zs * rows
        for c in range(0, w_ref.shape[2], 256):
            columns = slice(c, c + 256)
            total = None if first else pre_in[span, columns]
            for x, where in zip(xs, spans):
                term = dot(x, w_ref[0, where, columns])
                total = term if total is None else total + term
            pre_ref[span, columns] = total
        squares = None
        for x, block in zip(xs, blocks):
            plain = x.astype(F32) * gain_inv_ref[block]
            plain = plain * plain
            for c in range(0, width, 128):
                part = plain[:, c : c + 128]
                squares = part if squares is None else squares + part
        squares = jnp.sum(squares, axis=1, keepdims=True)
        sq_ref[span, :] = squares if first else squares + sq_in[span, :]


def expert_in(me, sides, gain_inv, w, orders, odd, before=(), after=()):
    pieces = [piece for side in sides for piece in side]
    rows = pieces[0].shape[2]
    total = sum(side[0].shape[1] for side in sides) * rows
    return call(
        functools.partial(expert_in_kernel, orders, odd, not before),
        "expert_in",
        [pltpu.VMEM((total, w.shape[2]), F32), pltpu.VMEM((total, 1), F32)],
        (me,),
        (*pieces, gain_inv, w, *before),
        after,
    )


def expert_out_kernel(orders, me_ref, pre_ref, sq_ref, weight_ref, w_ref, *outs):
    me = me_ref[0]
    features = w_ref.shape[2]
    hidden_width = w_ref.shape[1]
    start = 0
    for side, order in enumerate(orders):
        own, sib = outs[2 * side : 2 * side + 2]
        count, zs, rows, width = own.shape
        span = slice(start, start + zs * rows)
        start += zs * rows
        inverse = lax.rsqrt(sq_ref[span, :] / features + EPS)
        gate = pre_ref[span, :hidden_width] * inverse
        up = pre_ref[span, hidden_width:] * inverse
        hidden = (silu(gate) * up).astype(BF16)
        weight = weight_ref[span, :]
        for odd, ref in ((1, sib), (0, own)):
            for n in range(count):
                block = me ^ (2 * order[n] + odd)
                columns = pl.ds(pl.multiple_of(block * width, width), width)
                result = dot(hidden, w_ref[0, :, columns]) * weight
                ref[n] = result.astype(BF16).reshape(zs, rows, width)


def expert_out(me, pre, sq, weight, w, orders, shapes):
    return call(
        functools.partial(expert_out_kernel, orders),
        "expert_out",
        [pltpu.VMEM(shape, BF16) for shape in shapes],
        (me,),
        (pre, sq, weight, w),
    )


def bit_reversed(count):
    bits = count.bit_length() - 1
    return [int(format(n, "b").zfill(bits)[::-1], 2) if bits else 0 for n in range(count)]


def add(a, b):
    return (a.astype(F32) + b.astype(F32)).astype(BF16)


def half_sum_kernel(a_ref, b_ref, keep_ref, send_ref):
    half = a_ref.shape[0] // 2
    keep_ref[...] = add(a_ref[:half], b_ref[:half])
    send_ref[...] = add(a_ref[half:], b_ref[half:])


def half_sum(a, b):
    shape = (a.shape[0] // 2, *a.shape[1:])
    return call(
        half_sum_kernel, "half_sum", [pltpu.VMEM(shape, BF16), pltpu.VMEM(shape, BF16)], (), (a, b)
    )


def on_device(
    tokens,
    states,
    router_ids,
    router_weights,
    input_gain,
    w_query,
    w_key,
    w_value,
    w_zgate,
    w_beta,
    w_alpha,
    decay_scale,
    dt_bias,
    gated_gain,
    w_out,
    post_gain,
    w_shared_in,
    w_shared_out,
    w_expert_in,
    w_expert_out,
):
    seq_count = lax.axis_size("seq")
    head_count = lax.axis_size("head")
    head_index = lax.axis_index("head")
    seq_index = lax.axis_index("seq")
    me = head_index.astype(jnp.int32).reshape(1)
    seqs, steps, width = tokens.shape
    rows = seqs * steps
    features = head_count * width
    pairs = head_count // 2
    axes = [1 << n for n in range(1, head_count.bit_length() - 1)]

    mine = jnp.transpose(tokens, (1, 0, 2)).reshape(rows, width)

    both = stack(mine, exchange(mine, "head", 1))
    gathered = [both] + [exchange(both, "head", 2 * p) for p in range(1, pairs)]

    ids = jnp.transpose(router_ids, (1, 0, 2)).reshape(rows, -1)
    chosen = jnp.transpose(router_weights, (1, 0, 2)).reshape(rows, -1)
    row_weights = []
    for z in range(seq_count):
        target = (seq_index ^ z) * head_count + head_index
        weight = jnp.sum(jnp.where(ids == target, chosen, 0.0), axis=1).reshape(1, rows)
        row_weights.append(exchange(weight, "seq", z) if z else weight)
    row_weight = jnp.concatenate(row_weights, axis=1).reshape(seq_count * rows, 1)

    value_heads = w_beta.shape[1]
    small = jnp.concatenate([w_beta, w_alpha], axis=1)
    small = jnp.transpose(small.reshape(head_count, width, 2 * value_heads), (0, 2, 1))
    small = jnp.pad(small, ((0, 0), (0, -2 * value_heads % 16), (0, 0)))

    own, sib, keys, deltas, totals = front(
        me,
        gathered,
        input_gain.reshape(head_count, 1, width),
        small,
        decay_scale.reshape(1, value_heads),
        dt_bias.reshape(1, value_heads),
        gated_gain.reshape(1, DV),
        w_query,
        w_key,
        w_value,
        w_zgate,
        w_out,
        states,
        row_weight,
        steps,
    )

    merged = add(own, exchange(sib, "head", 1))
    resid = mine.astype(F32) + merged[0].astype(F32)
    for p in range(1, pairs):
        resid = resid + exchange(merged[p], "head", 2 * p).astype(F32)
    gain_mine = lax.dynamic_slice_in_dim(post_gain, head_index * width, width, 0)
    x = (resid * gain_mine).astype(BF16)

    half = seq_count // 2
    slabs = [x] + [exchange(x, "seq", z) for z in range(1, seq_count)]
    natural, reverse = list(range(pairs)), bit_reversed(pairs)
    sides, siblings, firsts = [], [], []
    for slab, bits in ((slabs[:half], axes), (slabs[half:], axes[::-1])):
        side = slab[0][None]
        side = stack(*slab)[None] if half == 2 else jnp.stack(slab)[None]
        for bit in bits[:-1]:
            received = exchange(side, "head", bit)
            firsts.append(received)
            side = stack(side[0], received[0]) if side.shape[0] == 1 else jnp.concatenate([side, received])
        sides.append([side, exchange(side, "head", bits[-1])])
        siblings.append([exchange(piece, "head", 1) for piece in sides[-1]])
    gain_inv = (1.0 / post_gain).reshape(head_count, 1, width)
    middle = pairs // 2
    orders = tuple((tuple(o[:middle]), tuple(o[middle:])) for o in (natural, reverse))

    blocks = tuple(range(seqs // PER_BLOCK))
    cut = len(blocks) // 2
    states_out, done_1 = update(keys, deltas, totals, states, blocks[:cut], slabs[1])
    states_out, done_2 = update(
        keys, deltas, totals, states, blocks[cut:], firsts[0], states_out
    )
    pre = expert_in(me, sides, gain_inv, w_expert_in, orders, 0, after=(done_1, done_2))
    pre, squares = expert_in(me, siblings, gain_inv, w_expert_in, orders, 1, pre)
    shape = (pairs, half, rows, width)
    a_own, a_sib, b_own, b_sib = expert_out(
        me, pre, squares, row_weight, w_expert_out, (reverse, natural), (shape,) * 4
    )
    sums = []
    for own, sib, bits in ((a_own, a_sib, axes), (b_own, b_sib, axes[::-1])):
        received = exchange(sib, "head", 1)
        for bit in bits:
            own, sent = half_sum(own, received)
            received = exchange(sent, "head", bit)
        sums.append(add(own[0], received[0]))

    shared_pre = dot(x, w_shared_in)
    for bit in [1] + axes:
        sent = shared_pre.astype(BF16)
        shared_pre = sent.astype(F32) + exchange(sent, "head", bit).astype(F32)
    shared_pre = shared_pre * lax.rsqrt(squares[:rows] / features + EPS)
    half_shared = shared_pre.shape[1] // 2
    hidden = (silu(shared_pre[:, :half_shared]) * shared_pre[:, half_shared:]).astype(BF16)
    result = resid + dot(hidden, w_shared_out)

    for z in range(seq_count):
        part = sums[z // half][z % half]
        result = result + (exchange(part, "seq", z) if z else part).astype(F32)
    layer_out = jnp.transpose(result.astype(BF16).reshape(steps, seqs, width), (1, 0, 2))
    return (layer_out, states_out)


def solution(mesh):
    in_specs = (
        P("seq", None, "head"),
        P("seq", "head", None, None),
        P("seq", None, None),
        P("seq", None, None),
        P(),
        P(None, "head"),
        P(None, "head"),
        P(None, "head"),
        P(None, "head"),
        P(None, "head"),
        P(None, "head"),
        P("head"),
        P("head"),
        P(),
        P("head", None),
        P(),
        P("head", None),
        P(None, "head"),
        P(("seq", "head"), None, None),
        P(("seq", "head"), None, None),
    )
    out_specs = (P("seq", None, "head"), P("seq", "head", None, None))
    return jax.shard_map(
        on_device, mesh=mesh, in_specs=in_specs, out_specs=out_specs, check_vma=False
    )
```

```python
import functools

import jax
import jax.numpy as jnp
from jax import lax
from jax.experimental import pallas as pl
from jax.experimental.pallas import tpu as pltpu
from jax.sharding import PartitionSpec as P

DK = 128
DV = 128
EPS = 1e-06
SLOTS = 16
F32 = jnp.float32
BF16 = jnp.bfloat16
VMEM_LIMIT = 16 * 1024 * 1024


def dot(a, b):
    return jnp.dot(a, b, preferred_element_type=F32)


def silu(v):
    return v / (1.0 + jnp.exp(-v))


def split(v):
    high = v.astype(BF16)
    low = (v - high.astype(F32)).astype(BF16)
    return high, low


def pin(x):
    return pltpu.with_memory_space_constraint(x, pltpu.VMEM)


VMEM_SPEC = pl.BlockSpec(memory_space=pltpu.VMEM)
SMEM_SPEC = pl.BlockSpec(memory_space=pltpu.SMEM)
ANY_SPEC = pl.BlockSpec(memory_space=pl.ANY)


def call(body, name, out_shapes, smem, pinned, loose=(), scratch=(), aliases=None, outs=None):
    return pl.pallas_call(
        body,
        out_shape=tuple(out_shapes),
        in_specs=[SMEM_SPEC] * len(smem) + [VMEM_SPEC] * len(pinned) + [ANY_SPEC] * len(loose),
        out_specs=tuple(outs or [VMEM_SPEC] * len(out_shapes)),
        scratch_shapes=list(scratch),
        input_output_aliases=aliases or {},
        compiler_params=pltpu.CompilerParams(vmem_limit_bytes=VMEM_LIMIT),
        name=name,
    )(*smem, *(pin(x) for x in pinned), *loose)


def exchange(x, axis, bit):
    size = lax.axis_size(axis)
    return lax.ppermute(x, axis, [(i, i ^ bit) for i in range(size)])


def stack_kernel(a_ref, b_ref, *refs):
    out_ref = refs[-1]
    out_ref[0] = a_ref[...]
    out_ref[1] = b_ref[...]


def stack(a, b, after=()):
    [out] = call(stack_kernel, "stack", [pltpu.VMEM((2, *a.shape), a.dtype)], (), (a, b), after)
    return out


def load_kernel(count, *refs):
    sources, targets, sems = refs[:count], refs[-1 - count : -1], refs[-1]
    copies = [pltpu.make_async_copy(a, b, sems.at[n]) for n, (a, b) in enumerate(zip(sources, targets))]
    for copy in copies:
        copy.start()
    for copy in copies:
        copy.wait()


def load(arrays, after=()):
    return call(
        functools.partial(load_kernel, len(arrays)),
        "load",
        [pltpu.VMEM(x.shape, x.dtype) for x in arrays],
        (),
        (),
        (*(pltpu.with_memory_space_constraint(x, pltpu.HBM) for x in arrays), *after),
        [pltpu.SemaphoreType.DMA((len(arrays),))],
    )


def front_kernel(
    steps,
    head_count,
    me_ref,
    *refs,
):
    x_refs = refs[: head_count // 2]
    (
        gain_ref,
        small_ref,
        pack_ref,
        wq,
        wk,
        wv,
        wz,
        wo,
        states,
        _,
        own_ref,
        sib_ref,
        keys_ref,
        delta_ref,
        total_ref,
        left,
        recalls,
    ) = refs[head_count // 2 :]
    me = me_ref[0]
    _, rows, width = x_refs[0].shape
    seqs = rows // steps
    key_heads = wq.shape[1] // DK
    value_heads = wv.shape[1] // DV
    group = value_heads // key_heads
    pair = group * DV

    squares = jnp.zeros((rows, 1), F32)
    for j in range(head_count):
        xj = x_refs[j // 2][j % 2].astype(F32)
        squares = squares + jnp.sum(xj * xj, axis=1, keepdims=True)
    inverse = lax.rsqrt(squares / (head_count * width) + EPS)
    normed = []
    spans = []
    for j in range(head_count):
        block = me ^ j
        normed.append((x_refs[j // 2][j % 2].astype(F32) * inverse * gain_ref[block]).astype(BF16))
        spans.append(pl.ds(pl.multiple_of(block * width, width), width))

    def project(w_ref):
        total = None
        for j in range(head_count):
            term = dot(normed[j], w_ref[spans[j], :])
            total = term if total is None else total + term
        return total

    small = None
    for j in range(head_count):
        term = lax.dot_general(
            normed[j],
            small_ref[me ^ j],
            (((1,), (1,)), ((), ())),
            preferred_element_type=F32,
        )
        small = term if small is None else small + term
    betas = 1.0 / (1.0 + jnp.exp(-small[:, :value_heads]))
    alphas = small[:, value_heads : 2 * value_heads] + pack_ref[1:2, :value_heads]
    softplus = jnp.maximum(alphas, 0.0) + jnp.log1p(jnp.exp(-jnp.abs(alphas)))
    decays = jnp.exp(-pack_ref[0:1, :value_heads] * softplus)

    def units(v):
        return v * lax.rsqrt(jnp.sum(v * v, axis=1, keepdims=True) + EPS)

    queries_all = silu(project(wq))
    keys_all = silu(project(wk))
    keys, queries = [], []
    for i in range(key_heads):
        k = units(keys_all[:, i * DK : (i + 1) * DK])
        q = units(queries_all[:, i * DK : (i + 1) * DK]) * DK ** (-0.5)
        keys_ref[i] = k
        keys.append([k[t * seqs : (t + 1) * seqs] for t in range(steps)])
        queries.append([q[t * seqs : (t + 1) * seqs] for t in range(steps)])
        for t in range(steps):
            for at, v in ((t, keys[i][t]), (steps + t, queries[i][t])):
                high = v.astype(BF16).astype(F32)
                left[i, pl.ds(at, seqs, stride=SLOTS), :] = high
                left[i, pl.ds(2 * steps + at, seqs, stride=SLOTS), :] = v - high
        for at in range(4 * steps, SLOTS):
            left[i, pl.ds(at, seqs, stride=SLOTS), :] = jnp.zeros((seqs, DK), F32)
    values_all = silu(project(wv))
    gates = silu(project(wz))

    def one(s, carry):
        base = pl.multiple_of(s * SLOTS, SLOTS)
        for i in range(key_heads):
            lhs = left[i, pl.ds(base, SLOTS), :].astype(BF16)
            rhs = jnp.concatenate([states[s, i * group + u] for u in range(group)], axis=1)
            high, low = split(rhs)
            answer = dot(jnp.concatenate([lhs, lhs], axis=1), jnp.concatenate([high, low], axis=0))
            for u in range(group):
                recalls[i * group + u, pl.ds(base, SLOTS), :] = answer[:, u * DV : (u + 1) * DV]
        return carry

    lax.fori_loop(0, seqs, one, 0, unroll=4)

    def wide(columns, t, i):
        return jnp.concatenate(
            [
                jnp.broadcast_to(
                    columns[t * seqs : (t + 1) * seqs, i * group + u : i * group + u + 1],
                    (seqs, DV),
                )
                for u in range(group)
            ],
            axis=1,
        )

    mixed_rows = [[] for _ in range(steps)]
    for i in range(key_heads):
        decay = [wide(decays, t, i) for t in range(steps)]
        beta = [wide(betas, t, i) for t in range(steps)]

        def read(at):
            return jnp.concatenate(
                [
                    recalls[i * group + u, pl.ds(at, seqs, stride=SLOTS), :]
                    + recalls[i * group + u, pl.ds(2 * steps + at, seqs, stride=SLOTS), :]
                    for u in range(group)
                ],
                axis=1,
            )

        deltas = []
        running = None
        for t in range(steps):
            running = decay[t] if running is None else running * decay[t]
            recall = running * read(t)
            answer = running * read(steps + t)
            deltas = [d * decay[t] for d in deltas]
            for u, d in enumerate(deltas):
                recall = recall + d * jnp.sum(keys[i][t] * keys[i][u], axis=1, keepdims=True)
                answer = answer + d * jnp.sum(queries[i][t] * keys[i][u], axis=1, keepdims=True)
            value = values_all[t * seqs : (t + 1) * seqs, i * pair : (i + 1) * pair]
            delta = beta[t] * (value - recall)
            answer = answer + delta * jnp.sum(queries[i][t] * keys[i][t], axis=1, keepdims=True)
            deltas.append(delta)
            mixed_rows[t].append(answer)
        for t in range(steps):
            delta_ref[i, t] = deltas[t]
        total_ref[i] = running
    mixed = jnp.concatenate([jnp.concatenate(m, axis=1) for m in mixed_rows], axis=0)
    gated = []
    for h in range(value_heads):
        m = mixed[:, h * DV : (h + 1) * DV]
        m = m * lax.rsqrt(jnp.mean(m * m, axis=1, keepdims=True) + EPS)
        gated.append((m * pack_ref[2:3, :DV] * gates[:, h * DV : (h + 1) * DV]).astype(BF16))
    gated = jnp.concatenate(gated, axis=1)
    for c in range(head_count):
        piece = dot(gated, wo[:, c * width : (c + 1) * width]).astype(BF16)
        away = me ^ c

        @pl.when(away % 2 == 0)
        def _():
            own_ref[away // 2] = piece

        @pl.when(away % 2 == 1)
        def _():
            sib_ref[away // 2] = piece


def front(me, xs, gain, small, pack, wq, wk, wv, wz, wo, states, after, steps):
    _, rows, width = xs[0].shape
    head_count = 2 * len(xs)
    seqs = rows // steps
    key_heads = wq.shape[1] // DK
    value_heads = wv.shape[1] // DV
    pair = value_heads // key_heads * DV
    return call(
        functools.partial(front_kernel, steps, head_count),
        "front",
        [
            pltpu.VMEM((head_count // 2, rows, width), BF16),
            pltpu.VMEM((head_count // 2, rows, width), BF16),
            pltpu.VMEM((key_heads, rows, DK), F32),
            pltpu.VMEM((key_heads, steps, seqs, pair), F32),
            pltpu.VMEM((key_heads, seqs, pair), F32),
        ],
        (me,),
        (*xs, gain, small, pack, wq, wk, wv, wz, wo, states),
        (after,),
        [
            pltpu.VMEM((key_heads, seqs * SLOTS, DK), F32),
            pltpu.VMEM((value_heads, seqs * SLOTS, DV), F32),
        ],
    )


def rows_kernel(pairs, *refs):
    merged_ref, received = refs[0], refs[1:pairs]
    mine_ref, gain_ref, extra_ref, w_ref, _ = refs[pairs : pairs + 5]
    resid_ref, x_ref, shared_ref = refs[pairs + 5 : pairs + 8]
    messages = refs[pairs + 8 :]
    rows = mine_ref.shape[0]
    resid = mine_ref[...].astype(F32) + merged_ref[0].astype(F32)
    for ref in received:
        resid = resid + ref[...].astype(F32)
    resid_ref[...] = resid
    x = (resid * gain_ref[...]).astype(BF16)
    x_ref[...] = x
    for z, ref in enumerate(messages):
        ref[:rows, :] = x
        ref[rows:, :] = extra_ref[z + 1]
    shared_ref[...] = dot(x, w_ref[...]).astype(BF16)


def make_rows(merged, received, mine, gain, extra, w, after):
    rows, width = mine.shape
    message = pltpu.VMEM((rows + extra.shape[1], width), BF16)
    return call(
        functools.partial(rows_kernel, merged.shape[0]),
        "rows",
        [
            pltpu.VMEM((rows, width), F32),
            pltpu.VMEM((rows, width), BF16),
            pltpu.VMEM((rows, w.shape[1]), BF16),
            *([message] * (extra.shape[0] - 1)),
        ],
        (),
        (merged, *received, mine, gain, extra, w),
        after,
    )


def slab_kernel(a_ref, b_ref, out_ref):
    rows = out_ref.shape[1]
    out_ref[0] = a_ref[:rows, :]
    out_ref[1] = b_ref[:rows, :]


def slab_pair(a, b, rows):
    [out] = call(slab_kernel, "slab", [pltpu.VMEM((2, rows, a.shape[1]), BF16)], (), (a, b))
    return out


PER_BLOCK = DK // SLOTS


def update_kernel(steps, blocks, keys_ref, delta_ref, total_ref, states_ref, *refs):
    out_ref, done_ref, left, right, olds, buffers, old_sems, sems = refs[-8:]
    loads = []
    for n, block in enumerate(blocks):
        span = pl.ds(block * PER_BLOCK, PER_BLOCK)
        loads.append(pltpu.make_async_copy(states_ref.at[span], olds.at[n], old_sems.at[n]))
        loads[-1].start()
    key_heads, rows, _ = keys_ref.shape
    seqs = rows // steps
    group = states_ref.shape[1] // key_heads
    first, count = blocks[0] * PER_BLOCK, len(blocks) * PER_BLOCK
    for i in range(key_heads):
        for at in range(SLOTS):
            rows_at = pl.ds(at, count, stride=SLOTS)
            t = at % steps
            k = keys_ref[i, t * seqs + first : t * seqs + first + count, :]
            k_high = k.astype(BF16).astype(F32)
            k = k - k_high if at >= 2 * steps else k_high
            left[i, rows_at, :] = k if at < 3 * steps else jnp.zeros_like(k)
            for u in range(group):
                d = delta_ref[i, t, first : first + count, u * DV : (u + 1) * DV]
                d_high = d.astype(BF16).astype(F32)
                d = d - d_high if steps <= at < 2 * steps else d_high
                right[i * group + u, rows_at, :] = d if at < 3 * steps else jnp.zeros_like(d)
    slot_of = lax.broadcasted_iota(jnp.int32, (DK, DK), 1) // SLOTS
    copies = []
    for n, block in enumerate(blocks):
        if n >= 2:
            copies[n - 2].wait()
        loads[n].wait()
        buffer = buffers.at[n % 2]
        span = slice(n * DK, (n + 1) * DK)
        for i in range(key_heads):
            lhs = jnp.transpose(left[i, span, :])
            rhs = jnp.concatenate([right[i * group + u, span, :] for u in range(group)], axis=1)
            rhs = rhs.astype(BF16)
            for m in range(PER_BLOCK):
                s = block * PER_BLOCK + m
                masked = jnp.where(slot_of == m, lhs, 0.0).astype(BF16)
                change = dot(masked, rhs)
                for u in range(group):
                    columns = slice(u * DV, (u + 1) * DV)
                    h = i * group + u
                    total = total_ref[i, s : s + 1, columns]
                    buffer[m, h] = olds[n, m, h] * total + change[:, columns]
        span = pl.ds(block * PER_BLOCK, PER_BLOCK)
        copies.append(pltpu.make_async_copy(buffer, out_ref.at[span], sems.at[n % 2]))
        copies[-1].start()
    for copy in copies[-2:]:
        copy.wait()
    done_ref[...] = jnp.zeros_like(done_ref)


def update(keys, deltas, totals, states, blocks, after, before=None):
    key_heads, steps, seqs, pair = deltas.shape
    rows = len(blocks) * DK
    value_heads = states.shape[1]
    loose = after if before is None else (before, *after)
    return call(
        functools.partial(update_kernel, steps, blocks),
        "update",
        [jax.ShapeDtypeStruct(states.shape, F32), jax.ShapeDtypeStruct((8, 128), F32)],
        (),
        (keys, deltas, totals),
        (pltpu.with_memory_space_constraint(states, pltpu.HBM), *loose),
        [
            pltpu.VMEM((key_heads, rows, DK), F32),
            pltpu.VMEM((value_heads, rows, DV), F32),
            pltpu.VMEM((len(blocks), PER_BLOCK, *states.shape[1:]), F32),
            pltpu.VMEM((2, PER_BLOCK, *states.shape[1:]), F32),
            pltpu.SemaphoreType.DMA((len(blocks),)),
            pltpu.SemaphoreType.DMA((2,)),
        ],
        None if before is None else {4: 0},
        [ANY_SPEC, VMEM_SPEC],
    )


def expert_in_kernel(orders, odd, first, me_ref, *refs):
    pieces = refs[: sum(map(len, orders))]
    refs = refs[len(pieces) :]
    gain_inv_ref, w_ref = refs[:2]
    if first:
        pre_ref, sq_ref = refs[-2:]
    else:
        pre_in, sq_in = refs[2:4]
        pre_ref, sq_ref = refs[-2:]
    me = me_ref[0]
    start, at = 0, 0
    for order in orders:
        blocks, xs = [], []
        for part in order:
            ref = pieces[at]
            at += 1
            _, zs, rows, width = ref.shape
            for n, place in enumerate(part):
                xs.append(ref[n].reshape(zs * rows, width))
                blocks.append(me ^ (2 * place + odd))
        spans = [pl.ds(pl.multiple_of(b * width, width), width) for b in blocks]
        span = slice(start, start + zs * rows)
        start += zs * rows
        for c in range(0, w_ref.shape[2], 256):
            columns = slice(c, c + 256)
            total = None if first else pre_in[span, columns]
            for x, where in zip(xs, spans):
                term = dot(x, w_ref[0, where, columns])
                total = term if total is None else total + term
            pre_ref[span, columns] = total
        squares = None
        for x, block in zip(xs, blocks):
            plain = x.astype(F32) * gain_inv_ref[block]
            plain = plain * plain
            for c in range(0, width, 128):
                part = plain[:, c : c + 128]
                squares = part if squares is None else squares + part
        squares = jnp.sum(squares, axis=1, keepdims=True)
        sq_ref[span, :] = squares if first else squares + sq_in[span, :]


def expert_in(me, sides, gain_inv, w, orders, odd, before=(), after=()):
    pieces = [piece for side in sides for piece in side]
    rows = pieces[0].shape[2]
    total = sum(side[0].shape[1] for side in sides) * rows
    return call(
        functools.partial(expert_in_kernel, orders, odd, not before),
        "expert_in",
        [pltpu.VMEM((total, w.shape[2]), F32), pltpu.VMEM((total, 1), F32)],
        (me,),
        (*pieces, gain_inv, w, *before),
        after,
    )


def expert_out_kernel(orders, me_ref, pre_ref, sq_ref, extra_ref, w_ref, *refs):
    me = me_ref[0]
    messages, outs = refs[:-4], refs[-4:]
    features = w_ref.shape[2]
    hidden_width = w_ref.shape[1]
    start = 0
    for side, order in enumerate(orders):
        own, sib = outs[2 * side : 2 * side + 2]
        count, zs, rows, width = own.shape
        span = slice(start, start + zs * rows)
        start += zs * rows
        inverse = lax.rsqrt(sq_ref[span, :] / features + EPS)
        gate = pre_ref[span, :hidden_width] * inverse
        up = pre_ref[span, hidden_width:] * inverse
        hidden = (silu(gate) * up).astype(BF16)
        weight = []
        for z in range(side * zs, (side + 1) * zs):
            extra = messages[z - 1][rows:, :] if z else extra_ref[0]
            columns = jnp.transpose(extra.astype(F32))
            weight.append(columns[:rows, 0:1] + columns[:rows, 1:2])
        weight = jnp.concatenate(weight, axis=0)
        for odd, ref in ((1, sib), (0, own)):
            for n in range(count):
                block = me ^ (2 * order[n] + odd)
                columns = pl.ds(pl.multiple_of(block * width, width), width)
                result = dot(hidden, w_ref[0, :, columns]) * weight
                ref[n] = result.astype(BF16).reshape(zs, rows, width)


def expert_out(me, pre, sq, extra, w, messages, orders, shapes, after):
    return call(
        functools.partial(expert_out_kernel, orders),
        "expert_out",
        [pltpu.VMEM(shape, BF16) for shape in shapes],
        (me,),
        (pre, sq, extra, w, *messages),
        after,
    )


def bit_reversed(count):
    bits = count.bit_length() - 1
    return [int(format(n, "b").zfill(bits)[::-1], 2) if bits else 0 for n in range(count)]


def add(a, b):
    return (a.astype(F32) + b.astype(F32)).astype(BF16)


def half_sum_kernel(a_ref, b_ref, keep_ref, send_ref):
    half = a_ref.shape[0] // 2
    keep_ref[...] = add(a_ref[:half], b_ref[:half])
    send_ref[...] = add(a_ref[half:], b_ref[half:])


def half_sum(a, b):
    shape = (a.shape[0] // 2, *a.shape[1:])
    return call(
        half_sum_kernel, "half_sum", [pltpu.VMEM(shape, BF16), pltpu.VMEM(shape, BF16)], (), (a, b)
    )


def last_sum_kernel(a_ref, b_ref, *outs):
    for z, ref in enumerate(outs):
        ref[...] = add(a_ref[0, z], b_ref[0, z])


def last_sum(a, b):
    _, zs, rows, width = a.shape
    return call(last_sum_kernel, "last_sum", [pltpu.VMEM((rows, width), BF16)] * zs, (), (a, b))


def one_sum_kernel(a_ref, b_ref, *refs):
    refs[-1][...] = add(a_ref[...], b_ref[...])


def one_sum(a, b, after=()):
    [out] = call(one_sum_kernel, "one_sum", [pltpu.VMEM(a.shape, BF16)], (), (a, b), after)
    return out


def shared_kernel(features, a_ref, b_ref, sq_ref, resid_ref, w_ref, out_ref):
    rows = a_ref.shape[0]
    half = a_ref.shape[1] // 2
    inverse = lax.rsqrt(sq_ref[:rows, :] / features + EPS)
    pre = (a_ref[...].astype(F32) + b_ref[...].astype(F32)) * inverse
    hidden = (silu(pre[:, :half]) * pre[:, half:]).astype(BF16)
    out_ref[...] = resid_ref[...] + dot(hidden, w_ref[...])


def shared_tail(features, a, b, sq, resid, w):
    [out] = call(
        functools.partial(shared_kernel, features),
        "shared",
        [pltpu.VMEM(resid.shape, F32)],
        (),
        (a, b, sq, resid, w),
    )
    return out


def on_device(
    tokens,
    states,
    router_ids,
    router_weights,
    input_gain,
    w_query,
    w_key,
    w_value,
    w_zgate,
    w_beta,
    w_alpha,
    decay_scale,
    dt_bias,
    gated_gain,
    w_out,
    post_gain,
    w_shared_in,
    w_shared_out,
    w_expert_in,
    w_expert_out,
):
    seq_count = lax.axis_size("seq")
    head_count = lax.axis_size("head")
    head_index = lax.axis_index("head")
    seq_index = lax.axis_index("seq")
    me = head_index.astype(jnp.int32).reshape(1)
    seqs, steps, width = tokens.shape
    rows = seqs * steps
    features = head_count * width
    pairs = head_count // 2
    axes = [1 << n for n in range(1, head_count.bit_length() - 1)]

    mine = jnp.transpose(tokens, (1, 0, 2)).reshape(rows, width)
    value_heads = w_beta.shape[1]
    gain = input_gain.reshape(head_count, 1, width)
    gain_after = post_gain.reshape(head_count, 1, width)

    neighbour = exchange(mine, "head", 1)
    mine, gain, gain_after, w_query, w_key, w_value, w_zgate = load(
        (mine, gain, gain_after, w_query, w_key, w_value, w_zgate)
    )
    both = stack(mine, neighbour)
    gathered = [both] + [exchange(both, "head", 2 * p) for p in range(1, pairs)]
    states_here, w_out, w_shared_in, w_shared_out = load(
        (states, w_out, w_shared_in, w_shared_out), (both,)
    )

    ids = jnp.transpose(router_ids, (1, 0, 2)).reshape(rows, -1)
    chosen = jnp.transpose(router_weights, (1, 0, 2)).reshape(rows, -1)
    targets = (seq_index ^ jnp.arange(seq_count, dtype=jnp.int32)) * head_count + head_index
    named = ids[None] == targets[:, None, None]
    weights = jnp.sum(jnp.where(named, chosen[None], 0.0), axis=2)
    high, low = split(weights)
    extra = jnp.stack([high, low], axis=1)
    extra = jnp.pad(extra, ((0, 0), (0, 14), (0, width - rows)))

    small = jnp.concatenate([w_beta, w_alpha], axis=1)
    small = jnp.transpose(small.reshape(head_count, width, 2 * value_heads), (0, 2, 1))
    small = jnp.pad(small, ((0, 0), (0, -2 * value_heads % 16), (0, 0)))
    pack = jnp.stack(
        [
            jnp.pad(decay_scale, (0, DV - value_heads)),
            jnp.pad(dt_bias, (0, DV - value_heads)),
            gated_gain,
        ]
    )

    own, sib, keys, deltas, totals = front(
        me, gathered, gain, small, pack, w_query, w_key, w_value, w_zgate, w_out, states_here, extra, steps
    )

    merged = one_sum(own, exchange(sib, "head", 1))
    received = [exchange(merged[p], "head", 2 * p) for p in range(1, pairs)]
    w_in, w_down = load((w_expert_in, w_expert_out), (merged,))
    gain_mine = lax.dynamic_index_in_dim(gain_after, head_index, 0, keepdims=False)
    resid, x, shared_pre, *messages = make_rows(
        merged, received, mine, gain_mine, extra, w_shared_in, (w_in,)
    )

    half = seq_count // 2
    messages = [exchange(m, "seq", z + 1) for z, m in enumerate(messages)]
    shared_pre = one_sum(shared_pre, exchange(shared_pre, "head", axes[0]))
    shared_next = one_sum(shared_pre, exchange(shared_pre, "head", 1))
    slabs = [x] + messages
    natural, reverse = list(range(pairs)), bit_reversed(pairs)
    blocks = tuple(range(seqs // PER_BLOCK))
    cut = len(blocks) // 2
    sides, siblings, tie = [], [], ()
    for slab, bits in ((slabs[:half], axes), (slabs[half:], axes[::-1])):
        if half == 2:
            side = slab_pair(*slab, rows)[None]
        else:
            side = jnp.stack([m[:rows] for m in slab])[None]
        for bit in bits[:-1]:
            received = exchange(side, "head", bit)
            if not tie:
                states_out, done_1 = update(keys, deltas, totals, states, blocks[:cut], (side, shared_pre))
                tie = (done_1,)
            if side.shape[0] == 1:
                side = stack(side[0], received[0], tie)
            else:
                side = jnp.concatenate([side, received])
        sides.append([side, exchange(side, "head", bits[-1])])
        siblings.append([exchange(piece, "head", 1) for piece in sides[-1]])
    gain_inv = 1.0 / gain_after
    middle = pairs // 2
    orders = tuple((tuple(o[:middle]), tuple(o[middle:])) for o in (natural, reverse))

    states_out, done_2 = update(
        keys, deltas, totals, states, blocks[cut:], (sides[1][0], shared_next), states_out
    )
    pre = expert_in(me, sides, gain_inv, w_in, orders, 0, after=(done_2,))
    pre, squares = expert_in(me, siblings, gain_inv, w_in, orders, 1, pre)
    shared_pre, shared_received = shared_next, None
    for bit in axes[1:]:
        if shared_received is not None:
            shared_pre = one_sum(shared_pre, shared_received)
        shared_received = exchange(shared_pre, "head", bit)
    shape = (pairs, half, rows, width)
    a_own, a_sib, b_own, b_sib = expert_out(
        me, pre, squares, extra, w_down, messages, (reverse, natural), (shape,) * 4, (shared_received,)
    )
    base = shared_tail(features, shared_pre, shared_received, squares, resid, w_shared_out)
    slabs = []
    for own, sib, bits in ((a_own, a_sib, axes), (b_own, b_sib, axes[::-1])):
        received = exchange(sib, "head", 1)
        for bit in bits:
            own, sent = half_sum(own, received)
            received = exchange(sent, "head", bit)
        slabs += last_sum(own, received)
    result = base + slabs[0].astype(F32)
    for z in range(1, seq_count):
        result = result + exchange(slabs[z], "seq", z).astype(F32)
    layer_out = jnp.transpose(result.astype(BF16).reshape(steps, seqs, width), (1, 0, 2))
    return (layer_out, states_out)


def solution(mesh):
    in_specs = (
        P("seq", None, "head"),
        P("seq", "head", None, None),
        P("seq", None, None),
        P("seq", None, None),
        P(),
        P(None, "head"),
        P(None, "head"),
        P(None, "head"),
        P(None, "head"),
        P(None, "head"),
        P(None, "head"),
        P("head"),
        P("head"),
        P(),
        P("head", None),
        P(),
        P("head", None),
        P(None, "head"),
        P(("seq", "head"), None, None),
        P(("seq", "head"), None, None),
    )
    out_specs = (P("seq", None, "head"), P("seq", "head", None, None))
    return jax.shard_map(
        on_device, mesh=mesh, in_specs=in_specs, out_specs=out_specs, check_vma=False
    )
```

```python
import functools

import jax
import jax.numpy as jnp
from jax import lax
from jax.experimental import pallas as pl
from jax.experimental.pallas import tpu as pltpu
from jax.sharding import PartitionSpec as P

DK = 128
DV = 128
EPS = 1e-06
SLOTS = 16
F32 = jnp.float32
BF16 = jnp.bfloat16
VMEM_LIMIT = 24 * 1024 * 1024


def dot(a, b):
    return jnp.dot(a, b, preferred_element_type=F32)


def silu(v):
    return v / (1.0 + jnp.exp(-v))


def split(v):
    high = v.astype(BF16)
    low = (v - high.astype(F32)).astype(BF16)
    return high, low


def pin(x):
    return pltpu.with_memory_space_constraint(x, pltpu.VMEM)


VMEM_SPEC = pl.BlockSpec(memory_space=pltpu.VMEM)
SMEM_SPEC = pl.BlockSpec(memory_space=pltpu.SMEM)
ANY_SPEC = pl.BlockSpec(memory_space=pl.ANY)


def call(body, name, out_shapes, smem, pinned, loose=(), scratch=(), aliases=None, outs=None):
    return pl.pallas_call(
        body,
        out_shape=tuple(out_shapes),
        in_specs=[SMEM_SPEC] * len(smem) + [VMEM_SPEC] * len(pinned) + [ANY_SPEC] * len(loose),
        out_specs=tuple(outs or [VMEM_SPEC] * len(out_shapes)),
        scratch_shapes=list(scratch),
        input_output_aliases=aliases or {},
        compiler_params=pltpu.CompilerParams(vmem_limit_bytes=VMEM_LIMIT),
        name=name,
    )(*smem, *(pin(x) for x in pinned), *loose)


def exchange(x, axis, bit):
    size = lax.axis_size(axis)
    return lax.ppermute(x, axis, [(i, i ^ bit) for i in range(size)])


def stack_kernel(a_ref, b_ref, *refs):
    out_ref = refs[-1]
    out_ref[0] = a_ref[...]
    out_ref[1] = b_ref[...]


def stack(a, b, after=()):
    [out] = call(stack_kernel, "stack", [pltpu.VMEM((2, *a.shape), a.dtype)], (), (a, b), after)
    return out


def load_kernel(count, *refs):
    sources, targets, sems = refs[:count], refs[-1 - count : -1], refs[-1]
    copies = [pltpu.make_async_copy(a, b, sems.at[n]) for n, (a, b) in enumerate(zip(sources, targets))]
    for copy in copies:
        copy.start()
    for copy in copies:
        copy.wait()


def load(arrays, after=()):
    return call(
        functools.partial(load_kernel, len(arrays)),
        "load",
        [pltpu.VMEM(x.shape, x.dtype) for x in arrays],
        (),
        (),
        (*(pltpu.with_memory_space_constraint(x, pltpu.HBM) for x in arrays), *after),
        [pltpu.SemaphoreType.DMA((len(arrays),))],
    )


def bring_kernel(count, seq_count, head_count, me_ref, seq_ref, *refs):
    sources, (ids_hbm, chosen_hbm, gain_after_hbm) = refs[:count], refs[count : count + 3]
    refs = refs[count + 4 :]
    targets, (extra_ref, gain_mine_ref, gain_inv_ref) = refs[:count], refs[count : count + 3]
    ids, chosen, gain_after, sems = refs[count + 3 :]
    sources = (ids_hbm, chosen_hbm, gain_after_hbm, *sources)
    targets = (ids, chosen, gain_after, *targets)
    copies = [pltpu.make_async_copy(a, b, sems.at[n]) for n, (a, b) in enumerate(zip(sources, targets))]
    for copy in copies:
        copy.start()
    for copy in copies[:3]:
        copy.wait()
    me, seq = me_ref[0], seq_ref[0]
    gain_mine_ref[...] = gain_after[me]
    gain_inv_ref[...] = 1.0 / gain_after[...]
    top, steps, seqs = ids.shape
    for z in range(seq_count):
        target = (seq ^ z) * head_count + me
        weight = jnp.zeros((steps, seqs), F32)
        for n in range(top):
            weight = weight + jnp.where(ids[n] == target, chosen[n], 0.0)
        high = weight.astype(BF16).astype(F32)
        both = jnp.concatenate([high, weight - high], axis=0)
        rows, width = extra_ref.shape[1:]
        both = jnp.concatenate([both, jnp.zeros((rows - 2 * steps, seqs), F32)], axis=0)
        both = jnp.concatenate([both, jnp.zeros((rows, width - seqs), F32)], axis=1)
        extra_ref[z] = both.astype(BF16)
    for copy in copies[3:]:
        copy.wait()


def bring(me, seq, arrays, ids, chosen, gain_after, seq_count, after):
    head_count, _, width = gain_after.shape
    count = len(arrays)
    hbm = (pltpu.with_memory_space_constraint(x, pltpu.HBM) for x in (*arrays, ids, chosen, gain_after))
    return call(
        functools.partial(bring_kernel, count, seq_count, head_count),
        "bring",
        [pltpu.VMEM(x.shape, x.dtype) for x in arrays]
        + [
            pltpu.VMEM((seq_count, 16, width), BF16),
            pltpu.VMEM((1, width), F32),
            pltpu.VMEM(gain_after.shape, F32),
        ],
        (me, seq),
        (),
        (*hbm, after),
        [
            pltpu.VMEM(ids.shape, jnp.int32),
            pltpu.VMEM(chosen.shape, F32),
            pltpu.VMEM(gain_after.shape, F32),
            pltpu.SemaphoreType.DMA((count + 3,)),
        ],
    )


def front_kernel(
    steps,
    head_count,
    me_ref,
    *refs,
):
    x_refs = refs[: head_count // 2]
    (
        gain_ref,
        small_ref,
        pack_ref,
        wq,
        wk,
        wv,
        wz,
        wo_hbm,
        states_hbm,
        own_ref,
        sib_ref,
        keys_ref,
        delta_ref,
        total_ref,
        wo,
        states,
        left,
        recalls,
        sems,
    ) = refs[head_count // 2 :]
    me = me_ref[0]
    _, rows, width = x_refs[0].shape
    seqs = rows // steps
    key_heads = wq.shape[1] // DK
    value_heads = wv.shape[1] // DV
    group = value_heads // key_heads
    pair = group * DV

    parts = sems.shape[0] - 1
    part = seqs // parts
    copies = []
    for n in range(parts):
        span = pl.ds(n * part, part)
        copies.append(pltpu.make_async_copy(states_hbm.at[span], states.at[span], sems.at[n]))
    copies.append(pltpu.make_async_copy(wo_hbm, wo, sems.at[parts]))
    for copy in copies:
        copy.start()

    squares = jnp.zeros((rows, 1), F32)
    for j in range(head_count):
        xj = x_refs[j // 2][j % 2].astype(F32)
        squares = squares + jnp.sum(xj * xj, axis=1, keepdims=True)
    inverse = lax.rsqrt(squares / (head_count * width) + EPS)
    normed = []
    spans = []
    for j in range(head_count):
        block = me ^ j
        normed.append((x_refs[j // 2][j % 2].astype(F32) * inverse * gain_ref[block]).astype(BF16))
        spans.append(pl.ds(pl.multiple_of(block * width, width), width))

    def project(w_ref):
        total = None
        for j in range(head_count):
            term = dot(normed[j], w_ref[spans[j], :])
            total = term if total is None else total + term
        return total

    small = None
    for j in range(head_count):
        term = lax.dot_general(
            normed[j],
            small_ref[me ^ j],
            (((1,), (1,)), ((), ())),
            preferred_element_type=F32,
        )
        small = term if small is None else small + term
    betas = 1.0 / (1.0 + jnp.exp(-small[:, :value_heads]))
    alphas = small[:, value_heads : 2 * value_heads] + pack_ref[1:2, :value_heads]
    softplus = jnp.maximum(alphas, 0.0) + jnp.log1p(jnp.exp(-jnp.abs(alphas)))
    decays = jnp.exp(-pack_ref[0:1, :value_heads] * softplus)

    def units(v):
        return v * lax.rsqrt(jnp.sum(v * v, axis=1, keepdims=True) + EPS)

    queries_all = silu(project(wq))
    keys_all = silu(project(wk))
    keys, queries = [], []
    for i in range(key_heads):
        k = units(keys_all[:, i * DK : (i + 1) * DK])
        q = units(queries_all[:, i * DK : (i + 1) * DK]) * DK ** (-0.5)
        keys_ref[i] = k
        keys.append([k[t * seqs : (t + 1) * seqs] for t in range(steps)])
        queries.append([q[t * seqs : (t + 1) * seqs] for t in range(steps)])
        for t in range(steps):
            for at, v in ((t, keys[i][t]), (steps + t, queries[i][t])):
                high = v.astype(BF16).astype(F32)
                left[i, pl.ds(at, seqs, stride=SLOTS), :] = high
                left[i, pl.ds(2 * steps + at, seqs, stride=SLOTS), :] = v - high
        for at in range(4 * steps, SLOTS):
            left[i, pl.ds(at, seqs, stride=SLOTS), :] = jnp.zeros((seqs, DK), F32)
    values_all = silu(project(wv))
    gates = silu(project(wz))

    def one(s, carry):
        base = pl.multiple_of(s * SLOTS, SLOTS)
        for i in range(key_heads):
            lhs = left[i, pl.ds(base, SLOTS), :].astype(BF16)
            rhs = jnp.concatenate([states[s, i * group + u] for u in range(group)], axis=1)
            high, low = split(rhs)
            answer = dot(jnp.concatenate([lhs, lhs], axis=1), jnp.concatenate([high, low], axis=0))
            for u in range(group):
                recalls[i * group + u, pl.ds(base, SLOTS), :] = answer[:, u * DV : (u + 1) * DV]
        return carry

    for n in range(parts):
        copies[n].wait()
        lax.fori_loop(n * part, (n + 1) * part, one, 0, unroll=4)

    def wide(columns, t, i):
        return jnp.concatenate(
            [
                jnp.broadcast_to(
                    columns[t * seqs : (t + 1) * seqs, i * group + u : i * group + u + 1],
                    (seqs, DV),
                )
                for u in range(group)
            ],
            axis=1,
        )

    mixed_rows = [[] for _ in range(steps)]
    for i in range(key_heads):
        decay = [wide(decays, t, i) for t in range(steps)]
        beta = [wide(betas, t, i) for t in range(steps)]

        def read(at):
            return jnp.concatenate(
                [
                    recalls[i * group + u, pl.ds(at, seqs, stride=SLOTS), :]
                    + recalls[i * group + u, pl.ds(2 * steps + at, seqs, stride=SLOTS), :]
                    for u in range(group)
                ],
                axis=1,
            )

        deltas = []
        running = None
        for t in range(steps):
            running = decay[t] if running is None else running * decay[t]
            recall = running * read(t)
            answer = running * read(steps + t)
            deltas = [d * decay[t] for d in deltas]
            for u, d in enumerate(deltas):
                recall = recall + d * jnp.sum(keys[i][t] * keys[i][u], axis=1, keepdims=True)
                answer = answer + d * jnp.sum(queries[i][t] * keys[i][u], axis=1, keepdims=True)
            value = values_all[t * seqs : (t + 1) * seqs, i * pair : (i + 1) * pair]
            delta = beta[t] * (value - recall)
            answer = answer + delta * jnp.sum(queries[i][t] * keys[i][t], axis=1, keepdims=True)
            deltas.append(delta)
            mixed_rows[t].append(answer)
        for t in range(steps):
            delta_ref[i, t] = deltas[t]
        total_ref[i] = running
    mixed = jnp.concatenate([jnp.concatenate(m, axis=1) for m in mixed_rows], axis=0)
    gated = []
    for h in range(value_heads):
        m = mixed[:, h * DV : (h + 1) * DV]
        m = m * lax.rsqrt(jnp.mean(m * m, axis=1, keepdims=True) + EPS)
        gated.append((m * pack_ref[2:3, :DV] * gates[:, h * DV : (h + 1) * DV]).astype(BF16))
    gated = jnp.concatenate(gated, axis=1)
    copies[parts].wait()
    for c in range(head_count):
        piece = dot(gated, wo[:, c * width : (c + 1) * width]).astype(BF16)
        away = me ^ c

        @pl.when(away % 2 == 0)
        def _():
            own_ref[away // 2] = piece

        @pl.when(away % 2 == 1)
        def _():
            sib_ref[away // 2] = piece


def front(me, xs, gain, small, pack, wq, wk, wv, wz, wo, states, steps):
    _, rows, width = xs[0].shape
    head_count = 2 * len(xs)
    seqs = rows // steps
    key_heads = wq.shape[1] // DK
    value_heads = wv.shape[1] // DV
    pair = value_heads // key_heads * DV
    return call(
        functools.partial(front_kernel, steps, head_count),
        "front",
        [
            pltpu.VMEM((head_count // 2, rows, width), BF16),
            pltpu.VMEM((head_count // 2, rows, width), BF16),
            pltpu.VMEM((key_heads, rows, DK), F32),
            pltpu.VMEM((key_heads, steps, seqs, pair), F32),
            pltpu.VMEM((key_heads, seqs, pair), F32),
        ],
        (me,),
        (*xs, gain, small, pack, wq, wk, wv, wz),
        [pltpu.with_memory_space_constraint(x, pltpu.HBM) for x in (wo, states)],
        [
            pltpu.VMEM(wo.shape, BF16),
            pltpu.VMEM(states.shape, F32),
            pltpu.VMEM((key_heads, seqs * SLOTS, DK), F32),
            pltpu.VMEM((value_heads, seqs * SLOTS, DV), F32),
            pltpu.SemaphoreType.DMA((5,)),
        ],
    )


def rows_kernel(pairs, *refs):
    merged_ref, received = refs[0], refs[1:pairs]
    mine_ref, gain_ref, extra_ref, _ = refs[pairs : pairs + 4]
    resid_ref, x_ref = refs[pairs + 4 : pairs + 6]
    messages = refs[pairs + 6 :]
    rows = mine_ref.shape[0]
    resid = mine_ref[...].astype(F32) + merged_ref[0].astype(F32)
    for ref in received:
        resid = resid + ref[...].astype(F32)
    resid_ref[...] = resid
    x = (resid * gain_ref[...]).astype(BF16)
    x_ref[...] = x
    for z, ref in enumerate(messages):
        ref[:rows, :] = x
        ref[rows:, :] = extra_ref[z + 1]


def make_rows(merged, received, mine, gain, extra, after):
    rows, width = mine.shape
    message = pltpu.VMEM((rows + extra.shape[1], width), BF16)
    return call(
        functools.partial(rows_kernel, merged.shape[0]),
        "rows",
        [
            pltpu.VMEM((rows, width), F32),
            pltpu.VMEM((rows, width), BF16),
            *([message] * (extra.shape[0] - 1)),
        ],
        (),
        (merged, *received, mine, gain, extra),
        after,
    )


def slab_kernel(a_ref, b_ref, *refs):
    out_ref = refs[-1]
    rows = out_ref.shape[1]
    out_ref[0] = a_ref[:rows, :]
    out_ref[1] = b_ref[:rows, :]


def slab_pair(a, b, rows, after):
    [out] = call(slab_kernel, "slab", [pltpu.VMEM((2, rows, a.shape[1]), BF16)], (), (a, b), after)
    return out


PER_BLOCK = DK // SLOTS


def update_kernel(steps, blocks, keys_ref, delta_ref, total_ref, states_ref, *refs):
    out_ref, done_ref, left, right, olds, buffers, old_sems, sems = refs[-8:]
    loads = []
    for n, block in enumerate(blocks):
        span = pl.ds(block * PER_BLOCK, PER_BLOCK)
        loads.append(pltpu.make_async_copy(states_ref.at[span], olds.at[n], old_sems.at[n]))
        loads[-1].start()
    key_heads, rows, _ = keys_ref.shape
    seqs = rows // steps
    group = states_ref.shape[1] // key_heads
    first, count = blocks[0] * PER_BLOCK, len(blocks) * PER_BLOCK
    for i in range(key_heads):
        for at in range(SLOTS):
            rows_at = pl.ds(at, count, stride=SLOTS)
            t = at % steps
            k = keys_ref[i, t * seqs + first : t * seqs + first + count, :]
            k_high = k.astype(BF16).astype(F32)
            k = k - k_high if at >= 2 * steps else k_high
            left[i, rows_at, :] = k if at < 3 * steps else jnp.zeros_like(k)
            for u in range(group):
                d = delta_ref[i, t, first : first + count, u * DV : (u + 1) * DV]
                d_high = d.astype(BF16).astype(F32)
                d = d - d_high if steps <= at < 2 * steps else d_high
                right[i * group + u, rows_at, :] = d if at < 3 * steps else jnp.zeros_like(d)
    slot_of = lax.broadcasted_iota(jnp.int32, (DK, DK), 1) // SLOTS
    copies = []
    for n, block in enumerate(blocks):
        if n >= 2:
            copies[n - 2].wait()
        loads[n].wait()
        buffer = buffers.at[n % 2]
        span = slice(n * DK, (n + 1) * DK)
        for i in range(key_heads):
            lhs = jnp.transpose(left[i, span, :])
            rhs = jnp.concatenate([right[i * group + u, span, :] for u in range(group)], axis=1)
            rhs = rhs.astype(BF16)
            for m in range(PER_BLOCK):
                s = block * PER_BLOCK + m
                masked = jnp.where(slot_of == m, lhs, 0.0).astype(BF16)
                change = dot(masked, rhs)
                for u in range(group):
                    columns = slice(u * DV, (u + 1) * DV)
                    h = i * group + u
                    total = total_ref[i, s : s + 1, columns]
                    buffer[m, h] = olds[n, m, h] * total + change[:, columns]
        span = pl.ds(block * PER_BLOCK, PER_BLOCK)
        copies.append(pltpu.make_async_copy(buffer, out_ref.at[span], sems.at[n % 2]))
        copies[-1].start()
    for copy in copies[-2:]:
        copy.wait()
    done_ref[...] = jnp.zeros_like(done_ref)


def update(keys, deltas, totals, states, blocks, after, before=None):
    key_heads, steps, seqs, pair = deltas.shape
    rows = len(blocks) * DK
    value_heads = states.shape[1]
    loose = after if before is None else (before, *after)
    return call(
        functools.partial(update_kernel, steps, blocks),
        "update",
        [jax.ShapeDtypeStruct(states.shape, F32), jax.ShapeDtypeStruct((8, 128), F32)],
        (),
        (keys, deltas, totals),
        (pltpu.with_memory_space_constraint(states, pltpu.HBM), *loose),
        [
            pltpu.VMEM((key_heads, rows, DK), F32),
            pltpu.VMEM((value_heads, rows, DV), F32),
            pltpu.VMEM((len(blocks), PER_BLOCK, *states.shape[1:]), F32),
            pltpu.VMEM((2, PER_BLOCK, *states.shape[1:]), F32),
            pltpu.SemaphoreType.DMA((len(blocks),)),
            pltpu.SemaphoreType.DMA((2,)),
        ],
        None if before is None else {4: 0},
        [ANY_SPEC, VMEM_SPEC],
    )


def expert_in_kernel(orders, odd, first, me_ref, *refs):
    pieces = refs[: sum(map(len, orders))]
    refs = refs[len(pieces) :]
    gain_inv_ref, w_ref = refs[:2]
    if first:
        pre_ref, sq_ref = refs[-2:]
    else:
        pre_in, sq_in = refs[2:4]
        pre_ref, sq_ref = refs[-2:]
    me = me_ref[0]
    start, at = 0, 0
    for order in orders:
        blocks, xs = [], []
        for part in order:
            ref = pieces[at]
            at += 1
            _, zs, rows, width = ref.shape
            for n, place in enumerate(part):
                xs.append(ref[n].reshape(zs * rows, width))
                blocks.append(me ^ (2 * place + odd))
        spans = [pl.ds(pl.multiple_of(b * width, width), width) for b in blocks]
        span = slice(start, start + zs * rows)
        start += zs * rows
        for c in range(0, w_ref.shape[2], 256):
            columns = slice(c, c + 256)
            total = None if first else pre_in[span, columns]
            for x, where in zip(xs, spans):
                term = dot(x, w_ref[0, where, columns])
                total = term if total is None else total + term
            pre_ref[span, columns] = total
        squares = None
        for x, block in zip(xs, blocks):
            plain = x.astype(F32) * gain_inv_ref[block]
            plain = plain * plain
            for c in range(0, width, 128):
                part = plain[:, c : c + 128]
                squares = part if squares is None else squares + part
        squares = jnp.sum(squares, axis=1, keepdims=True)
        sq_ref[span, :] = squares if first else squares + sq_in[span, :]


def expert_in(me, sides, gain_inv, w, orders, odd, before=(), after=()):
    pieces = [piece for side in sides for piece in side]
    rows = pieces[0].shape[2]
    total = sum(side[0].shape[1] for side in sides) * rows
    return call(
        functools.partial(expert_in_kernel, orders, odd, not before),
        "expert_in",
        [pltpu.VMEM((total, w.shape[2]), F32), pltpu.VMEM((total, 1), F32)],
        (me,),
        (*pieces, gain_inv, w, *before),
        after,
    )


def expert_out_kernel(orders, steps, me_ref, pre_ref, sq_ref, extra_ref, w_ref, *refs):
    me = me_ref[0]
    messages, outs = refs[:-5], refs[-4:]
    features = w_ref.shape[2]
    hidden_width = w_ref.shape[1]
    start = 0
    for side, order in enumerate(orders):
        own, sib = outs[2 * side : 2 * side + 2]
        count, zs, rows, width = own.shape
        span = slice(start, start + zs * rows)
        start += zs * rows
        inverse = lax.rsqrt(sq_ref[span, :] / features + EPS)
        gate = pre_ref[span, :hidden_width] * inverse
        up = pre_ref[span, hidden_width:] * inverse
        hidden = (silu(gate) * up).astype(BF16)
        weight = []
        for z in range(side * zs, (side + 1) * zs):
            extra = messages[z - 1][rows:, :] if z else extra_ref[0]
            columns = jnp.transpose(extra.astype(F32))
            for t in range(steps):
                both = columns[:, t : t + 1] + columns[:, steps + t : steps + t + 1]
                weight.append(both[: rows // steps])
        weight = jnp.concatenate(weight, axis=0)
        for odd, ref in ((1, sib), (0, own)):
            for n in range(count):
                block = me ^ (2 * order[n] + odd)
                columns = pl.ds(pl.multiple_of(block * width, width), width)
                result = dot(hidden, w_ref[0, :, columns]) * weight
                ref[n] = result.astype(BF16).reshape(zs, rows, width)


def expert_out(me, pre, sq, extra, w, messages, orders, shapes, steps, after):
    return call(
        functools.partial(expert_out_kernel, orders, steps),
        "expert_out",
        [pltpu.VMEM(shape, BF16) for shape in shapes],
        (me,),
        (pre, sq, extra, w, *messages),
        after,
    )


def bit_reversed(count):
    bits = count.bit_length() - 1
    return [int(format(n, "b").zfill(bits)[::-1], 2) if bits else 0 for n in range(count)]


def add(a, b):
    return (a.astype(F32) + b.astype(F32)).astype(BF16)


def half_sum_kernel(a_ref, b_ref, *refs):
    keep_ref, send_ref = refs[-2:]
    half = a_ref.shape[0] // 2
    keep_ref[...] = add(a_ref[:half], b_ref[:half])
    send_ref[...] = add(a_ref[half:], b_ref[half:])


def half_sum(a, b, after=()):
    shape = (a.shape[0] // 2, *a.shape[1:])
    return call(
        half_sum_kernel,
        "half_sum",
        [pltpu.VMEM(shape, BF16), pltpu.VMEM(shape, BF16)],
        (),
        (a, b),
        after,
    )


def last_sum_kernel(a_ref, b_ref, *outs):
    for z, ref in enumerate(outs):
        ref[...] = add(a_ref[0, z], b_ref[0, z])


def last_sum(a, b):
    _, zs, rows, width = a.shape
    return call(last_sum_kernel, "last_sum", [pltpu.VMEM((rows, width), BF16)] * zs, (), (a, b))


def one_sum_kernel(a_ref, b_ref, *refs):
    refs[-1][...] = add(a_ref[...], b_ref[...])


def one_sum(a, b, after=()):
    [out] = call(one_sum_kernel, "one_sum", [pltpu.VMEM(a.shape, BF16)], (), (a, b), after)
    return out


def shared_in_kernel(me_ref, x_ref, w_ref, *refs):
    refs = refs[-2:]
    half = w_ref.shape[1] // 2
    part = half // 2
    pre = dot(x_ref[...], w_ref[...]).astype(BF16)
    odd = me_ref[0] % 2
    for core in range(2):
        for up in range(2):
            piece = pre[:, up * half + core * part : up * half + (core + 1) * part]

            @pl.when(odd == core)
            def _():
                refs[0][:, up * part : (up + 1) * part] = piece

            @pl.when(odd != core)
            def _():
                refs[1][:, up * part : (up + 1) * part] = piece


def shared_in(me, x, w, after):
    shape = (x.shape[0], w.shape[1] // 2)
    return call(
        shared_in_kernel, "shared_in", [pltpu.VMEM(shape, BF16)] * 2, (me,), (x, w), after
    )


def shared_hidden_kernel(features, a_ref, b_ref, sq_ref, out_ref):
    rows = a_ref.shape[0]
    half = a_ref.shape[1] // 2
    inverse = lax.rsqrt(sq_ref[:rows, :] / features + EPS)
    pre = (a_ref[...].astype(F32) + b_ref[...].astype(F32)) * inverse
    out_ref[...] = (silu(pre[:, :half]) * pre[:, half:]).astype(BF16)


def shared_hidden(features, a, b, sq):
    [out] = call(
        functools.partial(shared_hidden_kernel, features),
        "shared_hidden",
        [pltpu.VMEM((a.shape[0], a.shape[1] // 2), BF16)],
        (),
        (a, b, sq),
    )
    return out


def shared_out_kernel(me_ref, a_ref, b_ref, resid_ref, w_ref, out_ref):
    part = a_ref.shape[1]
    odd = me_ref[0] % 2
    total = resid_ref[...]
    for core, ref in ((odd, a_ref), (1 - odd, b_ref)):
        total = total + dot(ref[...], w_ref[pl.ds(pl.multiple_of(core * part, part), part), :])
    out_ref[...] = total


def shared_out(me, a, b, resid, w):
    [out] = call(
        shared_out_kernel, "shared_out", [pltpu.VMEM(resid.shape, F32)], (me,), (a, b, resid, w)
    )
    return out


def on_device(
    tokens,
    states,
    router_ids,
    router_weights,
    input_gain,
    w_query,
    w_key,
    w_value,
    w_zgate,
    w_beta,
    w_alpha,
    decay_scale,
    dt_bias,
    gated_gain,
    w_out,
    post_gain,
    w_shared_in,
    w_shared_out,
    w_expert_in,
    w_expert_out,
):
    seq_count = lax.axis_size("seq")
    head_count = lax.axis_size("head")
    head_index = lax.axis_index("head")
    seq_index = lax.axis_index("seq")
    me = head_index.astype(jnp.int32).reshape(1)
    seqs, steps, width = tokens.shape
    rows = seqs * steps
    features = head_count * width
    pairs = head_count // 2
    axes = [1 << n for n in range(1, head_count.bit_length() - 1)]

    mine = jnp.transpose(tokens, (1, 0, 2)).reshape(rows, width)
    value_heads = w_beta.shape[1]
    small = jnp.concatenate([w_beta, w_alpha], axis=1)
    small = jnp.transpose(small.reshape(head_count, width, 2 * value_heads), (0, 2, 1))
    small = jnp.pad(small, ((0, 0), (0, -2 * value_heads % 16), (0, 0)))
    pack = jnp.stack(
        [
            jnp.pad(decay_scale, (0, DV - value_heads)),
            jnp.pad(dt_bias, (0, DV - value_heads)),
            gated_gain,
        ]
    )

    neighbour = exchange(mine, "head", 1)
    [mine] = load((mine,))
    both = stack(mine, neighbour)
    gathered = [both] + [exchange(both, "head", 2 * p) for p in range(1, pairs)]
    w_query, w_key, w_value, w_zgate, w_shared_in, w_shared_out, gain, extra, gain_mine, gain_inv = bring(
        me,
        seq_index.astype(jnp.int32).reshape(1),
        (
            w_query,
            w_key,
            w_value,
            w_zgate,
            w_shared_in,
            w_shared_out,
            input_gain.reshape(head_count, 1, width),
        ),
        jnp.transpose(router_ids, (2, 1, 0)),
        jnp.transpose(router_weights, (2, 1, 0)),
        post_gain.reshape(head_count, 1, width),
        seq_count,
        both,
    )
    own, sib, keys, deltas, totals = front(
        me, gathered, gain, small, pack, w_query, w_key, w_value, w_zgate, w_out, states, steps
    )

    merged = one_sum(own, exchange(sib, "head", 1))
    received = [exchange(merged[p], "head", 2 * p) for p in range(1, pairs)]
    w_in, w_down = load((w_expert_in, w_expert_out), (merged,))
    resid, x, *messages = make_rows(merged, received, mine, gain_mine, extra, (w_in,))

    half = seq_count // 2
    messages = [exchange(m, "seq", z + 1) for z, m in enumerate(messages)]
    slabs = [x] + messages
    natural, reverse = list(range(pairs)), bit_reversed(pairs)
    blocks = tuple(range(seqs // PER_BLOCK))
    cut = len(blocks) // 2
    shared_pre, sent = shared_in(me, x, w_shared_in, (messages[0],))
    shared_pre = one_sum(shared_pre, exchange(sent, "head", 1))
    shared_received = exchange(shared_pre, "head", axes[0])
    sides, tie = [], ()
    for slab, bits in ((slabs[:half], axes), (slabs[half:], axes[::-1])):
        if half == 2:
            side = slab_pair(*slab, rows, tie)[None]
        else:
            side = jnp.stack([m[:rows] for m in slab])[None]
        if not tie:
            states_out, done_1 = update(keys, deltas, totals, states, blocks[:cut], (messages[0],))
            tie = (done_1, shared_pre)
        for bit in bits[:-1]:
            received = exchange(side, "head", bit)
            if side.shape[0] == 1:
                side = stack(side[0], received[0])
            else:
                side = jnp.concatenate([side, received])
        sides.append([side, exchange(side, "head", bits[-1])])
    siblings = [[exchange(piece, "head", 1) for piece in side] for side in sides]
    middle = pairs // 2
    orders = tuple((tuple(o[:middle]), tuple(o[middle:])) for o in (natural, reverse))

    pre = expert_in(me, sides, gain_inv, w_in, orders, 0, after=(done_1,))
    pre, squares = expert_in(me, siblings, gain_inv, w_in, orders, 1, pre)
    shape = (pairs, half, rows, width)
    a_own, a_sib, b_own, b_sib = expert_out(
        me, pre, squares, extra, w_down, messages, (reverse, natural), (shape,) * 4, steps, (shared_received,)
    )
    owns = [a_own, b_own]
    received = [exchange(sib, "head", 1) for sib in (a_sib, b_sib)]
    tie = ()
    for n, bits in enumerate(zip(axes, axes[::-1])):
        for side, bit in enumerate(bits):
            owns[side], sent = half_sum(owns[side], received[side], tie)
            received[side] = exchange(sent, "head", bit)
        if n == 0:
            states_out, done_2 = update(
                keys, deltas, totals, states, blocks[cut:], tuple(owns), states_out
            )
            tie = (done_2,)
        else:
            shared_pre = one_sum(shared_pre, shared_received, (owns[1],))
            shared_received = exchange(shared_pre, "head", axes[n])
    hidden = shared_hidden(features, shared_pre, shared_received, squares)
    base = shared_out(me, hidden, exchange(hidden, "head", 1), resid, w_shared_out)
    slabs = []
    for side in range(2):
        slabs += last_sum(owns[side], received[side])
    result = base + slabs[0].astype(F32)
    for z in range(1, seq_count):
        result = result + exchange(slabs[z], "seq", z).astype(F32)
    layer_out = jnp.transpose(result.astype(BF16).reshape(steps, seqs, width), (1, 0, 2))
    return (layer_out, states_out)


def solution(mesh):
    in_specs = (
        P("seq", None, "head"),
        P("seq", "head", None, None),
        P("seq", None, None),
        P("seq", None, None),
        P(),
        P(None, "head"),
        P(None, "head"),
        P(None, "head"),
        P(None, "head"),
        P(None, "head"),
        P(None, "head"),
        P("head"),
        P("head"),
        P(),
        P("head", None),
        P(),
        P("head", None),
        P(None, "head"),
        P(("seq", "head"), None, None),
        P(("seq", "head"), None, None),
    )
    out_specs = (P("seq", None, "head"), P("seq", "head", None, None))
    return jax.shard_map(
        on_device, mesh=mesh, in_specs=in_specs, out_specs=out_specs, check_vma=False
    )
```

```python
import functools

import jax
import jax.numpy as jnp
from jax import lax
from jax.experimental import pallas as pl
from jax.experimental.pallas import tpu as pltpu
from jax.sharding import PartitionSpec as P

DK = 128
DV = 128
EPS = 1e-06
SLOTS = 16
F32 = jnp.float32
BF16 = jnp.bfloat16
VMEM_LIMIT = 24 * 1024 * 1024


def dot(a, b):
    return jnp.dot(a, b, preferred_element_type=F32)


def silu(v):
    return v / (1.0 + jnp.exp(-v))


def split(v):
    high = v.astype(BF16)
    low = (v - high.astype(F32)).astype(BF16)
    return high, low


def pin(x):
    return pltpu.with_memory_space_constraint(x, pltpu.VMEM)


VMEM_SPEC = pl.BlockSpec(memory_space=pltpu.VMEM)
SMEM_SPEC = pl.BlockSpec(memory_space=pltpu.SMEM)
ANY_SPEC = pl.BlockSpec(memory_space=pl.ANY)


def call(body, name, out_shapes, smem, pinned, loose=(), scratch=(), aliases=None, outs=None):
    return pl.pallas_call(
        body,
        out_shape=tuple(out_shapes),
        in_specs=[SMEM_SPEC] * len(smem) + [VMEM_SPEC] * len(pinned) + [ANY_SPEC] * len(loose),
        out_specs=tuple(outs or [VMEM_SPEC] * len(out_shapes)),
        scratch_shapes=list(scratch),
        input_output_aliases=aliases or {},
        compiler_params=pltpu.CompilerParams(vmem_limit_bytes=VMEM_LIMIT),
        name=name,
    )(*smem, *(pin(x) for x in pinned), *loose)


def exchange(x, axis, bit):
    size = lax.axis_size(axis)
    return lax.ppermute(x, axis, [(i, i ^ bit) for i in range(size)])


def stack_kernel(*refs):
    for n, ref in enumerate(refs[:-1]):
        refs[-1][n] = ref[...]


def stack(*arrays):
    shape = (len(arrays), *arrays[0].shape)
    [out] = call(stack_kernel, "stack", [pltpu.VMEM(shape, arrays[0].dtype)], (), arrays)
    return out


def load_kernel(count, *refs):
    sources, targets, sems = refs[:count], refs[-1 - count : -1], refs[-1]
    copies = [pltpu.make_async_copy(a, b, sems.at[n]) for n, (a, b) in enumerate(zip(sources, targets))]
    for copy in copies:
        copy.start()
    for copy in copies:
        copy.wait()


def load(arrays, after=()):
    return call(
        functools.partial(load_kernel, len(arrays)),
        "load",
        [pltpu.VMEM(x.shape, x.dtype) for x in arrays],
        (),
        (),
        (*(pltpu.with_memory_space_constraint(x, pltpu.HBM) for x in arrays), *after),
        [pltpu.SemaphoreType.DMA((len(arrays),))],
    )


def bring_kernel(count, vectors, seq_count, head_count, me_ref, seq_ref, *refs):
    small = 3 + vectors
    sources, refs = refs[: small + count], refs[small + count :]
    targets, (pack_ref, extra_ref, gain_mine_ref, gain_inv_ref) = refs[:count], refs[count : count + 4]
    scratch, sems = refs[count + 4 : -1], refs[-1]
    ids, chosen, gain_after = scratch[:3]
    targets = (*scratch, *targets)
    copies = [pltpu.make_async_copy(a, b, sems.at[n]) for n, (a, b) in enumerate(zip(sources, targets))]
    for copy in copies:
        copy.start()
    for copy in copies[:small]:
        copy.wait()
    for n, ref in enumerate(scratch[3:]):
        pack_ref[n : n + 1, : ref.shape[1]] = ref[...]
    me, seq = me_ref[0], seq_ref[0]
    gain_mine_ref[...] = gain_after[me]
    gain_inv_ref[...] = 1.0 / gain_after[...]
    top, steps, seqs = ids.shape
    for z in range(seq_count):
        target = (seq ^ z) * head_count + me
        weight = jnp.zeros((steps, seqs), F32)
        for n in range(top):
            weight = weight + jnp.where(ids[n] == target, chosen[n], 0.0)
        high = weight.astype(BF16).astype(F32)
        both = jnp.concatenate([high, weight - high], axis=0)
        rows, width = extra_ref.shape[1:]
        both = jnp.concatenate([both, jnp.zeros((rows - 2 * steps, seqs), F32)], axis=0)
        both = jnp.concatenate([both, jnp.zeros((rows, width - seqs), F32)], axis=1)
        extra_ref[z] = both.astype(BF16)
    for copy in copies[small:]:
        copy.wait()


def bring(me, seq, arrays, vectors, ids, chosen, gain_after, seq_count):
    head_count, _, width = gain_after.shape
    small = (ids, chosen, gain_after, *vectors)
    return call(
        functools.partial(bring_kernel, len(arrays), len(vectors), seq_count, head_count),
        "bring",
        [pltpu.VMEM(x.shape, x.dtype) for x in arrays]
        + [
            pltpu.VMEM((8, 128), F32),
            pltpu.VMEM((seq_count, 16, width), BF16),
            pltpu.VMEM((1, width), F32),
            pltpu.VMEM(gain_after.shape, F32),
        ],
        (me, seq),
        (),
        [pltpu.with_memory_space_constraint(x, pltpu.HBM) for x in (*small, *arrays)],
        [pltpu.VMEM(x.shape, x.dtype) for x in small]
        + [pltpu.SemaphoreType.DMA((len(small) + len(arrays),))],
    )


def front_kernel(
    steps,
    head_count,
    me_ref,
    *refs,
):
    x_refs = refs[:2]
    (
        gain_ref,
        small_ref,
        pack_ref,
        wq,
        wk,
        wv,
        wz,
        wo_hbm,
        states_hbm,
        own_ref,
        sib_ref,
        keys_ref,
        delta_ref,
        total_ref,
        wo,
        states,
        left,
        recalls,
        sems,
    ) = refs[2:]
    me = me_ref[0]
    _, rows, width = x_refs[0].shape
    seqs = rows // steps
    key_heads = wq.shape[1] // DK
    value_heads = wv.shape[1] // DV
    group = value_heads // key_heads
    pair = group * DV

    parts = sems.shape[0] - 1
    part = seqs // parts
    copies = []
    for n in range(parts):
        span = pl.ds(n * part, part)
        copies.append(pltpu.make_async_copy(states_hbm.at[span], states.at[span], sems.at[n]))
    copies.append(pltpu.make_async_copy(wo_hbm, wo, sems.at[parts]))
    for copy in copies:
        copy.start()

    squares = jnp.zeros((rows, 1), F32)
    for j in range(head_count):
        xj = x_refs[j % 2][j // 2].astype(F32)
        squares = squares + jnp.sum(xj * xj, axis=1, keepdims=True)
    inverse = lax.rsqrt(squares / (head_count * width) + EPS)
    normed = []
    spans = []
    for j in range(head_count):
        block = me ^ j
        normed.append((x_refs[j % 2][j // 2].astype(F32) * inverse * gain_ref[block]).astype(BF16))
        spans.append(pl.ds(pl.multiple_of(block * width, width), width))

    def project(w_ref):
        total = None
        for j in range(head_count):
            term = dot(normed[j], w_ref[spans[j], :])
            total = term if total is None else total + term
        return total

    small = None
    for j in range(head_count):
        term = lax.dot_general(
            normed[j],
            small_ref[me ^ j],
            (((1,), (1,)), ((), ())),
            preferred_element_type=F32,
        )
        small = term if small is None else small + term
    betas = 1.0 / (1.0 + jnp.exp(-small[:, :value_heads]))
    alphas = small[:, value_heads : 2 * value_heads] + pack_ref[1:2, :value_heads]
    softplus = jnp.maximum(alphas, 0.0) + jnp.log1p(jnp.exp(-jnp.abs(alphas)))
    decays = jnp.exp(-pack_ref[0:1, :value_heads] * softplus)

    def units(v):
        return v * lax.rsqrt(jnp.sum(v * v, axis=1, keepdims=True) + EPS)

    queries_all = silu(project(wq))
    keys_all = silu(project(wk))
    keys, queries = [], []
    for i in range(key_heads):
        k = units(keys_all[:, i * DK : (i + 1) * DK])
        q = units(queries_all[:, i * DK : (i + 1) * DK]) * DK ** (-0.5)
        keys_ref[i] = k
        keys.append([k[t * seqs : (t + 1) * seqs] for t in range(steps)])
        queries.append([q[t * seqs : (t + 1) * seqs] for t in range(steps)])
        for t in range(steps):
            for at, v in ((t, keys[i][t]), (steps + t, queries[i][t])):
                high = v.astype(BF16).astype(F32)
                left[i, pl.ds(at, seqs, stride=SLOTS), :] = high
                left[i, pl.ds(2 * steps + at, seqs, stride=SLOTS), :] = v - high
        for at in range(4 * steps, SLOTS):
            left[i, pl.ds(at, seqs, stride=SLOTS), :] = jnp.zeros((seqs, DK), F32)
    values_all = silu(project(wv))
    gates = silu(project(wz))

    def one(s, carry):
        base = pl.multiple_of(s * SLOTS, SLOTS)
        for i in range(key_heads):
            lhs = left[i, pl.ds(base, SLOTS), :].astype(BF16)
            rhs = jnp.concatenate([states[s, i * group + u] for u in range(group)], axis=1)
            high, low = split(rhs)
            answer = dot(jnp.concatenate([lhs, lhs], axis=1), jnp.concatenate([high, low], axis=0))
            for u in range(group):
                recalls[i * group + u, pl.ds(base, SLOTS), :] = answer[:, u * DV : (u + 1) * DV]
        return carry

    for n in range(parts):
        copies[n].wait()
        lax.fori_loop(n * part, (n + 1) * part, one, 0, unroll=4)

    def wide(columns, t, i):
        return jnp.concatenate(
            [
                jnp.broadcast_to(
                    columns[t * seqs : (t + 1) * seqs, i * group + u : i * group + u + 1],
                    (seqs, DV),
                )
                for u in range(group)
            ],
            axis=1,
        )

    mixed_rows = [[] for _ in range(steps)]
    for i in range(key_heads):
        decay = [wide(decays, t, i) for t in range(steps)]
        beta = [wide(betas, t, i) for t in range(steps)]

        def read(at):
            return jnp.concatenate(
                [
                    recalls[i * group + u, pl.ds(at, seqs, stride=SLOTS), :]
                    + recalls[i * group + u, pl.ds(2 * steps + at, seqs, stride=SLOTS), :]
                    for u in range(group)
                ],
                axis=1,
            )

        deltas = []
        running = None
        for t in range(steps):
            running = decay[t] if running is None else running * decay[t]
            recall = running * read(t)
            answer = running * read(steps + t)
            deltas = [d * decay[t] for d in deltas]
            for u, d in enumerate(deltas):
                recall = recall + d * jnp.sum(keys[i][t] * keys[i][u], axis=1, keepdims=True)
                answer = answer + d * jnp.sum(queries[i][t] * keys[i][u], axis=1, keepdims=True)
            value = values_all[t * seqs : (t + 1) * seqs, i * pair : (i + 1) * pair]
            delta = beta[t] * (value - recall)
            answer = answer + delta * jnp.sum(queries[i][t] * keys[i][t], axis=1, keepdims=True)
            deltas.append(delta)
            mixed_rows[t].append(answer)
        for t in range(steps):
            delta_ref[i, t] = deltas[t]
        total_ref[i] = running
    mixed = jnp.concatenate([jnp.concatenate(m, axis=1) for m in mixed_rows], axis=0)
    gated = []
    for h in range(value_heads):
        m = mixed[:, h * DV : (h + 1) * DV]
        m = m * lax.rsqrt(jnp.mean(m * m, axis=1, keepdims=True) + EPS)
        gated.append((m * pack_ref[2:3, :DV] * gates[:, h * DV : (h + 1) * DV]).astype(BF16))
    gated = jnp.concatenate(gated, axis=1)
    copies[parts].wait()
    for c in range(head_count):
        piece = dot(gated, wo[:, c * width : (c + 1) * width]).astype(BF16)
        away = me ^ c

        @pl.when(away % 2 == 0)
        def _():
            own_ref[away // 2] = piece

        @pl.when(away % 2 == 1)
        def _():
            sib_ref[away // 2] = piece


def front(me, xs, gain, small, pack, wq, wk, wv, wz, wo, states, steps):
    pairs, rows, width = xs[0].shape
    head_count = 2 * pairs
    seqs = rows // steps
    key_heads = wq.shape[1] // DK
    value_heads = wv.shape[1] // DV
    pair = value_heads // key_heads * DV
    return call(
        functools.partial(front_kernel, steps, head_count),
        "front",
        [
            pltpu.VMEM((head_count // 2, rows, width), BF16),
            pltpu.VMEM((head_count // 2, rows, width), BF16),
            pltpu.VMEM((key_heads, rows, DK), F32),
            pltpu.VMEM((key_heads, steps, seqs, pair), F32),
            pltpu.VMEM((key_heads, seqs, pair), F32),
        ],
        (me,),
        (*xs, gain, small, pack, wq, wk, wv, wz),
        [pltpu.with_memory_space_constraint(x, pltpu.HBM) for x in (wo, states)],
        [
            pltpu.VMEM(wo.shape, BF16),
            pltpu.VMEM(states.shape, F32),
            pltpu.VMEM((key_heads, seqs * SLOTS, DK), F32),
            pltpu.VMEM((value_heads, seqs * SLOTS, DV), F32),
            pltpu.SemaphoreType.DMA((5,)),
        ],
    )


def rows_kernel(pairs, *refs):
    merged_ref, received = refs[0], refs[1:pairs]
    mine_ref, gain_ref, extra_ref, _ = refs[pairs : pairs + 4]
    resid_ref, x_ref = refs[pairs + 4 : pairs + 6]
    messages = refs[pairs + 6 :]
    rows = mine_ref.shape[0]
    resid = mine_ref[...].astype(F32) + merged_ref[0].astype(F32)
    for ref in received:
        resid = resid + ref[...].astype(F32)
    resid_ref[...] = resid
    x = (resid * gain_ref[...]).astype(BF16)
    x_ref[...] = x
    for z, ref in enumerate(messages):
        ref[:rows, :] = x
        ref[rows:, :] = extra_ref[z + 1]


def make_rows(merged, received, mine, gain, extra, after):
    rows, width = mine.shape
    message = pltpu.VMEM((rows + extra.shape[1], width), BF16)
    return call(
        functools.partial(rows_kernel, merged.shape[0]),
        "rows",
        [
            pltpu.VMEM((rows, width), F32),
            pltpu.VMEM((rows, width), BF16),
            *([message] * (extra.shape[0] - 1)),
        ],
        (),
        (merged, *received, mine, gain, extra),
        after,
    )


def slab_kernel(a_ref, b_ref, *refs):
    out_ref = refs[-1]
    rows = out_ref.shape[1]
    out_ref[0] = a_ref[:rows, :]
    out_ref[1] = b_ref[:rows, :]


def slab_pair(a, b, rows, after):
    [out] = call(slab_kernel, "slab", [pltpu.VMEM((2, rows, a.shape[1]), BF16)], (), (a, b), after)
    return out


PER_BLOCK = DK // SLOTS


def update_kernel(steps, blocks, keys_ref, delta_ref, total_ref, states_ref, *refs):
    out_ref, done_ref, left, right, olds, buffers, old_sems, sems = refs[-8:]
    loads = []
    for n, block in enumerate(blocks):
        span = pl.ds(block * PER_BLOCK, PER_BLOCK)
        loads.append(pltpu.make_async_copy(states_ref.at[span], olds.at[n], old_sems.at[n]))
        loads[-1].start()
    key_heads, rows, _ = keys_ref.shape
    seqs = rows // steps
    group = states_ref.shape[1] // key_heads
    first, count = blocks[0] * PER_BLOCK, len(blocks) * PER_BLOCK
    for i in range(key_heads):
        for at in range(SLOTS):
            rows_at = pl.ds(at, count, stride=SLOTS)
            t = at % steps
            k = keys_ref[i, t * seqs + first : t * seqs + first + count, :]
            k_high = k.astype(BF16).astype(F32)
            k = k - k_high if at >= 2 * steps else k_high
            left[i, rows_at, :] = k if at < 3 * steps else jnp.zeros_like(k)
            for u in range(group):
                d = delta_ref[i, t, first : first + count, u * DV : (u + 1) * DV]
                d_high = d.astype(BF16).astype(F32)
                d = d - d_high if steps <= at < 2 * steps else d_high
                right[i * group + u, rows_at, :] = d if at < 3 * steps else jnp.zeros_like(d)
    slot_of = lax.broadcasted_iota(jnp.int32, (DK, DK), 1) // SLOTS
    copies = []
    for n, block in enumerate(blocks):
        if n >= 2:
            copies[n - 2].wait()
        loads[n].wait()
        buffer = buffers.at[n % 2]
        span = slice(n * DK, (n + 1) * DK)
        for i in range(key_heads):
            lhs = jnp.transpose(left[i, span, :])
            rhs = jnp.concatenate([right[i * group + u, span, :] for u in range(group)], axis=1)
            rhs = rhs.astype(BF16)
            for m in range(PER_BLOCK):
                s = block * PER_BLOCK + m
                masked = jnp.where(slot_of == m, lhs, 0.0).astype(BF16)
                change = dot(masked, rhs)
                for u in range(group):
                    columns = slice(u * DV, (u + 1) * DV)
                    h = i * group + u
                    total = total_ref[i, s : s + 1, columns]
                    buffer[m, h] = olds[n, m, h] * total + change[:, columns]
        span = pl.ds(block * PER_BLOCK, PER_BLOCK)
        copies.append(pltpu.make_async_copy(buffer, out_ref.at[span], sems.at[n % 2]))
        copies[-1].start()
    for copy in copies[-2:]:
        copy.wait()
    done_ref[...] = jnp.zeros_like(done_ref)


def update(keys, deltas, totals, states, blocks, after, before=None):
    key_heads, steps, seqs, pair = deltas.shape
    rows = len(blocks) * DK
    value_heads = states.shape[1]
    loose = after if before is None else (before, *after)
    return call(
        functools.partial(update_kernel, steps, blocks),
        "update",
        [jax.ShapeDtypeStruct(states.shape, F32), jax.ShapeDtypeStruct((8, 128), F32)],
        (),
        (keys, deltas, totals),
        (pltpu.with_memory_space_constraint(states, pltpu.HBM), *loose),
        [
            pltpu.VMEM((key_heads, rows, DK), F32),
            pltpu.VMEM((value_heads, rows, DV), F32),
            pltpu.VMEM((len(blocks), PER_BLOCK, *states.shape[1:]), F32),
            pltpu.VMEM((2, PER_BLOCK, *states.shape[1:]), F32),
            pltpu.SemaphoreType.DMA((len(blocks),)),
            pltpu.SemaphoreType.DMA((2,)),
        ],
        None if before is None else {4: 0},
        [ANY_SPEC, VMEM_SPEC],
    )


def blocks_of(pieces, order, odd, me):
    xs, places = [], []
    for ref, part in zip(pieces, order):
        _, zs, rows, width = ref.shape
        for n, place in enumerate(part):
            xs.append(ref[n].reshape(zs * rows, width))
            places.append(me ^ (2 * place + odd))
    return xs, places


def rows_squares(xs, places, gain_inv_ref):
    squares = None
    for x, place in zip(xs, places):
        plain = x.astype(F32) * gain_inv_ref[place]
        plain = plain * plain
        for c in range(0, x.shape[1], 128):
            part = plain[:, c : c + 128]
            squares = part if squares is None else squares + part
    return jnp.sum(squares, axis=1, keepdims=True)


def columns_sum(total, xs, places, w_ref, columns):
    for x, place in zip(xs, places):
        width = x.shape[1]
        term = dot(x, w_ref[0, pl.ds(pl.multiple_of(place * width, width), width), columns])
        total = term if total is None else total + term
    return total


def expert_first_kernel(order, me_ref, *refs):
    pieces, (gain_inv_ref, w_ref) = refs[: len(order)], refs[len(order) : len(order) + 2]
    pre_ref, sq_ref = refs[-2:]
    xs, places = blocks_of(pieces, order, 0, me_ref[0])
    for c in range(0, w_ref.shape[2], 256):
        columns = slice(c, c + 256)
        pre_ref[:, columns] = columns_sum(None, xs, places, w_ref, columns)
    sq_ref[...] = rows_squares(xs, places, gain_inv_ref)


def expert_first(me, pieces, gain_inv, w, order, after=()):
    total = pieces[0].shape[1] * pieces[0].shape[2]
    return call(
        functools.partial(expert_first_kernel, order),
        "expert_first",
        [pltpu.VMEM((total, w.shape[2]), F32), pltpu.VMEM((total, 1), F32)],
        (me,),
        (*pieces, gain_inv, w),
        after,
    )


def expert_rest_kernel(order, order_out, steps, whole, me_ref, *refs):
    pieces, refs = refs[: len(order)], refs[len(order) :]
    gain_inv_ref, w_ref, pre_ref, sq_ref, down_ref = refs[:5]
    own, sib, sq_out = refs[-3:]
    me = me_ref[0]
    features = down_ref.shape[2]
    hidden_width = down_ref.shape[1]
    count, zs, rows, width = own.shape
    xs, places = blocks_of(pieces, order, 1, me)
    squares = sq_ref[...] + rows_squares(xs, places, gain_inv_ref)
    sq_out[...] = squares
    inverse = lax.rsqrt(squares / features + EPS)
    hidden = []
    for c in range(0, hidden_width, 256):
        parts = []
        for at in (c, hidden_width + c):
            columns = slice(at, at + 256)
            parts.append(columns_sum(pre_ref[:, columns], xs, places, w_ref, columns) * inverse)
        hidden.append((silu(parts[0]) * parts[1]).astype(BF16))
    hidden = jnp.concatenate(hidden, axis=1)
    weight = []
    for z in range(zs):
        ref = refs[5 + z]
        extra = ref[0] if z == 0 and whole else ref[rows:, :]
        columns = jnp.transpose(extra.astype(F32))
        for t in range(steps):
            both = columns[:, t : t + 1] + columns[:, steps + t : steps + t + 1]
            weight.append(both[: rows // steps])
    weight = jnp.concatenate(weight, axis=0)
    for odd, ref in ((1, sib), (0, own)):
        for n in range(count):
            block = me ^ (2 * order_out[n] + odd)
            columns = pl.ds(pl.multiple_of(block * width, width), width)
            result = dot(hidden, down_ref[0, :, columns]) * weight
            ref[n] = result.astype(BF16).reshape(zs, rows, width)


def expert_rest(me, pieces, gain_inv, w, pre, sq, down, weights, order, order_out, steps, whole, after):
    count = 2 * pieces[0].shape[0]
    shape = (count, *pieces[0].shape[1:])
    return call(
        functools.partial(expert_rest_kernel, order, order_out, steps, whole),
        "expert_rest",
        [pltpu.VMEM(shape, BF16), pltpu.VMEM(shape, BF16), pltpu.VMEM(sq.shape, F32)],
        (me,),
        (*pieces, gain_inv, w, pre, sq, down, *weights),
        after,
    )


def bit_reversed(count):
    bits = count.bit_length() - 1
    return [int(format(n, "b").zfill(bits)[::-1], 2) if bits else 0 for n in range(count)]


def add(a, b):
    return (a.astype(F32) + b.astype(F32)).astype(BF16)


def half_sum_kernel(a_ref, b_ref, *refs):
    keep_ref, send_ref = refs[-2:]
    half = a_ref.shape[0] // 2
    keep_ref[...] = add(a_ref[:half], b_ref[:half])
    send_ref[...] = add(a_ref[half:], b_ref[half:])


def half_sum(a, b, after=()):
    shape = (a.shape[0] // 2, *a.shape[1:])
    return call(
        half_sum_kernel,
        "half_sum",
        [pltpu.VMEM(shape, BF16), pltpu.VMEM(shape, BF16)],
        (),
        (a, b),
        after,
    )


def last_sum_kernel(a_ref, b_ref, *outs):
    for z, ref in enumerate(outs):
        ref[...] = add(a_ref[0, z], b_ref[0, z])


def last_sum(a, b):
    _, zs, rows, width = a.shape
    return call(last_sum_kernel, "last_sum", [pltpu.VMEM((rows, width), BF16)] * zs, (), (a, b))


def one_sum_kernel(a_ref, b_ref, *refs):
    refs[-1][...] = add(a_ref[...], b_ref[...])


def one_sum(a, b, after=()):
    [out] = call(one_sum_kernel, "one_sum", [pltpu.VMEM(a.shape, BF16)], (), (a, b), after)
    return out


def shared_in_kernel(me_ref, x_ref, w_ref, *refs):
    refs = refs[-2:]
    half = w_ref.shape[1] // 2
    part = half // 2
    pre = dot(x_ref[...], w_ref[...]).astype(BF16)
    odd = me_ref[0] % 2
    for core in range(2):
        for up in range(2):
            piece = pre[:, up * half + core * part : up * half + (core + 1) * part]

            @pl.when(odd == core)
            def _():
                refs[0][:, up * part : (up + 1) * part] = piece

            @pl.when(odd != core)
            def _():
                refs[1][:, up * part : (up + 1) * part] = piece


def shared_in(me, x, w, after):
    shape = (x.shape[0], w.shape[1] // 2)
    return call(
        shared_in_kernel, "shared_in", [pltpu.VMEM(shape, BF16)] * 2, (me,), (x, w), after
    )


def shared_hidden_kernel(features, a_ref, b_ref, sq_ref, out_ref):
    rows = a_ref.shape[0]
    half = a_ref.shape[1] // 2
    inverse = lax.rsqrt(sq_ref[:rows, :] / features + EPS)
    pre = (a_ref[...].astype(F32) + b_ref[...].astype(F32)) * inverse
    out_ref[...] = (silu(pre[:, :half]) * pre[:, half:]).astype(BF16)


def shared_hidden(features, a, b, sq):
    [out] = call(
        functools.partial(shared_hidden_kernel, features),
        "shared_hidden",
        [pltpu.VMEM((a.shape[0], a.shape[1] // 2), BF16)],
        (),
        (a, b, sq),
    )
    return out


def shared_out_kernel(me_ref, a_ref, b_ref, resid_ref, w_ref, out_ref):
    part = a_ref.shape[1]
    odd = me_ref[0] % 2
    total = resid_ref[...]
    for core, ref in ((odd, a_ref), (1 - odd, b_ref)):
        total = total + dot(ref[...], w_ref[pl.ds(pl.multiple_of(core * part, part), part), :])
    out_ref[...] = total


def shared_out(me, a, b, resid, w):
    [out] = call(
        shared_out_kernel, "shared_out", [pltpu.VMEM(resid.shape, F32)], (me,), (a, b, resid, w)
    )
    return out


def on_device(
    tokens,
    states,
    router_ids,
    router_weights,
    input_gain,
    w_query,
    w_key,
    w_value,
    w_zgate,
    w_beta,
    w_alpha,
    decay_scale,
    dt_bias,
    gated_gain,
    w_out,
    post_gain,
    w_shared_in,
    w_shared_out,
    w_expert_in,
    w_expert_out,
):
    seq_count = lax.axis_size("seq")
    head_count = lax.axis_size("head")
    head_index = lax.axis_index("head")
    seq_index = lax.axis_index("seq")
    me = head_index.astype(jnp.int32).reshape(1)
    seqs, steps, width = tokens.shape
    rows = seqs * steps
    features = head_count * width
    pairs = head_count // 2
    axes = [1 << n for n in range(1, head_count.bit_length() - 1)]

    mine = jnp.transpose(tokens, (1, 0, 2)).reshape(rows, width)
    value_heads = w_beta.shape[1]
    small = jnp.concatenate([w_beta, w_alpha], axis=1)
    small = jnp.transpose(small.reshape(head_count, width, 2 * value_heads), (0, 2, 1))
    small = jnp.pad(small, ((0, 0), (0, -2 * value_heads % 16), (0, 0)))

    others = [exchange(mine, "head", 2 * p) for p in range(1, pairs)]
    mine, w_query, w_key, w_shared_in, w_shared_out, gain, pack, extra, gain_mine, gain_inv = bring(
        me,
        seq_index.astype(jnp.int32).reshape(1),
        (
            mine,
            w_query,
            w_key,
            w_shared_in,
            w_shared_out,
            input_gain.reshape(head_count, 1, width),
        ),
        [v.reshape(1, -1) for v in (decay_scale, dt_bias, gated_gain)],
        jnp.transpose(router_ids, (2, 1, 0)),
        jnp.transpose(router_weights, (2, 1, 0)),
        post_gain.reshape(head_count, 1, width),
        seq_count,
    )
    own_tokens = stack(mine, *others)
    sib_tokens = exchange(own_tokens, "head", 1)
    w_value, w_zgate = load((w_value, w_zgate), (own_tokens,))
    gathered = (own_tokens, sib_tokens)
    own, sib, keys, deltas, totals = front(
        me, gathered, gain, small, pack, w_query, w_key, w_value, w_zgate, w_out, states, steps
    )

    merged = one_sum(own, exchange(sib, "head", 1))
    received = [exchange(merged[p], "head", 2 * p) for p in range(1, pairs)]
    w_in, w_down = load((w_expert_in, w_expert_out), (merged,))
    resid, x, *messages = make_rows(merged, received, mine, gain_mine, extra, (w_in,))

    half = seq_count // 2
    messages = [exchange(m, "seq", z + 1) for z, m in enumerate(messages)]
    slabs = [x] + messages
    natural, reverse = list(range(pairs)), bit_reversed(pairs)
    blocks = tuple(range(seqs // PER_BLOCK))
    cut = len(blocks) // 2
    shared_pre, sent = shared_in(me, x, w_shared_in, ())
    shared_pre = one_sum(shared_pre, exchange(sent, "head", 1))
    shared_received = exchange(shared_pre, "head", axes[0])
    sides, tie = [], ()
    for slab, bits in ((slabs[:half], axes), (slabs[half:], axes[::-1])):
        if half == 2:
            side = slab_pair(*slab, rows, tie)[None]
        else:
            side = jnp.stack([m[:rows] for m in slab])[None]
        if not tie:
            states_out, done_1 = update(keys, deltas, totals, states, blocks[:cut], (messages[0],))
            tie = (done_1, shared_pre)
        for bit in bits[:-1]:
            received = exchange(side, "head", bit)
            if side.shape[0] == 1:
                side = stack(side[0], received[0])
            else:
                side = jnp.concatenate([side, received])
        sides.append([side, exchange(side, "head", bits[-1])])
    siblings = [[exchange(piece, "head", 1) for piece in side] for side in sides]
    middle = pairs // 2
    orders = tuple((tuple(o[:middle]), tuple(o[middle:])) for o in (natural, reverse))

    firsts = [
        expert_first(me, side, gain_inv, w_in, order, (done_1,)) for side, order in zip(sides, orders)
    ]
    owns, sibs, squares = [], [], []
    weights = (extra, *messages)
    ties = ((), (shared_received,))
    for n, order_out in enumerate((reverse, natural)):
        own, sib, square = expert_rest(
            me,
            siblings[n],
            gain_inv,
            w_in,
            *firsts[n],
            w_down,
            weights[n * half : (n + 1) * half],
            orders[n],
            order_out,
            steps,
            n == 0,
            ties[n],
        )
        owns.append(own)
        sibs.append(sib)
        squares.append(square)
    received = [exchange(sib, "head", 1) for sib in sibs]
    tie = ()
    for n, bits in enumerate(zip(axes, axes[::-1])):
        for side, bit in enumerate(bits):
            owns[side], sent = half_sum(owns[side], received[side], tie)
            received[side] = exchange(sent, "head", bit)
        if n == 0:
            states_out, done_2 = update(
                keys, deltas, totals, states, blocks[cut:], tuple(owns), states_out
            )
            tie = (done_2,)
        else:
            shared_pre = one_sum(shared_pre, shared_received, (owns[1],))
            shared_received = exchange(shared_pre, "head", axes[n])
    hidden = shared_hidden(features, shared_pre, shared_received, squares[0])
    base = shared_out(me, hidden, exchange(hidden, "head", 1), resid, w_shared_out)
    slabs = []
    for side in range(2):
        slabs += last_sum(owns[side], received[side])
    result = base + slabs[0].astype(F32)
    for z in range(1, seq_count):
        result = result + exchange(slabs[z], "seq", z).astype(F32)
    layer_out = jnp.transpose(result.astype(BF16).reshape(steps, seqs, width), (1, 0, 2))
    return (layer_out, states_out)


def solution(mesh):
    in_specs = (
        P("seq", None, "head"),
        P("seq", "head", None, None),
        P("seq", None, None),
        P("seq", None, None),
        P(),
        P(None, "head"),
        P(None, "head"),
        P(None, "head"),
        P(None, "head"),
        P(None, "head"),
        P(None, "head"),
        P("head"),
        P("head"),
        P(),
        P("head", None),
        P(),
        P("head", None),
        P(None, "head"),
        P(("seq", "head"), None, None),
        P(("seq", "head"), None, None),
    )
    out_specs = (P("seq", None, "head"), P("seq", "head", None, None))
    return jax.shard_map(
        on_device, mesh=mesh, in_specs=in_specs, out_specs=out_specs, check_vma=False
    )
```

```python
import functools

import jax
import jax.numpy as jnp
from jax import lax
from jax.experimental import pallas as pl
from jax.experimental.pallas import tpu as pltpu
from jax.sharding import PartitionSpec as P

DK = 128
DV = 128
EPS = 1e-06
SLOTS = 16
F32 = jnp.float32
BF16 = jnp.bfloat16
VMEM_LIMIT = 24 * 1024 * 1024


def dot(a, b):
    return jnp.dot(a, b, preferred_element_type=F32)


def silu(v):
    return v / (1.0 + jnp.exp(-v))


def split(v):
    high = v.astype(BF16)
    low = (v - high.astype(F32)).astype(BF16)
    return high, low


def pin(x):
    return pltpu.with_memory_space_constraint(x, pltpu.VMEM)


VMEM_SPEC = pl.BlockSpec(memory_space=pltpu.VMEM)
SMEM_SPEC = pl.BlockSpec(memory_space=pltpu.SMEM)
ANY_SPEC = pl.BlockSpec(memory_space=pl.ANY)


def call(body, name, out_shapes, smem, pinned, loose=(), scratch=(), aliases=None, outs=None):
    return pl.pallas_call(
        body,
        out_shape=tuple(out_shapes),
        in_specs=[SMEM_SPEC] * len(smem) + [VMEM_SPEC] * len(pinned) + [ANY_SPEC] * len(loose),
        out_specs=tuple(outs or [VMEM_SPEC] * len(out_shapes)),
        scratch_shapes=list(scratch),
        input_output_aliases=aliases or {},
        compiler_params=pltpu.CompilerParams(vmem_limit_bytes=VMEM_LIMIT),
        name=name,
    )(*smem, *(pin(x) for x in pinned), *loose)


def exchange(x, axis, bit):
    size = lax.axis_size(axis)
    return lax.ppermute(x, axis, [(i, i ^ bit) for i in range(size)])


def stack_kernel(count, *refs):
    for n, ref in enumerate(refs[:count]):
        refs[-1][n] = ref[...]


def stack(arrays, after=()):
    shape = (len(arrays), *arrays[0].shape)
    body = functools.partial(stack_kernel, len(arrays))
    [out] = call(body, "stack", [pltpu.VMEM(shape, arrays[0].dtype)], (), arrays, after)
    return out


def load_kernel(count, *refs):
    sources, targets, sems = refs[:count], refs[-1 - count : -1], refs[-1]
    copies = [pltpu.make_async_copy(a, b, sems.at[n]) for n, (a, b) in enumerate(zip(sources, targets))]
    for copy in copies:
        copy.start()
    for copy in copies:
        copy.wait()


def load(arrays, after=()):
    return call(
        functools.partial(load_kernel, len(arrays)),
        "load",
        [pltpu.VMEM(x.shape, x.dtype) for x in arrays],
        (),
        (),
        (*(pltpu.with_memory_space_constraint(x, pltpu.HBM) for x in arrays), *after),
        [pltpu.SemaphoreType.DMA((len(arrays),))],
    )


def bring_kernel(count, vectors, seq_count, head_count, me_ref, seq_ref, *refs):
    small = 3 + vectors
    sources, refs = refs[: small + count], refs[small + count :]
    targets, (pack_ref, extra_ref, gain_mine_ref, gain_inv_ref) = refs[:count], refs[count : count + 4]
    scratch, sems = refs[count + 4 : -1], refs[-1]
    ids, chosen, gain_after = scratch[:3]
    targets = (*scratch, *targets)
    copies = [pltpu.make_async_copy(a, b, sems.at[n]) for n, (a, b) in enumerate(zip(sources, targets))]
    for copy in copies:
        copy.start()
    for copy in copies[:small]:
        copy.wait()
    for n, ref in enumerate(scratch[3:]):
        pack_ref[n : n + 1, : ref.shape[1]] = ref[...]
    me, seq = me_ref[0], seq_ref[0]
    gain_mine_ref[...] = gain_after[me]
    gain_inv_ref[...] = 1.0 / gain_after[...]
    top, steps, seqs = ids.shape
    for z in range(seq_count):
        target = (seq ^ z) * head_count + me
        weight = jnp.zeros((steps, seqs), F32)
        for n in range(top):
            weight = weight + jnp.where(ids[n] == target, chosen[n], 0.0)
        high = weight.astype(BF16).astype(F32)
        both = jnp.concatenate([high, weight - high], axis=0)
        rows, width = extra_ref.shape[1:]
        both = jnp.concatenate([both, jnp.zeros((rows - 2 * steps, seqs), F32)], axis=0)
        both = jnp.concatenate([both, jnp.zeros((rows, width - seqs), F32)], axis=1)
        extra_ref[z] = both.astype(BF16)
    for copy in copies[small:]:
        copy.wait()


def bring(me, seq, arrays, vectors, ids, chosen, gain_after, seq_count):
    head_count, _, width = gain_after.shape
    small = (ids, chosen, gain_after, *vectors)
    return call(
        functools.partial(bring_kernel, len(arrays), len(vectors), seq_count, head_count),
        "bring",
        [pltpu.VMEM(x.shape, x.dtype) for x in arrays]
        + [
            pltpu.VMEM((8, 128), F32),
            pltpu.VMEM((seq_count, 16, width), BF16),
            pltpu.VMEM((1, width), F32),
            pltpu.VMEM(gain_after.shape, F32),
        ],
        (me, seq),
        (),
        [pltpu.with_memory_space_constraint(x, pltpu.HBM) for x in (*small, *arrays)],
        [pltpu.VMEM(x.shape, x.dtype) for x in small]
        + [pltpu.SemaphoreType.DMA((len(small) + len(arrays),))],
    )


def front_kernel(
    steps,
    head_count,
    me_ref,
    *refs,
):
    x_refs = refs[:2]
    (
        gain_ref,
        small_ref,
        pack_ref,
        wq,
        wk,
        wv,
        wz,
        wo_hbm,
        states_hbm,
        own_ref,
        sib_ref,
        keys_ref,
        delta_ref,
        total_ref,
        wo,
        states,
        left,
        recalls,
        sems,
    ) = refs[2:]
    me = me_ref[0]
    _, rows, width = x_refs[0].shape
    seqs = rows // steps
    key_heads = wq.shape[1] // DK
    value_heads = wv.shape[1] // DV
    group = value_heads // key_heads
    pair = group * DV

    parts = sems.shape[0] - 1
    part = seqs // parts
    copies = []
    for n in range(parts):
        span = pl.ds(n * part, part)
        copies.append(pltpu.make_async_copy(states_hbm.at[span], states.at[span], sems.at[n]))
    copies.append(pltpu.make_async_copy(wo_hbm, wo, sems.at[parts]))
    for copy in copies:
        copy.start()

    squares = jnp.zeros((rows, 1), F32)
    for j in range(head_count):
        xj = x_refs[j % 2][j // 2].astype(F32)
        squares = squares + jnp.sum(xj * xj, axis=1, keepdims=True)
    inverse = lax.rsqrt(squares / (head_count * width) + EPS)
    normed = []
    spans = []
    for j in range(head_count):
        block = me ^ j
        normed.append((x_refs[j % 2][j // 2].astype(F32) * inverse * gain_ref[block]).astype(BF16))
        spans.append(pl.ds(pl.multiple_of(block * width, width), width))

    def project(w_ref):
        total = None
        for j in range(head_count):
            term = dot(normed[j], w_ref[spans[j], :])
            total = term if total is None else total + term
        return total

    small = None
    for j in range(head_count):
        term = lax.dot_general(
            normed[j],
            small_ref[me ^ j],
            (((1,), (1,)), ((), ())),
            preferred_element_type=F32,
        )
        small = term if small is None else small + term
    betas = 1.0 / (1.0 + jnp.exp(-small[:, :value_heads]))
    alphas = small[:, value_heads : 2 * value_heads] + pack_ref[1:2, :value_heads]
    softplus = jnp.maximum(alphas, 0.0) + jnp.log1p(jnp.exp(-jnp.abs(alphas)))
    decays = jnp.exp(-pack_ref[0:1, :value_heads] * softplus)

    def units(v):
        return v * lax.rsqrt(jnp.sum(v * v, axis=1, keepdims=True) + EPS)

    queries_all = silu(project(wq))
    keys_all = silu(project(wk))
    keys, queries = [], []
    for i in range(key_heads):
        k = units(keys_all[:, i * DK : (i + 1) * DK])
        q = units(queries_all[:, i * DK : (i + 1) * DK]) * DK ** (-0.5)
        keys_ref[i] = k
        keys.append([k[t * seqs : (t + 1) * seqs] for t in range(steps)])
        queries.append([q[t * seqs : (t + 1) * seqs] for t in range(steps)])
        for t in range(steps):
            for at, v in ((t, keys[i][t]), (steps + t, queries[i][t])):
                high = v.astype(BF16).astype(F32)
                left[i, pl.ds(at, seqs, stride=SLOTS), :] = high
                left[i, pl.ds(2 * steps + at, seqs, stride=SLOTS), :] = v - high
        for at in range(4 * steps, SLOTS):
            left[i, pl.ds(at, seqs, stride=SLOTS), :] = jnp.zeros((seqs, DK), F32)
    values_all = silu(project(wv))
    gates = silu(project(wz))

    def one(s, carry):
        base = pl.multiple_of(s * SLOTS, SLOTS)
        for i in range(key_heads):
            lhs = left[i, pl.ds(base, SLOTS), :].astype(BF16)
            rhs = jnp.concatenate([states[s, i * group + u] for u in range(group)], axis=1)
            high, low = split(rhs)
            answer = dot(jnp.concatenate([lhs, lhs], axis=1), jnp.concatenate([high, low], axis=0))
            for u in range(group):
                recalls[i * group + u, pl.ds(base, SLOTS), :] = answer[:, u * DV : (u + 1) * DV]
        return carry

    for n in range(parts):
        copies[n].wait()
        lax.fori_loop(n * part, (n + 1) * part, one, 0, unroll=4)

    def wide(columns, t, i):
        return jnp.concatenate(
            [
                jnp.broadcast_to(
                    columns[t * seqs : (t + 1) * seqs, i * group + u : i * group + u + 1],
                    (seqs, DV),
                )
                for u in range(group)
            ],
            axis=1,
        )

    mixed_rows = [[] for _ in range(steps)]
    for i in range(key_heads):
        decay = [wide(decays, t, i) for t in range(steps)]
        beta = [wide(betas, t, i) for t in range(steps)]

        def read(at):
            return jnp.concatenate(
                [
                    recalls[i * group + u, pl.ds(at, seqs, stride=SLOTS), :]
                    + recalls[i * group + u, pl.ds(2 * steps + at, seqs, stride=SLOTS), :]
                    for u in range(group)
                ],
                axis=1,
            )

        deltas = []
        running = None
        for t in range(steps):
            running = decay[t] if running is None else running * decay[t]
            recall = running * read(t)
            answer = running * read(steps + t)
            deltas = [d * decay[t] for d in deltas]
            for u, d in enumerate(deltas):
                recall = recall + d * jnp.sum(keys[i][t] * keys[i][u], axis=1, keepdims=True)
                answer = answer + d * jnp.sum(queries[i][t] * keys[i][u], axis=1, keepdims=True)
            value = values_all[t * seqs : (t + 1) * seqs, i * pair : (i + 1) * pair]
            delta = beta[t] * (value - recall)
            answer = answer + delta * jnp.sum(queries[i][t] * keys[i][t], axis=1, keepdims=True)
            deltas.append(delta)
            mixed_rows[t].append(answer)
        for t in range(steps):
            delta_ref[i, t] = deltas[t]
        total_ref[i] = running
    mixed = jnp.concatenate([jnp.concatenate(m, axis=1) for m in mixed_rows], axis=0)
    gated = []
    for h in range(value_heads):
        m = mixed[:, h * DV : (h + 1) * DV]
        m = m * lax.rsqrt(jnp.mean(m * m, axis=1, keepdims=True) + EPS)
        gated.append((m * pack_ref[2:3, :DV] * gates[:, h * DV : (h + 1) * DV]).astype(BF16))
    gated = jnp.concatenate(gated, axis=1)
    copies[parts].wait()
    for c in range(head_count):
        piece = dot(gated, wo[:, c * width : (c + 1) * width]).astype(BF16)
        away = me ^ c

        @pl.when(away % 2 == 0)
        def _():
            own_ref[away // 2] = piece

        @pl.when(away % 2 == 1)
        def _():
            sib_ref[away // 2] = piece


def front(me, xs, gain, small, pack, wq, wk, wv, wz, wo, states, steps):
    pairs, rows, width = xs[0].shape
    head_count = 2 * pairs
    seqs = rows // steps
    key_heads = wq.shape[1] // DK
    value_heads = wv.shape[1] // DV
    pair = value_heads // key_heads * DV
    return call(
        functools.partial(front_kernel, steps, head_count),
        "front",
        [
            pltpu.VMEM((head_count // 2, rows, width), BF16),
            pltpu.VMEM((head_count // 2, rows, width), BF16),
            pltpu.VMEM((key_heads, rows, DK), F32),
            pltpu.VMEM((key_heads, steps, seqs, pair), F32),
            pltpu.VMEM((key_heads, seqs, pair), F32),
        ],
        (me,),
        (*xs, gain, small, pack, wq, wk, wv, wz),
        [pltpu.with_memory_space_constraint(x, pltpu.HBM) for x in (wo, states)],
        [
            pltpu.VMEM(wo.shape, BF16),
            pltpu.VMEM(states.shape, F32),
            pltpu.VMEM((key_heads, seqs * SLOTS, DK), F32),
            pltpu.VMEM((value_heads, seqs * SLOTS, DV), F32),
            pltpu.SemaphoreType.DMA((5,)),
        ],
    )


def rows_kernel(pairs, *refs):
    merged_ref, received = refs[0], refs[1:pairs]
    mine_ref, gain_ref, extra_ref, _ = refs[pairs : pairs + 4]
    resid_ref, x_ref = refs[pairs + 4 : pairs + 6]
    messages = refs[pairs + 6 :]
    rows = mine_ref.shape[0]
    resid = mine_ref[...].astype(F32) + merged_ref[0].astype(F32)
    for ref in received:
        resid = resid + ref[...].astype(F32)
    resid_ref[...] = resid
    x = (resid * gain_ref[...]).astype(BF16)
    x_ref[...] = x
    for z, ref in enumerate(messages):
        ref[:rows, :] = x
        ref[rows:, :] = extra_ref[z + 1]


def make_rows(merged, received, mine, gain, extra, after):
    rows, width = mine.shape
    message = pltpu.VMEM((rows + extra.shape[1], width), BF16)
    return call(
        functools.partial(rows_kernel, merged.shape[0]),
        "rows",
        [
            pltpu.VMEM((rows, width), F32),
            pltpu.VMEM((rows, width), BF16),
            *([message] * (extra.shape[0] - 1)),
        ],
        (),
        (merged, *received, mine, gain, extra),
        after,
    )


def slab_kernel(a_ref, b_ref, *refs):
    out_ref = refs[-1]
    rows = out_ref.shape[1]
    out_ref[0] = a_ref[:rows, :]
    out_ref[1] = b_ref[:rows, :]


def slab_pair(a, b, rows, after):
    [out] = call(slab_kernel, "slab", [pltpu.VMEM((2, rows, a.shape[1]), BF16)], (), (a, b), after)
    return out


PER_BLOCK = DK // SLOTS


def update_kernel(steps, blocks, keys_ref, delta_ref, total_ref, states_ref, *refs):
    out_ref, done_ref, left, right, olds, news, old_sems, sems = refs[-8:]
    half = PER_BLOCK // 2
    loads, stores = [], []
    for n, block in enumerate(blocks):
        for part in range(2):
            whole = pl.ds(block * PER_BLOCK + part * half, half)
            here = pl.ds(part * half, half)
            at = 2 * n + part
            loads.append(
                pltpu.make_async_copy(states_ref.at[whole], olds.at[n, here], old_sems.at[at])
            )
            stores.append(pltpu.make_async_copy(news.at[n, here], out_ref.at[whole], sems.at[at]))
            loads[-1].start()
    key_heads, rows, _ = keys_ref.shape
    seqs = rows // steps
    group = olds.shape[2] // key_heads
    first, count = blocks[0] * PER_BLOCK, len(blocks) * PER_BLOCK
    for i in range(key_heads):
        for at in range(SLOTS):
            rows_at = pl.ds(at, count, stride=SLOTS)
            t = at % steps
            k = keys_ref[i, t * seqs + first : t * seqs + first + count, :]
            k_high = k.astype(BF16).astype(F32)
            k = k - k_high if at >= 2 * steps else k_high
            left[i, rows_at, :] = k if at < 3 * steps else jnp.zeros_like(k)
            for u in range(group):
                d = delta_ref[i, t, first : first + count, u * DV : (u + 1) * DV]
                d_high = d.astype(BF16).astype(F32)
                d = d - d_high if steps <= at < 2 * steps else d_high
                right[i * group + u, rows_at, :] = d if at < 3 * steps else jnp.zeros_like(d)
    slot_of = lax.broadcasted_iota(jnp.int32, (DK, DK), 1) // SLOTS
    for n, block in enumerate(blocks):
        span = slice(n * DK, (n + 1) * DK)
        lhs = [jnp.transpose(left[i, span, :]) for i in range(key_heads)]
        rhs = [
            jnp.concatenate(
                [right[i * group + u, span, :] for u in range(group)], axis=1
            ).astype(BF16)
            for i in range(key_heads)
        ]
        for m in range(PER_BLOCK):
            if m % half == 0:
                loads[2 * n + m // half].wait()
            s = block * PER_BLOCK + m
            for i in range(key_heads):
                masked = jnp.where(slot_of == m, lhs[i], 0.0).astype(BF16)
                change = dot(masked, rhs[i])
                for u in range(group):
                    columns = slice(u * DV, (u + 1) * DV)
                    h = i * group + u
                    total = total_ref[i, s : s + 1, columns]
                    news[n, m, h] = olds[n, m, h] * total + change[:, columns]
            if m % half == half - 1:
                stores[2 * n + m // half].start()
    for copy in stores:
        copy.wait()
    done_ref[...] = jnp.zeros_like(done_ref)


def update(keys, deltas, totals, states, blocks, after, before=None):
    key_heads, steps, seqs, pair = deltas.shape
    rows = len(blocks) * DK
    value_heads = states.shape[1]
    loose = after if before is None else (before, *after)
    buffers = pltpu.VMEM((len(blocks), PER_BLOCK, *states.shape[1:]), F32)
    return call(
        functools.partial(update_kernel, steps, blocks),
        "update",
        [jax.ShapeDtypeStruct(states.shape, F32), jax.ShapeDtypeStruct((8, 128), F32)],
        (),
        (keys, deltas, totals),
        (pltpu.with_memory_space_constraint(states, pltpu.HBM), *loose),
        [
            pltpu.VMEM((key_heads, rows, DK), F32),
            pltpu.VMEM((value_heads, rows, DV), F32),
            buffers,
            buffers,
            pltpu.SemaphoreType.DMA((2 * len(blocks),)),
            pltpu.SemaphoreType.DMA((2 * len(blocks),)),
        ],
        None if before is None else {4: 0},
        [ANY_SPEC, VMEM_SPEC],
    )


def blocks_of(pieces, order, odd, me):
    xs, places = [], []
    for ref, part in zip(pieces, order):
        _, zs, rows, width = ref.shape
        for n, place in enumerate(part):
            xs.append(ref[n].reshape(zs * rows, width))
            places.append(me ^ (2 * place + odd))
    return xs, places


def rows_squares(xs, places, gain_inv_ref):
    squares = None
    for x, place in zip(xs, places):
        plain = x.astype(F32) * gain_inv_ref[place]
        plain = plain * plain
        for c in range(0, x.shape[1], 128):
            part = plain[:, c : c + 128]
            squares = part if squares is None else squares + part
    return jnp.sum(squares, axis=1, keepdims=True)


def columns_sum(total, xs, places, w_ref, columns):
    for x, place in zip(xs, places):
        width = x.shape[1]
        term = dot(x, w_ref[0, pl.ds(pl.multiple_of(place * width, width), width), columns])
        total = term if total is None else total + term
    return total


def expert_first_kernel(order, me_ref, *refs):
    pieces, (gain_inv_ref, w_ref) = refs[: len(order)], refs[len(order) : len(order) + 2]
    pre_ref, sq_ref = refs[-2:]
    xs, places = blocks_of(pieces, order, 0, me_ref[0])
    for c in range(0, w_ref.shape[2], 256):
        columns = slice(c, c + 256)
        pre_ref[:, columns] = columns_sum(None, xs, places, w_ref, columns)
    sq_ref[...] = rows_squares(xs, places, gain_inv_ref)


def expert_first(me, pieces, gain_inv, w, order, after=()):
    total = pieces[0].shape[1] * pieces[0].shape[2]
    return call(
        functools.partial(expert_first_kernel, order),
        "expert_first",
        [pltpu.VMEM((total, w.shape[2]), F32), pltpu.VMEM((total, 1), F32)],
        (me,),
        (*pieces, gain_inv, w),
        after,
    )


def expert_rest_kernel(order, order_out, steps, whole, me_ref, *refs):
    pieces, refs = refs[: len(order)], refs[len(order) :]
    gain_inv_ref, w_ref, pre_ref, sq_ref, down_ref = refs[:5]
    own, sib, sq_out = refs[-3:]
    me = me_ref[0]
    features = down_ref.shape[2]
    hidden_width = down_ref.shape[1]
    count, zs, rows, width = own.shape
    xs, places = blocks_of(pieces, order, 1, me)
    squares = sq_ref[...] + rows_squares(xs, places, gain_inv_ref)
    sq_out[...] = squares
    inverse = lax.rsqrt(squares / features + EPS)
    hidden = []
    for c in range(0, hidden_width, 256):
        parts = []
        for at in (c, hidden_width + c):
            columns = slice(at, at + 256)
            parts.append(columns_sum(pre_ref[:, columns], xs, places, w_ref, columns) * inverse)
        hidden.append((silu(parts[0]) * parts[1]).astype(BF16))
    hidden = jnp.concatenate(hidden, axis=1)
    weight = []
    for z in range(zs):
        ref = refs[5 + z]
        extra = ref[0] if z == 0 and whole else ref[rows:, :]
        columns = jnp.transpose(extra.astype(F32))
        for t in range(steps):
            both = columns[:, t : t + 1] + columns[:, steps + t : steps + t + 1]
            weight.append(both[: rows // steps])
    weight = jnp.concatenate(weight, axis=0)
    for odd, ref in ((1, sib), (0, own)):
        for n in range(count):
            block = me ^ (2 * order_out[n] + odd)
            columns = pl.ds(pl.multiple_of(block * width, width), width)
            result = dot(hidden, down_ref[0, :, columns]) * weight
            ref[n] = result.astype(BF16).reshape(zs, rows, width)


def expert_rest(me, pieces, gain_inv, w, pre, sq, down, weights, order, order_out, steps, whole, after):
    count = 2 * pieces[0].shape[0]
    shape = (count, *pieces[0].shape[1:])
    return call(
        functools.partial(expert_rest_kernel, order, order_out, steps, whole),
        "expert_rest",
        [pltpu.VMEM(shape, BF16), pltpu.VMEM(shape, BF16), pltpu.VMEM(sq.shape, F32)],
        (me,),
        (*pieces, gain_inv, w, pre, sq, down, *weights),
        after,
    )


def bit_reversed(count):
    bits = count.bit_length() - 1
    return [int(format(n, "b").zfill(bits)[::-1], 2) if bits else 0 for n in range(count)]


def add(a, b):
    return (a.astype(F32) + b.astype(F32)).astype(BF16)


def half_sum_kernel(a_ref, b_ref, *refs):
    keep_ref, send_ref = refs[-2:]
    half = a_ref.shape[0] // 2
    keep_ref[...] = add(a_ref[:half], b_ref[:half])
    send_ref[...] = add(a_ref[half:], b_ref[half:])


def half_sum(a, b, after=()):
    shape = (a.shape[0] // 2, *a.shape[1:])
    return call(
        half_sum_kernel,
        "half_sum",
        [pltpu.VMEM(shape, BF16), pltpu.VMEM(shape, BF16)],
        (),
        (a, b),
        after,
    )


def last_sum_kernel(a_ref, b_ref, *outs):
    for z, ref in enumerate(outs):
        ref[...] = add(a_ref[0, z], b_ref[0, z])


def last_sum(a, b):
    _, zs, rows, width = a.shape
    return call(last_sum_kernel, "last_sum", [pltpu.VMEM((rows, width), BF16)] * zs, (), (a, b))


def one_sum_kernel(a_ref, b_ref, *refs):
    refs[-1][...] = add(a_ref[...], b_ref[...])


def one_sum(a, b, after=()):
    [out] = call(one_sum_kernel, "one_sum", [pltpu.VMEM(a.shape, BF16)], (), (a, b), after)
    return out


def finish_kernel(count, *refs):
    total = refs[0][...]
    for ref in refs[1:count]:
        total = total + ref[...].astype(F32)
    refs[-1][...] = total.astype(BF16)


def finish(base, slab, received, after):
    arrays = (base, slab, *received)
    [out] = call(
        functools.partial(finish_kernel, len(arrays)),
        "finish",
        [jax.ShapeDtypeStruct(base.shape, BF16)],
        (),
        arrays,
        after,
    )
    return out


def shared_in_kernel(me_ref, x_ref, w_ref, *refs):
    refs = refs[-2:]
    half = w_ref.shape[1] // 2
    part = half // 2
    pre = dot(x_ref[...], w_ref[...]).astype(BF16)
    odd = me_ref[0] % 2
    for core in range(2):
        for up in range(2):
            piece = pre[:, up * half + core * part : up * half + (core + 1) * part]

            @pl.when(odd == core)
            def _():
                refs[0][:, up * part : (up + 1) * part] = piece

            @pl.when(odd != core)
            def _():
                refs[1][:, up * part : (up + 1) * part] = piece


def shared_in(me, x, w, after):
    shape = (x.shape[0], w.shape[1] // 2)
    return call(
        shared_in_kernel, "shared_in", [pltpu.VMEM(shape, BF16)] * 2, (me,), (x, w), after
    )


def shared_hidden_kernel(features, a_ref, b_ref, sq_ref, *refs):
    out_ref = refs[-1]
    rows = a_ref.shape[0]
    half = a_ref.shape[1] // 2
    inverse = lax.rsqrt(sq_ref[:rows, :] / features + EPS)
    pre = (a_ref[...].astype(F32) + b_ref[...].astype(F32)) * inverse
    out_ref[...] = (silu(pre[:, :half]) * pre[:, half:]).astype(BF16)


def shared_hidden(features, a, b, sq, after):
    [out] = call(
        functools.partial(shared_hidden_kernel, features),
        "shared_hidden",
        [pltpu.VMEM((a.shape[0], a.shape[1] // 2), BF16)],
        (),
        (a, b, sq),
        after,
    )
    return out


def shared_out_kernel(me_ref, a_ref, b_ref, resid_ref, w_ref, out_ref):
    part = a_ref.shape[1]
    odd = me_ref[0] % 2
    total = resid_ref[...]
    for core, ref in ((odd, a_ref), (1 - odd, b_ref)):
        total = total + dot(ref[...], w_ref[pl.ds(pl.multiple_of(core * part, part), part), :])
    out_ref[...] = total


def shared_out(me, a, b, resid, w):
    [out] = call(
        shared_out_kernel, "shared_out", [pltpu.VMEM(resid.shape, F32)], (me,), (a, b, resid, w)
    )
    return out


def on_device(
    tokens,
    states,
    router_ids,
    router_weights,
    input_gain,
    w_query,
    w_key,
    w_value,
    w_zgate,
    w_beta,
    w_alpha,
    decay_scale,
    dt_bias,
    gated_gain,
    w_out,
    post_gain,
    w_shared_in,
    w_shared_out,
    w_expert_in,
    w_expert_out,
):
    seq_count = lax.axis_size("seq")
    head_count = lax.axis_size("head")
    head_index = lax.axis_index("head")
    seq_index = lax.axis_index("seq")
    me = head_index.astype(jnp.int32).reshape(1)
    seqs, steps, width = tokens.shape
    rows = seqs * steps
    features = head_count * width
    pairs = head_count // 2
    axes = [1 << n for n in range(1, head_count.bit_length() - 1)]

    mine = jnp.transpose(tokens, (1, 0, 2)).reshape(rows, width)
    value_heads = w_beta.shape[1]
    small = jnp.concatenate([w_beta, w_alpha], axis=1)
    small = jnp.transpose(small.reshape(head_count, width, 2 * value_heads), (0, 2, 1))
    small = jnp.pad(small, ((0, 0), (0, -2 * value_heads % 16), (0, 0)))

    others = [exchange(mine, "head", 2 * p) for p in range(1, pairs)]
    mine, w_query, w_key, w_value, w_shared_in, w_shared_out, gain, pack, extra, gain_mine, gain_inv = bring(
        me,
        seq_index.astype(jnp.int32).reshape(1),
        (
            mine,
            w_query,
            w_key,
            w_value,
            w_shared_in,
            w_shared_out,
            input_gain.reshape(head_count, 1, width),
        ),
        [v.reshape(1, -1) for v in (decay_scale, dt_bias, gated_gain)],
        jnp.transpose(router_ids, (2, 1, 0)),
        jnp.transpose(router_weights, (2, 1, 0)),
        post_gain.reshape(head_count, 1, width),
        seq_count,
    )
    own_tokens = stack((mine, *others))
    sib_tokens = exchange(own_tokens, "head", 1)
    [w_zgate] = load((w_zgate,), (own_tokens,))
    gathered = (own_tokens, sib_tokens)
    own, sib, keys, deltas, totals = front(
        me, gathered, gain, small, pack, w_query, w_key, w_value, w_zgate, w_out, states, steps
    )

    merged = one_sum(own, exchange(sib, "head", 1))
    received = [exchange(merged[p], "head", 2 * p) for p in range(1, pairs)]
    w_in, w_down = load((w_expert_in, w_expert_out), (merged,))
    resid, x, *messages = make_rows(merged, received, mine, gain_mine, extra, (w_in,))

    half = seq_count // 2
    messages = [exchange(m, "seq", z + 1) for z, m in enumerate(messages)]
    slabs = [x] + messages
    natural, reverse = list(range(pairs)), bit_reversed(pairs)
    blocks = tuple(range(seqs // PER_BLOCK))
    quarters = [blocks[len(blocks) * n // 4 : len(blocks) * (n + 1) // 4] for n in range(4)]
    shared_pre, sent = shared_in(me, x, w_shared_in, ())
    shared_pre = one_sum(shared_pre, exchange(sent, "head", 1))
    shared_received = exchange(shared_pre, "head", axes[0])
    sides, tie = [], ()
    for slab, bits in ((slabs[:half], axes), (slabs[half:], axes[::-1])):
        if half == 2:
            side = slab_pair(*slab, rows, tie[:2])[None]
        else:
            side = jnp.stack([m[:rows] for m in slab])[None]
        if not sides:
            states_out, done = update(keys, deltas, totals, states, quarters[0], (side,))
            tie = (done, shared_pre)
        for bit in bits[:-1]:
            received = exchange(side, "head", bit)
            if side.shape[0] == 1:
                side = stack((side[0], received[0]), tie if sides else ())
            else:
                side = jnp.concatenate([side, received])
        if not sides:
            states_out, done = update(keys, deltas, totals, states, quarters[1], (side,), states_out)
            tie = (*tie, done, shared_received)
        sides.append([side, exchange(side, "head", bits[-1])])
    siblings = [[exchange(piece, "head", 1) for piece in side] for side in sides]
    middle = pairs // 2
    orders = tuple((tuple(o[:middle]), tuple(o[middle:])) for o in (natural, reverse))

    shared_pre = one_sum(shared_pre, shared_received, (sides[0][1], sides[1][1]))
    for bit in axes[1:-1]:
        shared_pre = one_sum(shared_pre, exchange(shared_pre, "head", bit))
    shared_received = exchange(shared_pre, "head", axes[-1])
    firsts = [
        expert_first(me, side, gain_inv, w_in, order, (done,)) for side, order in zip(sides, orders)
    ]
    owns, sibs, squares = [], [], []
    weights = (extra, *messages)
    ties = ((), (shared_received,))
    for n, order_out in enumerate((reverse, natural)):
        own, sib, square = expert_rest(
            me,
            siblings[n],
            gain_inv,
            w_in,
            *firsts[n],
            w_down,
            weights[n * half : (n + 1) * half],
            orders[n],
            order_out,
            steps,
            n == 0,
            ties[n],
        )
        owns.append(own)
        sibs.append(sib)
        squares.append(square)
    received = [exchange(sib, "head", 1) for sib in sibs]
    tie = ()
    for n, bits in enumerate(zip(axes, axes[::-1])):
        for side, bit in enumerate(bits):
            owns[side], sent = half_sum(owns[side], received[side], tie)
            received[side] = exchange(sent, "head", bit)
        if n == 0:
            states_out, done = update(
                keys, deltas, totals, states, quarters[2], tuple(owns), states_out
            )
            hidden = shared_hidden(features, shared_pre, shared_received, squares[0], tuple(owns))
            hidden_received = exchange(hidden, "head", 1)
            tie = (done, hidden_received)
    base = shared_out(me, hidden, hidden_received, resid, w_shared_out)
    slabs = []
    for side in range(2):
        slabs += last_sum(owns[side], received[side])
    states_out, done = update(keys, deltas, totals, states, quarters[3], (slabs[-1],), states_out)
    received = [exchange(slabs[z], "seq", z) for z in range(1, seq_count)]
    result = finish(base, slabs[0], received, (done,))
    layer_out = jnp.transpose(result.reshape(steps, seqs, width), (1, 0, 2))
    return (layer_out, states_out)


def solution(mesh):
    in_specs = (
        P("seq", None, "head"),
        P("seq", "head", None, None),
        P("seq", None, None),
        P("seq", None, None),
        P(),
        P(None, "head"),
        P(None, "head"),
        P(None, "head"),
        P(None, "head"),
        P(None, "head"),
        P(None, "head"),
        P("head"),
        P("head"),
        P(),
        P("head", None),
        P(),
        P("head", None),
        P(None, "head"),
        P(("seq", "head"), None, None),
        P(("seq", "head"), None, None),
    )
    out_specs = (P("seq", None, "head"), P("seq", "head", None, None))
    return jax.shard_map(
        on_device, mesh=mesh, in_specs=in_specs, out_specs=out_specs, check_vma=False
    )
```

```python
import functools

import jax
import jax.numpy as jnp
from jax import lax
from jax.experimental import pallas as pl
from jax.experimental.pallas import tpu as pltpu
from jax.sharding import PartitionSpec as P

DK = 128
DV = 128
EPS = 1e-06
SLOTS = 16
F32 = jnp.float32
BF16 = jnp.bfloat16
VMEM_LIMIT = 24 * 1024 * 1024


def dot(a, b):
    return jnp.dot(a, b, preferred_element_type=F32)


def silu(v):
    return v / (1.0 + jnp.exp(-v))


def split(v):
    high = v.astype(BF16)
    low = (v - high.astype(F32)).astype(BF16)
    return high, low


def pin(x):
    return pltpu.with_memory_space_constraint(x, pltpu.VMEM)


VMEM_SPEC = pl.BlockSpec(memory_space=pltpu.VMEM)
SMEM_SPEC = pl.BlockSpec(memory_space=pltpu.SMEM)
ANY_SPEC = pl.BlockSpec(memory_space=pl.ANY)


def call(body, name, out_shapes, smem, pinned, loose=(), scratch=(), aliases=None, outs=None):
    return pl.pallas_call(
        body,
        out_shape=tuple(out_shapes),
        in_specs=[SMEM_SPEC] * len(smem) + [VMEM_SPEC] * len(pinned) + [ANY_SPEC] * len(loose),
        out_specs=tuple(outs or [VMEM_SPEC] * len(out_shapes)),
        scratch_shapes=list(scratch),
        input_output_aliases=aliases or {},
        compiler_params=pltpu.CompilerParams(vmem_limit_bytes=VMEM_LIMIT),
        name=name,
    )(*smem, *(pin(x) for x in pinned), *loose)


def exchange(x, axis, bit):
    size = lax.axis_size(axis)
    return lax.ppermute(x, axis, [(i, i ^ bit) for i in range(size)])


def stack_kernel(count, *refs):
    for n, ref in enumerate(refs[:count]):
        refs[-1][n] = ref[...]


def stack(arrays, after=()):
    shape = (len(arrays), *arrays[0].shape)
    body = functools.partial(stack_kernel, len(arrays))
    [out] = call(body, "stack", [pltpu.VMEM(shape, arrays[0].dtype)], (), arrays, after)
    return out


def load_kernel(count, *refs):
    sources, targets, sems = refs[:count], refs[-1 - count : -1], refs[-1]
    copies = [pltpu.make_async_copy(a, b, sems.at[n]) for n, (a, b) in enumerate(zip(sources, targets))]
    for copy in copies:
        copy.start()
    for copy in copies:
        copy.wait()


def load(arrays, after=()):
    return call(
        functools.partial(load_kernel, len(arrays)),
        "load",
        [pltpu.VMEM(x.shape, x.dtype) for x in arrays],
        (),
        (),
        (*(pltpu.with_memory_space_constraint(x, pltpu.HBM) for x in arrays), *after),
        [pltpu.SemaphoreType.DMA((len(arrays),))],
    )


def bring_kernel(count, vectors, seq_count, head_count, me_ref, seq_ref, *refs):
    small = 3 + vectors
    sources, refs = refs[: small + count], refs[small + count :]
    targets, (pack_ref, extra_ref, gain_mine_ref, gain_inv_ref) = refs[:count], refs[count : count + 4]
    scratch, sems = refs[count + 4 : -1], refs[-1]
    ids, chosen, gain_after = scratch[:3]
    targets = (*scratch, *targets)
    copies = [pltpu.make_async_copy(a, b, sems.at[n]) for n, (a, b) in enumerate(zip(sources, targets))]
    for copy in copies:
        copy.start()
    for copy in copies[:small]:
        copy.wait()
    for n, ref in enumerate(scratch[3:]):
        pack_ref[n : n + 1, : ref.shape[1]] = ref[...]
    me, seq = me_ref[0], seq_ref[0]
    gain_mine_ref[...] = gain_after[me]
    gain_inv_ref[...] = 1.0 / gain_after[...]
    top, steps, seqs = ids.shape
    for z in range(seq_count):
        target = (seq ^ z) * head_count + me
        weight = jnp.zeros((steps, seqs), F32)
        for n in range(top):
            weight = weight + jnp.where(ids[n] == target, chosen[n], 0.0)
        high = weight.astype(BF16).astype(F32)
        both = jnp.concatenate([high, weight - high], axis=0)
        rows, width = extra_ref.shape[1:]
        both = jnp.concatenate([both, jnp.zeros((rows - 2 * steps, seqs), F32)], axis=0)
        both = jnp.concatenate([both, jnp.zeros((rows, width - seqs), F32)], axis=1)
        extra_ref[z] = both.astype(BF16)
    for copy in copies[small:]:
        copy.wait()


def bring(me, seq, arrays, vectors, ids, chosen, gain_after, seq_count):
    head_count, _, width = gain_after.shape
    small = (ids, chosen, gain_after, *vectors)
    return call(
        functools.partial(bring_kernel, len(arrays), len(vectors), seq_count, head_count),
        "bring",
        [pltpu.VMEM(x.shape, x.dtype) for x in arrays]
        + [
            pltpu.VMEM((8, 128), F32),
            pltpu.VMEM((seq_count, 16, width), BF16),
            pltpu.VMEM((1, width), F32),
            pltpu.VMEM(gain_after.shape, F32),
        ],
        (me, seq),
        (),
        [pltpu.with_memory_space_constraint(x, pltpu.HBM) for x in (*small, *arrays)],
        [pltpu.VMEM(x.shape, x.dtype) for x in small]
        + [pltpu.SemaphoreType.DMA((len(small) + len(arrays),))],
    )


def front_kernel(
    steps,
    head_count,
    me_ref,
    *refs,
):
    x_refs = refs[:2]
    (
        gain_ref,
        small_ref,
        pack_ref,
        wq,
        wk,
        wv,
        wz,
        wo_hbm,
        states_hbm,
        own_ref,
        sib_ref,
        keys_ref,
        delta_ref,
        total_ref,
        wo,
        states,
        left,
        recalls,
        sems,
    ) = refs[2:]
    me = me_ref[0]
    _, rows, width = x_refs[0].shape
    seqs = rows // steps
    key_heads = wq.shape[1] // DK
    value_heads = wv.shape[1] // DV
    group = value_heads // key_heads
    pair = group * DV

    parts = sems.shape[0] - 1
    part = seqs // parts
    copies = []
    for n in range(parts):
        span = pl.ds(n * part, part)
        copies.append(pltpu.make_async_copy(states_hbm.at[span], states.at[span], sems.at[n]))
    copies.append(pltpu.make_async_copy(wo_hbm, wo, sems.at[parts]))
    for copy in copies:
        copy.start()

    squares = jnp.zeros((rows, 1), F32)
    for j in range(head_count):
        xj = x_refs[j % 2][j // 2].astype(F32)
        squares = squares + jnp.sum(xj * xj, axis=1, keepdims=True)
    inverse = lax.rsqrt(squares / (head_count * width) + EPS)
    normed = []
    spans = []
    for j in range(head_count):
        block = me ^ j
        normed.append((x_refs[j % 2][j // 2].astype(F32) * inverse * gain_ref[block]).astype(BF16))
        spans.append(pl.ds(pl.multiple_of(block * width, width), width))

    def project(w_ref):
        total = None
        for j in range(head_count):
            term = dot(normed[j], w_ref[spans[j], :])
            total = term if total is None else total + term
        return total

    small = None
    for j in range(head_count):
        term = lax.dot_general(
            normed[j],
            small_ref[me ^ j],
            (((1,), (1,)), ((), ())),
            preferred_element_type=F32,
        )
        small = term if small is None else small + term
    betas = 1.0 / (1.0 + jnp.exp(-small[:, :value_heads]))
    alphas = small[:, value_heads : 2 * value_heads] + pack_ref[1:2, :value_heads]
    softplus = jnp.maximum(alphas, 0.0) + jnp.log1p(jnp.exp(-jnp.abs(alphas)))
    decays = jnp.exp(-pack_ref[0:1, :value_heads] * softplus)

    def units(v):
        return v * lax.rsqrt(jnp.sum(v * v, axis=1, keepdims=True) + EPS)

    queries_all = silu(project(wq))
    keys_all = silu(project(wk))
    keys, queries = [], []
    for i in range(key_heads):
        k = units(keys_all[:, i * DK : (i + 1) * DK])
        q = units(queries_all[:, i * DK : (i + 1) * DK]) * DK ** (-0.5)
        keys_ref[i] = k
        keys.append([k[t * seqs : (t + 1) * seqs] for t in range(steps)])
        queries.append([q[t * seqs : (t + 1) * seqs] for t in range(steps)])
        for t in range(steps):
            for at, v in ((t, keys[i][t]), (steps + t, queries[i][t])):
                high = v.astype(BF16).astype(F32)
                left[i, pl.ds(at, seqs, stride=SLOTS), :] = high
                left[i, pl.ds(2 * steps + at, seqs, stride=SLOTS), :] = v - high
        for at in range(4 * steps, SLOTS):
            left[i, pl.ds(at, seqs, stride=SLOTS), :] = jnp.zeros((seqs, DK), F32)
    values_all = silu(project(wv))
    gates = silu(project(wz))

    def one(s, carry):
        base = pl.multiple_of(s * SLOTS, SLOTS)
        for i in range(key_heads):
            lhs = left[i, pl.ds(base, SLOTS), :].astype(BF16)
            rhs = jnp.concatenate([states[s, i * group + u] for u in range(group)], axis=1)
            high, low = split(rhs)
            answer = dot(jnp.concatenate([lhs, lhs], axis=1), jnp.concatenate([high, low], axis=0))
            for u in range(group):
                recalls[i * group + u, pl.ds(base, SLOTS), :] = answer[:, u * DV : (u + 1) * DV]
        return carry

    for n in range(parts):
        copies[n].wait()
        lax.fori_loop(n * part, (n + 1) * part, one, 0, unroll=4)

    def wide(columns, t, i):
        return jnp.concatenate(
            [
                jnp.broadcast_to(
                    columns[t * seqs : (t + 1) * seqs, i * group + u : i * group + u + 1],
                    (seqs, DV),
                )
                for u in range(group)
            ],
            axis=1,
        )

    mixed_rows = [[] for _ in range(steps)]
    for i in range(key_heads):
        decay = [wide(decays, t, i) for t in range(steps)]
        beta = [wide(betas, t, i) for t in range(steps)]

        def read(at):
            return jnp.concatenate(
                [
                    recalls[i * group + u, pl.ds(at, seqs, stride=SLOTS), :]
                    + recalls[i * group + u, pl.ds(2 * steps + at, seqs, stride=SLOTS), :]
                    for u in range(group)
                ],
                axis=1,
            )

        deltas = []
        running = None
        for t in range(steps):
            running = decay[t] if running is None else running * decay[t]
            recall = running * read(t)
            answer = running * read(steps + t)
            deltas = [d * decay[t] for d in deltas]
            for u, d in enumerate(deltas):
                recall = recall + d * jnp.sum(keys[i][t] * keys[i][u], axis=1, keepdims=True)
                answer = answer + d * jnp.sum(queries[i][t] * keys[i][u], axis=1, keepdims=True)
            value = values_all[t * seqs : (t + 1) * seqs, i * pair : (i + 1) * pair]
            delta = beta[t] * (value - recall)
            answer = answer + delta * jnp.sum(queries[i][t] * keys[i][t], axis=1, keepdims=True)
            deltas.append(delta)
            mixed_rows[t].append(answer)
        for t in range(steps):
            delta_ref[i, t] = deltas[t]
        total_ref[i] = running
    mixed = jnp.concatenate([jnp.concatenate(m, axis=1) for m in mixed_rows], axis=0)
    gated = []
    for h in range(value_heads):
        m = mixed[:, h * DV : (h + 1) * DV]
        m = m * lax.rsqrt(jnp.mean(m * m, axis=1, keepdims=True) + EPS)
        gated.append((m * pack_ref[2:3, :DV] * gates[:, h * DV : (h + 1) * DV]).astype(BF16))
    gated = jnp.concatenate(gated, axis=1)
    copies[parts].wait()
    for c in range(head_count):
        piece = dot(gated, wo[:, c * width : (c + 1) * width]).astype(BF16)
        away = me ^ c

        @pl.when(away % 2 == 0)
        def _():
            own_ref[away // 2] = piece

        @pl.when(away % 2 == 1)
        def _():
            sib_ref[away // 2] = piece


def front(me, xs, gain, small, pack, wq, wk, wv, wz, wo, states, steps):
    pairs, rows, width = xs[0].shape
    head_count = 2 * pairs
    seqs = rows // steps
    key_heads = wq.shape[1] // DK
    value_heads = wv.shape[1] // DV
    pair = value_heads // key_heads * DV
    return call(
        functools.partial(front_kernel, steps, head_count),
        "front",
        [
            pltpu.VMEM((head_count // 2, rows, width), BF16),
            pltpu.VMEM((head_count // 2, rows, width), BF16),
            pltpu.VMEM((key_heads, rows, DK), F32),
            pltpu.VMEM((key_heads, steps, seqs, pair), F32),
            pltpu.VMEM((key_heads, seqs, pair), F32),
        ],
        (me,),
        (*xs, gain, small, pack, wq, wk, wv, wz),
        [pltpu.with_memory_space_constraint(x, pltpu.HBM) for x in (wo, states)],
        [
            pltpu.VMEM(wo.shape, BF16),
            pltpu.VMEM(states.shape, F32),
            pltpu.VMEM((key_heads, seqs * SLOTS, DK), F32),
            pltpu.VMEM((value_heads, seqs * SLOTS, DV), F32),
            pltpu.SemaphoreType.DMA((9,)),
        ],
    )


def rows_kernel(pairs, *refs):
    merged_ref, received = refs[0], refs[1:pairs]
    mine_ref, gain_ref, extra_ref, _ = refs[pairs : pairs + 4]
    resid_ref, x_ref = refs[pairs + 4 : pairs + 6]
    messages = refs[pairs + 6 :]
    rows = mine_ref.shape[0]
    resid = mine_ref[...].astype(F32) + merged_ref[0].astype(F32)
    for ref in received:
        resid = resid + ref[...].astype(F32)
    resid_ref[...] = resid
    x = (resid * gain_ref[...]).astype(BF16)
    x_ref[...] = x
    for z, ref in enumerate(messages):
        ref[:rows, :] = x
        ref[rows:, :] = extra_ref[z + 1]


def make_rows(merged, received, mine, gain, extra, after):
    rows, width = mine.shape
    message = pltpu.VMEM((rows + extra.shape[1], width), BF16)
    return call(
        functools.partial(rows_kernel, merged.shape[0]),
        "rows",
        [
            pltpu.VMEM((rows, width), F32),
            pltpu.VMEM((rows, width), BF16),
            *([message] * (extra.shape[0] - 1)),
        ],
        (),
        (merged, *received, mine, gain, extra),
        after,
    )


def keep_kernel(x_ref, *refs):
    refs[-1][...] = x_ref[...]


def keep(x, after):
    [out] = call(keep_kernel, "keep", [pltpu.VMEM(x.shape, x.dtype)], (), (x,), after)
    return out


def slab_kernel(a_ref, b_ref, *refs):
    out_ref = refs[-1]
    rows = out_ref.shape[1]
    out_ref[0] = a_ref[:rows, :]
    out_ref[1] = b_ref[:rows, :]


def slab_pair(a, b, rows, after):
    [out] = call(slab_kernel, "slab", [pltpu.VMEM((2, rows, a.shape[1]), BF16)], (), (a, b), after)
    return out


PER_BLOCK = DK // SLOTS


def update_kernel(steps, blocks, keys_ref, delta_ref, total_ref, states_ref, *refs):
    out_ref, done_ref, left, right, olds, news, old_sems, sems = refs[-8:]
    half = PER_BLOCK // 2
    loads, stores = [], []
    for n, block in enumerate(blocks):
        for part in range(2):
            whole = pl.ds(block * PER_BLOCK + part * half, half)
            here = pl.ds(part * half, half)
            at = 2 * n + part
            loads.append(
                pltpu.make_async_copy(states_ref.at[whole], olds.at[n, here], old_sems.at[at])
            )
            stores.append(pltpu.make_async_copy(news.at[n, here], out_ref.at[whole], sems.at[at]))
            loads[-1].start()
    key_heads, rows, _ = keys_ref.shape
    seqs = rows // steps
    group = olds.shape[2] // key_heads
    first, count = blocks[0] * PER_BLOCK, len(blocks) * PER_BLOCK
    for i in range(key_heads):
        for at in range(SLOTS):
            rows_at = pl.ds(at, count, stride=SLOTS)
            t = at % steps
            k = keys_ref[i, t * seqs + first : t * seqs + first + count, :]
            k_high = k.astype(BF16).astype(F32)
            k = k - k_high if at >= 2 * steps else k_high
            left[i, rows_at, :] = k if at < 3 * steps else jnp.zeros_like(k)
            for u in range(group):
                d = delta_ref[i, t, first : first + count, u * DV : (u + 1) * DV]
                d_high = d.astype(BF16).astype(F32)
                d = d - d_high if steps <= at < 2 * steps else d_high
                right[i * group + u, rows_at, :] = d if at < 3 * steps else jnp.zeros_like(d)
    slot_of = lax.broadcasted_iota(jnp.int32, (DK, DK), 1) // SLOTS
    for n, block in enumerate(blocks):
        span = slice(n * DK, (n + 1) * DK)
        lhs = [jnp.transpose(left[i, span, :]) for i in range(key_heads)]
        rhs = [
            jnp.concatenate(
                [right[i * group + u, span, :] for u in range(group)], axis=1
            ).astype(BF16)
            for i in range(key_heads)
        ]
        for m in range(PER_BLOCK):
            if m % half == 0:
                loads[2 * n + m // half].wait()
            s = block * PER_BLOCK + m
            for i in range(key_heads):
                masked = jnp.where(slot_of == m, lhs[i], 0.0).astype(BF16)
                change = dot(masked, rhs[i])
                for u in range(group):
                    columns = slice(u * DV, (u + 1) * DV)
                    h = i * group + u
                    total = total_ref[i, s : s + 1, columns]
                    news[n, m, h] = olds[n, m, h] * total + change[:, columns]
            if m % half == half - 1:
                stores[2 * n + m // half].start()
    for copy in stores:
        copy.wait()
    done_ref[...] = jnp.zeros_like(done_ref)


def update(keys, deltas, totals, states, blocks, after, before=None):
    key_heads, steps, seqs, pair = deltas.shape
    rows = len(blocks) * DK
    value_heads = states.shape[1]
    loose = after if before is None else (before, *after)
    buffers = pltpu.VMEM((len(blocks), PER_BLOCK, *states.shape[1:]), F32)
    return call(
        functools.partial(update_kernel, steps, blocks),
        "update",
        [jax.ShapeDtypeStruct(states.shape, F32), jax.ShapeDtypeStruct((8, 128), F32)],
        (),
        (keys, deltas, totals),
        (pltpu.with_memory_space_constraint(states, pltpu.HBM), *loose),
        [
            pltpu.VMEM((key_heads, rows, DK), F32),
            pltpu.VMEM((value_heads, rows, DV), F32),
            buffers,
            buffers,
            pltpu.SemaphoreType.DMA((2 * len(blocks),)),
            pltpu.SemaphoreType.DMA((2 * len(blocks),)),
        ],
        None if before is None else {4: 0},
        [ANY_SPEC, VMEM_SPEC],
    )


def blocks_of(pieces, order, odd, me):
    xs, places = [], []
    for ref, part in zip(pieces, order):
        _, zs, rows, width = ref.shape
        for n, place in enumerate(part):
            xs.append(ref[n].reshape(zs * rows, width))
            places.append(me ^ (2 * place + odd))
    return xs, places


def rows_squares(xs, places, gain_inv_ref):
    squares = None
    for x, place in zip(xs, places):
        plain = x.astype(F32) * gain_inv_ref[place]
        plain = plain * plain
        for c in range(0, x.shape[1], 128):
            part = plain[:, c : c + 128]
            squares = part if squares is None else squares + part
    return jnp.sum(squares, axis=1, keepdims=True)


def columns_sum(total, xs, places, w_ref, columns):
    for x, place in zip(xs, places):
        width = x.shape[1]
        term = dot(x, w_ref[0, pl.ds(pl.multiple_of(place * width, width), width), columns])
        total = term if total is None else total + term
    return total


def expert_first_kernel(order, me_ref, *refs):
    pieces, (gain_inv_ref, w_ref) = refs[: len(order)], refs[len(order) : len(order) + 2]
    pre_ref, sq_ref = refs[-2:]
    xs, places = blocks_of(pieces, order, 0, me_ref[0])
    for c in range(0, w_ref.shape[2], 256):
        columns = slice(c, c + 256)
        pre_ref[:, columns] = columns_sum(None, xs, places, w_ref, columns)
    sq_ref[...] = rows_squares(xs, places, gain_inv_ref)


def expert_first(me, pieces, gain_inv, w, order, after=()):
    total = pieces[0].shape[1] * pieces[0].shape[2]
    return call(
        functools.partial(expert_first_kernel, order),
        "expert_first",
        [pltpu.VMEM((total, w.shape[2]), F32), pltpu.VMEM((total, 1), F32)],
        (me,),
        (*pieces, gain_inv, w),
        after,
    )


def expert_rest_kernel(order, order_out, steps, whole, me_ref, *refs):
    pieces, refs = refs[: len(order)], refs[len(order) :]
    gain_inv_ref, w_ref, pre_ref, sq_ref, down_ref = refs[:5]
    own, sib, sq_out = refs[-3:]
    me = me_ref[0]
    features = down_ref.shape[2]
    hidden_width = down_ref.shape[1]
    count, zs, rows, width = own.shape
    xs, places = blocks_of(pieces, order, 1, me)
    squares = sq_ref[...] + rows_squares(xs, places, gain_inv_ref)
    sq_out[...] = squares
    inverse = lax.rsqrt(squares / features + EPS)
    hidden = []
    for c in range(0, hidden_width, 256):
        parts = []
        for at in (c, hidden_width + c):
            columns = slice(at, at + 256)
            parts.append(columns_sum(pre_ref[:, columns], xs, places, w_ref, columns) * inverse)
        hidden.append((silu(parts[0]) * parts[1]).astype(BF16))
    hidden = jnp.concatenate(hidden, axis=1)
    weight = []
    for z in range(zs):
        ref = refs[5 + z]
        extra = ref[0] if z == 0 and whole else ref[rows:, :]
        columns = jnp.transpose(extra.astype(F32))
        for t in range(steps):
            both = columns[:, t : t + 1] + columns[:, steps + t : steps + t + 1]
            weight.append(both[: rows // steps])
    weight = jnp.concatenate(weight, axis=0)
    for odd, ref in ((1, sib), (0, own)):
        for n in range(count):
            block = me ^ (2 * order_out[n] + odd)
            columns = pl.ds(pl.multiple_of(block * width, width), width)
            result = dot(hidden, down_ref[0, :, columns]) * weight
            ref[n] = result.astype(BF16).reshape(zs, rows, width)


def expert_rest(me, pieces, gain_inv, w, pre, sq, down, weights, order, order_out, steps, whole, after):
    count = 2 * pieces[0].shape[0]
    shape = (count, *pieces[0].shape[1:])
    return call(
        functools.partial(expert_rest_kernel, order, order_out, steps, whole),
        "expert_rest",
        [pltpu.VMEM(shape, BF16), pltpu.VMEM(shape, BF16), pltpu.VMEM(sq.shape, F32)],
        (me,),
        (*pieces, gain_inv, w, pre, sq, down, *weights),
        after,
    )


def bit_reversed(count):
    bits = count.bit_length() - 1
    return [int(format(n, "b").zfill(bits)[::-1], 2) if bits else 0 for n in range(count)]


def add(a, b):
    return (a.astype(F32) + b.astype(F32)).astype(BF16)


def half_sum_kernel(a_ref, b_ref, *refs):
    keep_ref, send_ref = refs[-2:]
    half = a_ref.shape[0] // 2
    keep_ref[...] = add(a_ref[:half], b_ref[:half])
    send_ref[...] = add(a_ref[half:], b_ref[half:])


def half_sum(a, b, after=()):
    shape = (a.shape[0] // 2, *a.shape[1:])
    return call(
        half_sum_kernel,
        "half_sum",
        [pltpu.VMEM(shape, BF16), pltpu.VMEM(shape, BF16)],
        (),
        (a, b),
        after,
    )


def last_sum_kernel(a_ref, b_ref, *outs):
    for z, ref in enumerate(outs):
        ref[...] = add(a_ref[0, z], b_ref[0, z])


def last_sum(a, b):
    _, zs, rows, width = a.shape
    return call(last_sum_kernel, "last_sum", [pltpu.VMEM((rows, width), BF16)] * zs, (), (a, b))


def one_sum_kernel(a_ref, b_ref, *refs):
    refs[-1][...] = add(a_ref[...], b_ref[...])


def one_sum(a, b, after=()):
    [out] = call(one_sum_kernel, "one_sum", [pltpu.VMEM(a.shape, BF16)], (), (a, b), after)
    return out


def finish_kernel(count, *refs):
    total = refs[0][...]
    for ref in refs[1:count]:
        total = total + ref[...].astype(F32)
    refs[-1][...] = total.astype(BF16)


def finish(base, slab, received, after):
    arrays = (base, slab, *received)
    [out] = call(
        functools.partial(finish_kernel, len(arrays)),
        "finish",
        [jax.ShapeDtypeStruct(base.shape, BF16)],
        (),
        arrays,
        after,
    )
    return out


def shared_in_kernel(me_ref, x_ref, w_ref, *refs):
    refs = refs[-2:]
    half = w_ref.shape[1] // 2
    part = half // 2
    pre = dot(x_ref[...], w_ref[...]).astype(BF16)
    odd = me_ref[0] % 2
    for core in range(2):
        for up in range(2):
            piece = pre[:, up * half + core * part : up * half + (core + 1) * part]

            @pl.when(odd == core)
            def _():
                refs[0][:, up * part : (up + 1) * part] = piece

            @pl.when(odd != core)
            def _():
                refs[1][:, up * part : (up + 1) * part] = piece


def shared_in(me, x, w, after):
    shape = (x.shape[0], w.shape[1] // 2)
    return call(
        shared_in_kernel, "shared_in", [pltpu.VMEM(shape, BF16)] * 2, (me,), (x, w), after
    )


def shared_hidden_kernel(features, a_ref, b_ref, sq_ref, *refs):
    out_ref = refs[-1]
    rows = a_ref.shape[0]
    half = a_ref.shape[1] // 2
    inverse = lax.rsqrt(sq_ref[:rows, :] / features + EPS)
    pre = (a_ref[...].astype(F32) + b_ref[...].astype(F32)) * inverse
    out_ref[...] = (silu(pre[:, :half]) * pre[:, half:]).astype(BF16)


def shared_hidden(features, a, b, sq, after):
    [out] = call(
        functools.partial(shared_hidden_kernel, features),
        "shared_hidden",
        [pltpu.VMEM((a.shape[0], a.shape[1] // 2), BF16)],
        (),
        (a, b, sq),
        after,
    )
    return out


def shared_out_kernel(me_ref, a_ref, b_ref, resid_ref, w_ref, out_ref):
    part = a_ref.shape[1]
    odd = me_ref[0] % 2
    total = resid_ref[...]
    for core, ref in ((odd, a_ref), (1 - odd, b_ref)):
        total = total + dot(ref[...], w_ref[pl.ds(pl.multiple_of(core * part, part), part), :])
    out_ref[...] = total


def shared_out(me, a, b, resid, w):
    [out] = call(
        shared_out_kernel, "shared_out", [pltpu.VMEM(resid.shape, F32)], (me,), (a, b, resid, w)
    )
    return out


def on_device(
    tokens,
    states,
    router_ids,
    router_weights,
    input_gain,
    w_query,
    w_key,
    w_value,
    w_zgate,
    w_beta,
    w_alpha,
    decay_scale,
    dt_bias,
    gated_gain,
    w_out,
    post_gain,
    w_shared_in,
    w_shared_out,
    w_expert_in,
    w_expert_out,
):
    seq_count = lax.axis_size("seq")
    head_count = lax.axis_size("head")
    head_index = lax.axis_index("head")
    seq_index = lax.axis_index("seq")
    me = head_index.astype(jnp.int32).reshape(1)
    seqs, steps, width = tokens.shape
    rows = seqs * steps
    features = head_count * width
    pairs = head_count // 2
    axes = [1 << n for n in range(1, head_count.bit_length() - 1)]

    mine = jnp.transpose(tokens, (1, 0, 2)).reshape(rows, width)
    value_heads = w_beta.shape[1]
    small = jnp.concatenate([w_beta, w_alpha], axis=1)
    small = jnp.transpose(small.reshape(head_count, width, 2 * value_heads), (0, 2, 1))
    small = jnp.pad(small, ((0, 0), (0, -2 * value_heads % 16), (0, 0)))

    others = [exchange(mine, "head", 2 * p) for p in range(1, pairs)]
    mine, w_query, w_key, w_value, w_shared_in, w_shared_out, gain, pack, extra, gain_mine, gain_inv = bring(
        me,
        seq_index.astype(jnp.int32).reshape(1),
        (
            mine,
            w_query,
            w_key,
            w_value,
            w_shared_in,
            w_shared_out,
            input_gain.reshape(head_count, 1, width),
        ),
        [v.reshape(1, -1) for v in (decay_scale, dt_bias, gated_gain)],
        jnp.transpose(router_ids, (2, 1, 0)),
        jnp.transpose(router_weights, (2, 1, 0)),
        post_gain.reshape(head_count, 1, width),
        seq_count,
    )
    own_tokens = stack((mine, *others))
    sib_tokens = exchange(own_tokens, "head", 1)
    [w_zgate] = load((w_zgate,), (own_tokens,))
    gathered = (own_tokens, sib_tokens)
    own, sib, keys, deltas, totals = front(
        me, gathered, gain, small, pack, w_query, w_key, w_value, w_zgate, w_out, states, steps
    )

    merged = one_sum(own, exchange(sib, "head", 1))
    received = [exchange(merged[p], "head", 2 * p) for p in range(1, pairs)]
    [w_in] = load((w_expert_in,), (merged,))
    resid, x, *messages = make_rows(merged, received, mine, gain_mine, extra, (w_in,))

    half = seq_count // 2
    messages = [exchange(m, "seq", z + 1) for z, m in enumerate(messages)]
    slabs = [x] + messages
    natural, reverse = list(range(pairs)), bit_reversed(pairs)
    blocks = tuple(range(seqs // PER_BLOCK))
    quarters = [blocks[len(blocks) * n // 4 : len(blocks) * (n + 1) // 4] for n in range(4)]
    shared_pre, sent = shared_in(me, x, w_shared_in, ())
    shared_pre = one_sum(shared_pre, exchange(sent, "head", 1))
    shared_received = exchange(shared_pre, "head", axes[0])
    sides, tie = [], ()
    for slab, bits in ((slabs[:half], axes), (slabs[half:], axes[::-1])):
        if half == 2:
            side = slab_pair(*slab, rows, tie[:2])[None]
        else:
            side = jnp.stack([m[:rows] for m in slab])[None]
        if not sides:
            states_out, done = update(keys, deltas, totals, states, quarters[0], (side,))
            tie = (done, shared_pre)
        for bit in bits[:-1]:
            received = exchange(side, "head", bit)
            if side.shape[0] == 1:
                side = stack((side[0], received[0]), tie if sides else ())
            else:
                side = jnp.concatenate([side, received])
        if not sides:
            [w_down] = load((w_expert_out,), (side,))
            tie = (*tie, w_down)
        sides.append([side, exchange(side, "head", bits[-1])])
    states_out, done = update(
        keys, deltas, totals, states, quarters[1] + quarters[2], (sides[0][0], sides[1][0]), states_out
    )
    siblings = [
        [exchange(side[0], "head", 1), exchange(keep(side[1], (done, shared_received)), "head", 1)] for side in sides
    ]
    middle = pairs // 2
    orders = tuple((tuple(o[:middle]), tuple(o[middle:])) for o in (natural, reverse))

    shared_pre = one_sum(shared_pre, shared_received, (sides[0][1], sides[1][1]))
    for bit in axes[1:-1]:
        shared_pre = one_sum(shared_pre, exchange(shared_pre, "head", bit))
    shared_received = exchange(shared_pre, "head", axes[-1])
    firsts = [
        expert_first(me, side, gain_inv, w_in, order, (done,)) for side, order in zip(sides, orders)
    ]
    owns, sibs, squares = [], [], []
    weights = (extra, *messages)
    ties = ((), (shared_received,))
    for n, order_out in enumerate((reverse, natural)):
        own, sib, square = expert_rest(
            me,
            siblings[n],
            gain_inv,
            w_in,
            *firsts[n],
            w_down,
            weights[n * half : (n + 1) * half],
            orders[n],
            order_out,
            steps,
            n == 0,
            ties[n],
        )
        owns.append(own)
        sibs.append(sib)
        squares.append(square)
    received = [exchange(sib, "head", 1) for sib in sibs]
    tie = ()
    for n, bits in enumerate(zip(axes, axes[::-1])):
        for side, bit in enumerate(bits):
            owns[side], sent = half_sum(owns[side], received[side], tie)
            received[side] = exchange(sent, "head", bit)
        if n == 0:
            states_out, done = update(
                keys, deltas, totals, states, quarters[3], tuple(owns), states_out
            )
            hidden = shared_hidden(features, shared_pre, shared_received, squares[0], tuple(owns))
            hidden_received = exchange(hidden, "head", 1)
            tie = (done, hidden_received)
    base = shared_out(me, hidden, hidden_received, resid, w_shared_out)
    slabs = []
    for side in range(2):
        slabs += last_sum(owns[side], received[side])
    received = [exchange(slabs[z], "seq", z) for z in range(1, seq_count)]
    result = finish(base, slabs[0], received, ())
    layer_out = jnp.transpose(result.reshape(steps, seqs, width), (1, 0, 2))
    return (layer_out, states_out)


def solution(mesh):
    in_specs = (
        P("seq", None, "head"),
        P("seq", "head", None, None),
        P("seq", None, None),
        P("seq", None, None),
        P(),
        P(None, "head"),
        P(None, "head"),
        P(None, "head"),
        P(None, "head"),
        P(None, "head"),
        P(None, "head"),
        P("head"),
        P("head"),
        P(),
        P("head", None),
        P(),
        P("head", None),
        P(None, "head"),
        P(("seq", "head"), None, None),
        P(("seq", "head"), None, None),
    )
    out_specs = (P("seq", None, "head"), P("seq", "head", None, None))
    return jax.shard_map(
        on_device, mesh=mesh, in_specs=in_specs, out_specs=out_specs, check_vma=False
    )
```

```python
import functools

import jax
import jax.numpy as jnp
from jax import lax
from jax.experimental import pallas as pl
from jax.experimental.pallas import tpu as pltpu
from jax.sharding import PartitionSpec as P

DK = 128
DV = 128
EPS = 1e-06
SLOTS = 16
F32 = jnp.float32
BF16 = jnp.bfloat16
VMEM_LIMIT = 24 * 1024 * 1024


def dot(a, b):
    return jnp.dot(a, b, preferred_element_type=F32)


def silu(v):
    return v / (1.0 + jnp.exp(-v))


def split(v):
    high = v.astype(BF16)
    low = (v - high.astype(F32)).astype(BF16)
    return high, low


def pin(x):
    return pltpu.with_memory_space_constraint(x, pltpu.VMEM)


VMEM_SPEC = pl.BlockSpec(memory_space=pltpu.VMEM)
SMEM_SPEC = pl.BlockSpec(memory_space=pltpu.SMEM)
ANY_SPEC = pl.BlockSpec(memory_space=pl.ANY)


def call(body, name, out_shapes, smem, pinned, loose=(), scratch=(), aliases=None, outs=None):
    return pl.pallas_call(
        body,
        out_shape=tuple(out_shapes),
        in_specs=[SMEM_SPEC] * len(smem) + [VMEM_SPEC] * len(pinned) + [ANY_SPEC] * len(loose),
        out_specs=tuple(outs or [VMEM_SPEC] * len(out_shapes)),
        scratch_shapes=list(scratch),
        input_output_aliases=aliases or {},
        compiler_params=pltpu.CompilerParams(vmem_limit_bytes=VMEM_LIMIT),
        name=name,
    )(*smem, *(pin(x) for x in pinned), *loose)


def exchange(x, axis, bit):
    size = lax.axis_size(axis)
    return lax.ppermute(x, axis, [(i, i ^ bit) for i in range(size)])


def stack_kernel(count, *refs):
    for n, ref in enumerate(refs[:count]):
        refs[-1][n] = ref[...]


def stack(arrays, after=()):
    shape = (len(arrays), *arrays[0].shape)
    body = functools.partial(stack_kernel, len(arrays))
    [out] = call(body, "stack", [pltpu.VMEM(shape, arrays[0].dtype)], (), arrays, after)
    return out


def load_kernel(count, *refs):
    sources, targets, sems = refs[:count], refs[-1 - count : -1], refs[-1]
    copies = [pltpu.make_async_copy(a, b, sems.at[n]) for n, (a, b) in enumerate(zip(sources, targets))]
    for copy in copies:
        copy.start()
    for copy in copies:
        copy.wait()


def load(arrays, after=()):
    return call(
        functools.partial(load_kernel, len(arrays)),
        "load",
        [pltpu.VMEM(x.shape, x.dtype) for x in arrays],
        (),
        (),
        (*(pltpu.with_memory_space_constraint(x, pltpu.HBM) for x in arrays), *after),
        [pltpu.SemaphoreType.DMA((len(arrays),))],
    )


def bring_kernel(count, vectors, seq_count, head_count, me_ref, seq_ref, *refs):
    small = 3 + vectors
    sources, refs = refs[: small + count], refs[small + count :]
    targets, (pack_ref, extra_ref, gain_mine_ref, gain_inv_ref) = refs[:count], refs[count : count + 4]
    scratch, sems = refs[count + 4 : -1], refs[-1]
    ids, chosen, gain_after = scratch[:3]
    targets = (*scratch, *targets)
    copies = [pltpu.make_async_copy(a, b, sems.at[n]) for n, (a, b) in enumerate(zip(sources, targets))]
    for copy in copies:
        copy.start()
    for copy in copies[:small]:
        copy.wait()
    for n, ref in enumerate(scratch[3:]):
        pack_ref[n : n + 1, : ref.shape[1]] = ref[...]
    me, seq = me_ref[0], seq_ref[0]
    gain_mine_ref[...] = gain_after[me]
    gain_inv_ref[...] = 1.0 / gain_after[...]
    top, steps, seqs = ids.shape
    for z in range(seq_count):
        target = (seq ^ z) * head_count + me
        weight = jnp.zeros((steps, seqs), F32)
        for n in range(top):
            weight = weight + jnp.where(ids[n] == target, chosen[n], 0.0)
        high = weight.astype(BF16).astype(F32)
        both = jnp.concatenate([high, weight - high], axis=0)
        rows, width = extra_ref.shape[1:]
        both = jnp.concatenate([both, jnp.zeros((rows - 2 * steps, seqs), F32)], axis=0)
        both = jnp.concatenate([both, jnp.zeros((rows, width - seqs), F32)], axis=1)
        extra_ref[z] = both.astype(BF16)
    for copy in copies[small:]:
        copy.wait()


def bring(me, seq, arrays, vectors, ids, chosen, gain_after, seq_count):
    head_count, _, width = gain_after.shape
    small = (ids, chosen, gain_after, *vectors)
    return call(
        functools.partial(bring_kernel, len(arrays), len(vectors), seq_count, head_count),
        "bring",
        [pltpu.VMEM(x.shape, x.dtype) for x in arrays]
        + [
            pltpu.VMEM((8, 128), F32),
            pltpu.VMEM((seq_count, 16, width), BF16),
            pltpu.VMEM((1, width), F32),
            pltpu.VMEM(gain_after.shape, F32),
        ],
        (me, seq),
        (),
        [pltpu.with_memory_space_constraint(x, pltpu.HBM) for x in (*small, *arrays)],
        [pltpu.VMEM(x.shape, x.dtype) for x in small]
        + [pltpu.SemaphoreType.DMA((len(small) + len(arrays),))],
    )


def front_kernel(
    steps,
    head_count,
    me_ref,
    *refs,
):
    x_refs = refs[:2]
    (
        gain_ref,
        small_ref,
        pack_ref,
        wq,
        wk,
        wv,
        wz,
        wo_hbm,
        states_hbm,
        own_ref,
        sib_ref,
        keys_ref,
        delta_ref,
        total_ref,
        wo,
        states,
        left,
        recalls,
        sems,
    ) = refs[2:]
    me = me_ref[0]
    _, rows, width = x_refs[0].shape
    seqs = rows // steps
    key_heads = wq.shape[1] // DK
    value_heads = wv.shape[1] // DV
    group = value_heads // key_heads
    pair = group * DV

    parts = sems.shape[0] - 1
    part = seqs // parts
    copies = []
    for n in range(parts):
        span = pl.ds(n * part, part)
        copies.append(pltpu.make_async_copy(states_hbm.at[span], states.at[span], sems.at[n]))
    copies.append(pltpu.make_async_copy(wo_hbm, wo, sems.at[parts]))
    for copy in copies:
        copy.start()

    squares = jnp.zeros((rows, 1), F32)
    for j in range(head_count):
        xj = x_refs[j % 2][j // 2].astype(F32)
        squares = squares + jnp.sum(xj * xj, axis=1, keepdims=True)
    inverse = lax.rsqrt(squares / (head_count * width) + EPS)
    normed = []
    spans = []
    for j in range(head_count):
        block = me ^ j
        normed.append((x_refs[j % 2][j // 2].astype(F32) * inverse * gain_ref[block]).astype(BF16))
        spans.append(pl.ds(pl.multiple_of(block * width, width), width))

    def project(w_ref):
        total = None
        for j in range(head_count):
            term = dot(normed[j], w_ref[spans[j], :])
            total = term if total is None else total + term
        return total

    small = None
    for j in range(head_count):
        term = lax.dot_general(
            normed[j],
            small_ref[me ^ j],
            (((1,), (1,)), ((), ())),
            preferred_element_type=F32,
        )
        small = term if small is None else small + term
    betas = 1.0 / (1.0 + jnp.exp(-small[:, :value_heads]))
    alphas = small[:, value_heads : 2 * value_heads] + pack_ref[1:2, :value_heads]
    softplus = jnp.maximum(alphas, 0.0) + jnp.log1p(jnp.exp(-jnp.abs(alphas)))
    decays = jnp.exp(-pack_ref[0:1, :value_heads] * softplus)

    def units(v):
        return v * lax.rsqrt(jnp.sum(v * v, axis=1, keepdims=True) + EPS)

    queries_all = silu(project(wq))
    keys_all = silu(project(wk))
    keys, queries = [], []
    for i in range(key_heads):
        k = units(keys_all[:, i * DK : (i + 1) * DK])
        q = units(queries_all[:, i * DK : (i + 1) * DK]) * DK ** (-0.5)
        keys_ref[i] = k
        keys.append([k[t * seqs : (t + 1) * seqs] for t in range(steps)])
        queries.append([q[t * seqs : (t + 1) * seqs] for t in range(steps)])
        for t in range(steps):
            for at, v in ((t, keys[i][t]), (steps + t, queries[i][t])):
                high = v.astype(BF16).astype(F32)
                left[i, pl.ds(at, seqs, stride=SLOTS), :] = high
                left[i, pl.ds(2 * steps + at, seqs, stride=SLOTS), :] = v - high
        for at in range(4 * steps, SLOTS):
            left[i, pl.ds(at, seqs, stride=SLOTS), :] = jnp.zeros((seqs, DK), F32)
    values_all = silu(project(wv))
    gates = silu(project(wz))

    def one(s, carry):
        base = pl.multiple_of(s * SLOTS, SLOTS)
        for i in range(key_heads):
            lhs = left[i, pl.ds(base, SLOTS), :].astype(BF16)
            rhs = jnp.concatenate([states[s, i * group + u] for u in range(group)], axis=1)
            high, low = split(rhs)
            answer = dot(jnp.concatenate([lhs, lhs], axis=1), jnp.concatenate([high, low], axis=0))
            for u in range(group):
                recalls[i * group + u, pl.ds(base, SLOTS), :] = answer[:, u * DV : (u + 1) * DV]
        return carry

    for n in range(parts):
        copies[n].wait()
        lax.fori_loop(n * part, (n + 1) * part, one, 0, unroll=4)

    def wide(columns, t, i):
        return jnp.concatenate(
            [
                jnp.broadcast_to(
                    columns[t * seqs : (t + 1) * seqs, i * group + u : i * group + u + 1],
                    (seqs, DV),
                )
                for u in range(group)
            ],
            axis=1,
        )

    mixed_rows = [[] for _ in range(steps)]
    for i in range(key_heads):
        decay = [wide(decays, t, i) for t in range(steps)]
        beta = [wide(betas, t, i) for t in range(steps)]

        def read(at):
            return jnp.concatenate(
                [
                    recalls[i * group + u, pl.ds(at, seqs, stride=SLOTS), :]
                    + recalls[i * group + u, pl.ds(2 * steps + at, seqs, stride=SLOTS), :]
                    for u in range(group)
                ],
                axis=1,
            )

        deltas = []
        running = None
        for t in range(steps):
            running = decay[t] if running is None else running * decay[t]
            recall = running * read(t)
            answer = running * read(steps + t)
            deltas = [d * decay[t] for d in deltas]
            for u, d in enumerate(deltas):
                recall = recall + d * jnp.sum(keys[i][t] * keys[i][u], axis=1, keepdims=True)
                answer = answer + d * jnp.sum(queries[i][t] * keys[i][u], axis=1, keepdims=True)
            value = values_all[t * seqs : (t + 1) * seqs, i * pair : (i + 1) * pair]
            delta = beta[t] * (value - recall)
            answer = answer + delta * jnp.sum(queries[i][t] * keys[i][t], axis=1, keepdims=True)
            deltas.append(delta)
            mixed_rows[t].append(answer)
        for t in range(steps):
            delta_ref[i, t] = deltas[t]
        total_ref[i] = running
    mixed = jnp.concatenate([jnp.concatenate(m, axis=1) for m in mixed_rows], axis=0)
    gated = []
    for h in range(value_heads):
        m = mixed[:, h * DV : (h + 1) * DV]
        m = m * lax.rsqrt(jnp.mean(m * m, axis=1, keepdims=True) + EPS)
        gated.append((m * pack_ref[2:3, :DV] * gates[:, h * DV : (h + 1) * DV]).astype(BF16))
    gated = jnp.concatenate(gated, axis=1)
    copies[parts].wait()
    for c in range(head_count):
        piece = dot(gated, wo[:, c * width : (c + 1) * width]).astype(BF16)
        away = me ^ c

        @pl.when(away % 2 == 0)
        def _():
            own_ref[away // 2] = piece

        @pl.when(away % 2 == 1)
        def _():
            sib_ref[away // 2] = piece


def front(me, xs, gain, small, pack, wq, wk, wv, wz, wo, states, steps):
    pairs, rows, width = xs[0].shape
    head_count = 2 * pairs
    seqs = rows // steps
    key_heads = wq.shape[1] // DK
    value_heads = wv.shape[1] // DV
    pair = value_heads // key_heads * DV
    return call(
        functools.partial(front_kernel, steps, head_count),
        "front",
        [
            pltpu.VMEM((head_count // 2, rows, width), BF16),
            pltpu.VMEM((head_count // 2, rows, width), BF16),
            pltpu.VMEM((key_heads, rows, DK), F32),
            pltpu.VMEM((key_heads, steps, seqs, pair), F32),
            pltpu.VMEM((key_heads, seqs, pair), F32),
        ],
        (me,),
        (*xs, gain, small, pack, wq, wk, wv, wz),
        [pltpu.with_memory_space_constraint(x, pltpu.HBM) for x in (wo, states)],
        [
            pltpu.VMEM(wo.shape, BF16),
            pltpu.VMEM(states.shape, F32),
            pltpu.VMEM((key_heads, seqs * SLOTS, DK), F32),
            pltpu.VMEM((value_heads, seqs * SLOTS, DV), F32),
            pltpu.SemaphoreType.DMA((9,)),
        ],
    )


def rows_kernel(pairs, *refs):
    merged_ref, received = refs[0], refs[1:pairs]
    mine_ref, gain_ref, extra_ref, _ = refs[pairs : pairs + 4]
    resid_ref, x_ref = refs[pairs + 4 : pairs + 6]
    messages = refs[pairs + 6 :]
    rows = mine_ref.shape[0]
    resid = mine_ref[...].astype(F32) + merged_ref[0].astype(F32)
    for ref in received:
        resid = resid + ref[...].astype(F32)
    resid_ref[...] = resid
    x = (resid * gain_ref[...]).astype(BF16)
    x_ref[...] = x
    for z, ref in enumerate(messages):
        ref[:rows, :] = x
        ref[rows:, :] = extra_ref[z + 1]


def make_rows(merged, received, mine, gain, extra, after):
    rows, width = mine.shape
    message = pltpu.VMEM((rows + extra.shape[1], width), BF16)
    return call(
        functools.partial(rows_kernel, merged.shape[0]),
        "rows",
        [
            pltpu.VMEM((rows, width), F32),
            pltpu.VMEM((rows, width), BF16),
            *([message] * (extra.shape[0] - 1)),
        ],
        (),
        (merged, *received, mine, gain, extra),
        after,
    )


def slab_kernel(a_ref, b_ref, *refs):
    out_ref = refs[-1]
    rows = out_ref.shape[1]
    out_ref[0] = a_ref[:rows, :]
    out_ref[1] = b_ref[:rows, :]


def slab_pair(a, b, rows, after):
    [out] = call(slab_kernel, "slab", [pltpu.VMEM((2, rows, a.shape[1]), BF16)], (), (a, b), after)
    return out


PER_BLOCK = DK // SLOTS


def update_kernel(steps, blocks, keys_ref, delta_ref, total_ref, states_ref, *refs):
    out_ref, done_ref, left, right, olds, news, old_sems, sems = refs[-8:]
    half = PER_BLOCK // 2
    loads, stores = [], []
    for n, block in enumerate(blocks):
        for part in range(2):
            whole = pl.ds(block * PER_BLOCK + part * half, half)
            here = pl.ds(part * half, half)
            at = 2 * n + part
            loads.append(
                pltpu.make_async_copy(states_ref.at[whole], olds.at[n, here], old_sems.at[at])
            )
            stores.append(pltpu.make_async_copy(news.at[n, here], out_ref.at[whole], sems.at[at]))
            loads[-1].start()
    key_heads, rows, _ = keys_ref.shape
    seqs = rows // steps
    group = olds.shape[2] // key_heads
    first, count = blocks[0] * PER_BLOCK, len(blocks) * PER_BLOCK
    for i in range(key_heads):
        for at in range(SLOTS):
            rows_at = pl.ds(at, count, stride=SLOTS)
            t = at % steps
            k = keys_ref[i, t * seqs + first : t * seqs + first + count, :]
            k_high = k.astype(BF16).astype(F32)
            k = k - k_high if at >= 2 * steps else k_high
            left[i, rows_at, :] = k if at < 3 * steps else jnp.zeros_like(k)
            for u in range(group):
                d = delta_ref[i, t, first : first + count, u * DV : (u + 1) * DV]
                d_high = d.astype(BF16).astype(F32)
                d = d - d_high if steps <= at < 2 * steps else d_high
                right[i * group + u, rows_at, :] = d if at < 3 * steps else jnp.zeros_like(d)
    slot_of = lax.broadcasted_iota(jnp.int32, (DK, DK), 1) // SLOTS
    for n, block in enumerate(blocks):
        span = slice(n * DK, (n + 1) * DK)
        lhs = [jnp.transpose(left[i, span, :]) for i in range(key_heads)]
        rhs = [
            jnp.concatenate(
                [right[i * group + u, span, :] for u in range(group)], axis=1
            ).astype(BF16)
            for i in range(key_heads)
        ]
        for m in range(PER_BLOCK):
            if m % half == 0:
                loads[2 * n + m // half].wait()
            s = block * PER_BLOCK + m
            for i in range(key_heads):
                masked = jnp.where(slot_of == m, lhs[i], 0.0).astype(BF16)
                change = dot(masked, rhs[i])
                for u in range(group):
                    columns = slice(u * DV, (u + 1) * DV)
                    h = i * group + u
                    total = total_ref[i, s : s + 1, columns]
                    news[n, m, h] = olds[n, m, h] * total + change[:, columns]
            if m % half == half - 1:
                stores[2 * n + m // half].start()
    for copy in stores:
        copy.wait()
    done_ref[...] = jnp.zeros_like(done_ref)


def update(keys, deltas, totals, states, blocks, after, before=None):
    key_heads, steps, seqs, pair = deltas.shape
    rows = len(blocks) * DK
    value_heads = states.shape[1]
    loose = after if before is None else (before, *after)
    buffers = pltpu.VMEM((len(blocks), PER_BLOCK, *states.shape[1:]), F32)
    return call(
        functools.partial(update_kernel, steps, blocks),
        "update",
        [jax.ShapeDtypeStruct(states.shape, F32), jax.ShapeDtypeStruct((8, 128), F32)],
        (),
        (keys, deltas, totals),
        (pltpu.with_memory_space_constraint(states, pltpu.HBM), *loose),
        [
            pltpu.VMEM((key_heads, rows, DK), F32),
            pltpu.VMEM((value_heads, rows, DV), F32),
            buffers,
            buffers,
            pltpu.SemaphoreType.DMA((2 * len(blocks),)),
            pltpu.SemaphoreType.DMA((2 * len(blocks),)),
        ],
        None if before is None else {4: 0},
        [ANY_SPEC, VMEM_SPEC],
    )


def blocks_of(pieces, order, odd, me):
    xs, places = [], []
    for ref, part in zip(pieces, order):
        _, zs, rows, width = ref.shape
        for n, place in enumerate(part):
            xs.append(ref[n].reshape(zs * rows, width))
            places.append(me ^ (2 * place + odd))
    return xs, places


def rows_squares(xs, places, gain_inv_ref):
    squares = None
    for x, place in zip(xs, places):
        plain = x.astype(F32) * gain_inv_ref[place]
        plain = plain * plain
        for c in range(0, x.shape[1], 128):
            part = plain[:, c : c + 128]
            squares = part if squares is None else squares + part
    return jnp.sum(squares, axis=1, keepdims=True)


def columns_sum(total, xs, places, w_ref, columns):
    for x, place in zip(xs, places):
        width = x.shape[1]
        term = dot(x, w_ref[0, pl.ds(pl.multiple_of(place * width, width), width), columns])
        total = term if total is None else total + term
    return total


def expert_first_kernel(order, me_ref, *refs):
    pieces, (gain_inv_ref, w_ref) = refs[: len(order)], refs[len(order) : len(order) + 2]
    pre_ref, sq_ref = refs[-2:]
    xs, places = blocks_of(pieces, order, 0, me_ref[0])
    for c in range(0, w_ref.shape[2], 256):
        columns = slice(c, c + 256)
        pre_ref[:, columns] = columns_sum(None, xs, places, w_ref, columns)
    sq_ref[...] = rows_squares(xs, places, gain_inv_ref)


def expert_first(me, pieces, gain_inv, w, order, after=()):
    total = pieces[0].shape[1] * pieces[0].shape[2]
    return call(
        functools.partial(expert_first_kernel, order),
        "expert_first",
        [pltpu.VMEM((total, w.shape[2]), F32), pltpu.VMEM((total, 1), F32)],
        (me,),
        (*pieces, gain_inv, w),
        after,
    )


def expert_rest_kernel(order, order_out, steps, whole, me_ref, *refs):
    pieces, refs = refs[: len(order)], refs[len(order) :]
    gain_inv_ref, w_ref, pre_ref, sq_ref, down_ref = refs[:5]
    own, sib, sq_out = refs[-3:]
    me = me_ref[0]
    features = down_ref.shape[2]
    hidden_width = down_ref.shape[1]
    count, zs, rows, width = own.shape
    xs, places = blocks_of(pieces, order, 1, me)
    squares = sq_ref[...] + rows_squares(xs, places, gain_inv_ref)
    sq_out[...] = squares
    inverse = lax.rsqrt(squares / features + EPS)
    hidden = []
    for c in range(0, hidden_width, 256):
        parts = []
        for at in (c, hidden_width + c):
            columns = slice(at, at + 256)
            parts.append(columns_sum(pre_ref[:, columns], xs, places, w_ref, columns) * inverse)
        hidden.append((silu(parts[0]) * parts[1]).astype(BF16))
    hidden = jnp.concatenate(hidden, axis=1)
    weight = []
    for z in range(zs):
        ref = refs[5 + z]
        extra = ref[0] if z == 0 and whole else ref[rows:, :]
        columns = jnp.transpose(extra.astype(F32))
        for t in range(steps):
            both = columns[:, t : t + 1] + columns[:, steps + t : steps + t + 1]
            weight.append(both[: rows // steps])
    weight = jnp.concatenate(weight, axis=0)
    for odd, ref in ((1, sib), (0, own)):
        for n in range(count):
            block = me ^ (2 * order_out[n] + odd)
            columns = pl.ds(pl.multiple_of(block * width, width), width)
            result = dot(hidden, down_ref[0, :, columns]) * weight
            ref[n] = result.astype(BF16).reshape(zs, rows, width)


def expert_rest(me, pieces, gain_inv, w, pre, sq, down, weights, order, order_out, steps, whole, after):
    count = len(order_out)
    shape = (count, *pieces[0].shape[1:])
    return call(
        functools.partial(expert_rest_kernel, order, order_out, steps, whole),
        "expert_rest",
        [pltpu.VMEM(shape, BF16), pltpu.VMEM(shape, BF16), pltpu.VMEM(sq.shape, F32)],
        (me,),
        (*pieces, gain_inv, w, pre, sq, down, *weights),
        after,
    )


def bit_reversed(count):
    bits = count.bit_length() - 1
    return [int(format(n, "b").zfill(bits)[::-1], 2) if bits else 0 for n in range(count)]


def add(a, b):
    return (a.astype(F32) + b.astype(F32)).astype(BF16)


def half_sum_kernel(a_ref, b_ref, *refs):
    keep_ref, send_ref = refs[-2:]
    half = a_ref.shape[0] // 2
    keep_ref[...] = add(a_ref[:half], b_ref[:half])
    send_ref[...] = add(a_ref[half:], b_ref[half:])


def half_sum(a, b, after=()):
    shape = (a.shape[0] // 2, *a.shape[1:])
    return call(
        half_sum_kernel,
        "half_sum",
        [pltpu.VMEM(shape, BF16), pltpu.VMEM(shape, BF16)],
        (),
        (a, b),
        after,
    )


def last_sum_kernel(a_ref, b_ref, *outs):
    for z, ref in enumerate(outs):
        ref[...] = add(a_ref[0, z], b_ref[0, z])


def last_sum(a, b):
    _, zs, rows, width = a.shape
    return call(last_sum_kernel, "last_sum", [pltpu.VMEM((rows, width), BF16)] * zs, (), (a, b))


def one_sum_kernel(a_ref, b_ref, *refs):
    refs[-1][...] = add(a_ref[...], b_ref[...])


def one_sum(a, b, after=()):
    [out] = call(one_sum_kernel, "one_sum", [pltpu.VMEM(a.shape, BF16)], (), (a, b), after)
    return out


def finish_kernel(count, *refs):
    total = refs[0][...]
    for ref in refs[1:count]:
        total = total + ref[...].astype(F32)
    refs[-1][...] = total.astype(BF16)


def finish(base, slab, received, after):
    arrays = (base, slab, *received)
    [out] = call(
        functools.partial(finish_kernel, len(arrays)),
        "finish",
        [jax.ShapeDtypeStruct(base.shape, BF16)],
        (),
        arrays,
        after,
    )
    return out


def shared_in_kernel(me_ref, x_ref, w_ref, *refs):
    refs = refs[-2:]
    chunks, _, width = refs[0].shape
    half = w_ref.shape[1] // 2
    part = half // 2
    pre = dot(x_ref[...], w_ref[...]).astype(BF16)
    odd = me_ref[0] % 2
    for core in range(2):
        for n in range(chunks):
            up, at = divmod(n * width, part)
            start = up * half + core * part + at
            piece = pre[:, start : start + width]

            @pl.when(odd == core)
            def _():
                refs[0][n] = piece

            @pl.when(odd != core)
            def _():
                refs[1][n] = piece


def shared_in(me, x, w, after):
    rows, width = x.shape
    shape = (w.shape[1] // 2 // width, rows, width)
    return call(
        shared_in_kernel, "shared_in", [pltpu.VMEM(shape, BF16)] * 2, (me,), (x, w), after
    )


def open_kernel(a_ref, b_ref, keep_ref, received_ref, *refs):
    out_ref = refs[-1]
    rows = out_ref.shape[2]
    out_ref[0, 0] = a_ref[:rows, :]
    out_ref[0, 1] = b_ref[:rows, :]
    out_ref[1] = add(keep_ref[...], received_ref[...])


def open_side(a, b, keep, received, after):
    shape = (2, *keep.shape)
    [out] = call(open_kernel, "open", [pltpu.VMEM(shape, BF16)], (), (a, b, keep, received), after)
    return out


def grow_kernel(mine_ref, received_ref, *refs):
    out_ref = refs[-1]
    count = mine_ref.shape[0] - 1
    out_ref[:count] = mine_ref[:count]
    out_ref[count : 2 * count] = received_ref[:count]
    out_ref[2 * count] = add(mine_ref[count], received_ref[count])


def grow(mine, received, after):
    shape = (2 * mine.shape[0] - 1, *mine.shape[1:])
    [out] = call(grow_kernel, "grow", [pltpu.VMEM(shape, BF16)], (), (mine, received), after)
    return out


def shared_hidden_kernel(features, a_ref, b_ref, sq_ref, *refs):
    out_ref = refs[-1]
    last, chunks, rows, width = a_ref.shape
    inverse = lax.rsqrt(sq_ref[:rows, :] / features + EPS)
    pre = [
        (a_ref[last - 1, n].astype(F32) + b_ref[last - 1, n].astype(F32)) * inverse
        for n in range(chunks)
    ]
    for n in range(chunks // 2):
        columns = slice(n * width, (n + 1) * width)
        out_ref[:, columns] = (silu(pre[n]) * pre[chunks // 2 + n]).astype(BF16)


def shared_hidden(features, a, b, sq, after):
    _, chunks, rows, width = a.shape
    [out] = call(
        functools.partial(shared_hidden_kernel, features),
        "shared_hidden",
        [pltpu.VMEM((rows, chunks // 2 * width), BF16)],
        (),
        (a, b, sq),
        after,
    )
    return out


def shared_out_kernel(me_ref, a_ref, b_ref, resid_ref, w_ref, out_ref):
    part = a_ref.shape[1]
    odd = me_ref[0] % 2
    total = resid_ref[...]
    for core, ref in ((odd, a_ref), (1 - odd, b_ref)):
        total = total + dot(ref[...], w_ref[pl.ds(pl.multiple_of(core * part, part), part), :])
    out_ref[...] = total


def shared_out(me, a, b, resid, w):
    [out] = call(
        shared_out_kernel, "shared_out", [pltpu.VMEM(resid.shape, F32)], (me,), (a, b, resid, w)
    )
    return out


def on_device(
    tokens,
    states,
    router_ids,
    router_weights,
    input_gain,
    w_query,
    w_key,
    w_value,
    w_zgate,
    w_beta,
    w_alpha,
    decay_scale,
    dt_bias,
    gated_gain,
    w_out,
    post_gain,
    w_shared_in,
    w_shared_out,
    w_expert_in,
    w_expert_out,
):
    seq_count = lax.axis_size("seq")
    head_count = lax.axis_size("head")
    head_index = lax.axis_index("head")
    seq_index = lax.axis_index("seq")
    me = head_index.astype(jnp.int32).reshape(1)
    seqs, steps, width = tokens.shape
    rows = seqs * steps
    features = head_count * width
    pairs = head_count // 2
    axes = [1 << n for n in range(1, head_count.bit_length() - 1)]

    mine = jnp.transpose(tokens, (1, 0, 2)).reshape(rows, width)
    value_heads = w_beta.shape[1]
    small = jnp.concatenate([w_beta, w_alpha], axis=1)
    small = jnp.transpose(small.reshape(head_count, width, 2 * value_heads), (0, 2, 1))
    small = jnp.pad(small, ((0, 0), (0, -2 * value_heads % 16), (0, 0)))

    others = [exchange(mine, "head", 2 * p) for p in range(1, pairs)]
    mine, w_query, w_key, w_value, w_shared_in, w_shared_out, gain, pack, extra, gain_mine, gain_inv = bring(
        me,
        seq_index.astype(jnp.int32).reshape(1),
        (
            mine,
            w_query,
            w_key,
            w_value,
            w_shared_in,
            w_shared_out,
            input_gain.reshape(head_count, 1, width),
        ),
        [v.reshape(1, -1) for v in (decay_scale, dt_bias, gated_gain)],
        jnp.transpose(router_ids, (2, 1, 0)),
        jnp.transpose(router_weights, (2, 1, 0)),
        post_gain.reshape(head_count, 1, width),
        seq_count,
    )
    own_tokens = stack((mine, *others))
    sib_tokens = exchange(own_tokens, "head", 1)
    [w_zgate] = load((w_zgate,), (own_tokens,))
    gathered = (own_tokens, sib_tokens)
    own, sib, keys, deltas, totals = front(
        me, gathered, gain, small, pack, w_query, w_key, w_value, w_zgate, w_out, states, steps
    )

    merged = one_sum(own, exchange(sib, "head", 1))
    received = [exchange(merged[p], "head", 2 * p) for p in range(1, pairs)]
    [w_in] = load((w_expert_in,), (merged,))
    resid, x, *messages = make_rows(merged, received, mine, gain_mine, extra, (w_in,))

    half = seq_count // 2
    messages = [exchange(m, "seq", z + 1) for z, m in enumerate(messages)]
    slabs = [x] + messages
    natural, reverse = list(range(pairs)), bit_reversed(pairs)
    blocks = tuple(range(seqs // PER_BLOCK))
    quarters = [blocks[len(blocks) * n // 4 : len(blocks) * (n + 1) // 4] for n in range(4)]
    shared_keep, sent = shared_in(me, x, w_shared_in, ())
    shared_received = exchange(sent, "head", 1)
    [w_down] = load((w_expert_out,), (shared_keep,))
    if half == 2:
        side = open_side(*slabs[:2], shared_keep, shared_received, (*slabs[2:], w_down))
    else:
        rows_only = jnp.stack([m[:rows] for m in slabs[:half]])
        side = jnp.stack([rows_only, add(shared_keep, shared_received)])
    if half == 2:
        other = slab_pair(*slabs[2:], rows, ())[None]
    else:
        other = jnp.stack([m[:rows] for m in slabs[half:]])[None]
    states_out, done = update(
        keys, deltas, totals, states, quarters[0] + quarters[1], (side, other)
    )
    for bit in axes[:0:-1]:
        received = exchange(other, "head", bit)
        if other.shape[0] == 1:
            other = stack((other[0], received[0]), (done,))
        else:
            other = jnp.concatenate([other, received])
    for bit in axes[:-1]:
        side = grow(side, exchange(side, "head", bit), (done, other))
    sides = [[side, exchange(side, "head", axes[-1])]]
    sides.append([other, exchange(other, "head", axes[0])])
    siblings = [[exchange(piece, "head", 1) for piece in side] for side in sides]
    middle = pairs // 2
    orders = tuple((tuple(o[:middle]), tuple(o[middle:])) for o in (natural, reverse))

    firsts = []
    for side, order in zip(sides, orders):
        firsts.append(expert_first(me, side, gain_inv, w_in, order, (done,)))
        done = firsts[-1][1]
    owns, sibs, squares = [], [], []
    weights = (extra, *messages)
    for n, order_out in enumerate((reverse, natural)):
        own, sib, square = expert_rest(
            me,
            siblings[n],
            gain_inv,
            w_in,
            *firsts[n],
            w_down,
            weights[n * half : (n + 1) * half],
            orders[n],
            order_out,
            steps,
            n == 0,
            tuple(owns),
        )
        owns.append(own)
        sibs.append(sib)
        squares.append(square)
    received = [exchange(sib, "head", 1) for sib in sibs]
    tie = ()
    for n, bits in enumerate(zip(axes, axes[::-1])):
        for side, bit in enumerate(bits):
            owns[side], sent = half_sum(owns[side], received[side], tie)
            received[side] = exchange(sent, "head", bit)
        if n == 0:
            states_out, done = update(
                keys, deltas, totals, states, quarters[2], tuple(owns), states_out
            )
            hidden = shared_hidden(features, *sides[0], squares[0], tuple(owns))
            hidden_received = exchange(hidden, "head", 1)
            tie = (done, hidden_received)
    base = shared_out(me, hidden, hidden_received, resid, w_shared_out)
    slabs = []
    for side in range(2):
        slabs += last_sum(owns[side], received[side])
    states_out, done = update(keys, deltas, totals, states, quarters[3], (slabs[-1],), states_out)
    received = [exchange(slabs[z], "seq", z) for z in range(1, seq_count)]
    result = finish(base, slabs[0], received, (done,))
    layer_out = jnp.transpose(result.reshape(steps, seqs, width), (1, 0, 2))
    return (layer_out, states_out)


def solution(mesh):
    in_specs = (
        P("seq", None, "head"),
        P("seq", "head", None, None),
        P("seq", None, None),
        P("seq", None, None),
        P(),
        P(None, "head"),
        P(None, "head"),
        P(None, "head"),
        P(None, "head"),
        P(None, "head"),
        P(None, "head"),
        P("head"),
        P("head"),
        P(),
        P("head", None),
        P(),
        P("head", None),
        P(None, "head"),
        P(("seq", "head"), None, None),
        P(("seq", "head"), None, None),
    )
    out_specs = (P("seq", None, "head"), P("seq", "head", None, None))
    return jax.shard_map(
        on_device, mesh=mesh, in_specs=in_specs, out_specs=out_specs, check_vma=False
    )
```

```python
import functools

import jax
import jax.numpy as jnp
from jax import lax
from jax.experimental import pallas as pl
from jax.experimental.pallas import tpu as pltpu
from jax.sharding import PartitionSpec as P

DK = 128
DV = 128
EPS = 1e-06
SLOTS = 16
F32 = jnp.float32
BF16 = jnp.bfloat16
VMEM_LIMIT = 24 * 1024 * 1024


def dot(a, b):
    return jnp.dot(a, b, preferred_element_type=F32)


def silu(v):
    return v / (1.0 + jnp.exp(-v))


def split(v):
    high = v.astype(BF16)
    low = (v - high.astype(F32)).astype(BF16)
    return high, low


def pin(x):
    return pltpu.with_memory_space_constraint(x, pltpu.VMEM)


VMEM_SPEC = pl.BlockSpec(memory_space=pltpu.VMEM)
SMEM_SPEC = pl.BlockSpec(memory_space=pltpu.SMEM)
ANY_SPEC = pl.BlockSpec(memory_space=pl.ANY)


def call(body, name, out_shapes, smem, pinned, loose=(), scratch=(), aliases=None, outs=None):
    return pl.pallas_call(
        body,
        out_shape=tuple(out_shapes),
        in_specs=[SMEM_SPEC] * len(smem) + [VMEM_SPEC] * len(pinned) + [ANY_SPEC] * len(loose),
        out_specs=tuple(outs or [VMEM_SPEC] * len(out_shapes)),
        scratch_shapes=list(scratch),
        input_output_aliases=aliases or {},
        compiler_params=pltpu.CompilerParams(vmem_limit_bytes=VMEM_LIMIT),
        name=name,
    )(*smem, *(pin(x) for x in pinned), *loose)


def exchange(x, axis, bit):
    size = lax.axis_size(axis)
    return lax.ppermute(x, axis, [(i, i ^ bit) for i in range(size)])


def stack_kernel(count, *refs):
    for n, ref in enumerate(refs[:count]):
        refs[-1][n] = ref[...]


def stack(arrays, after=()):
    shape = (len(arrays), *arrays[0].shape)
    body = functools.partial(stack_kernel, len(arrays))
    [out] = call(body, "stack", [pltpu.VMEM(shape, arrays[0].dtype)], (), arrays, after)
    return out


def load_kernel(count, *refs):
    sources, targets, sems = refs[:count], refs[-1 - count : -1], refs[-1]
    copies = [pltpu.make_async_copy(a, b, sems.at[n]) for n, (a, b) in enumerate(zip(sources, targets))]
    for copy in copies:
        copy.start()
    for copy in copies:
        copy.wait()


def load(arrays, after=()):
    return call(
        functools.partial(load_kernel, len(arrays)),
        "load",
        [pltpu.VMEM(x.shape, x.dtype) for x in arrays],
        (),
        (),
        (*(pltpu.with_memory_space_constraint(x, pltpu.HBM) for x in arrays), *after),
        [pltpu.SemaphoreType.DMA((len(arrays),))],
    )


def bring_kernel(count, vectors, seq_count, head_count, me_ref, seq_ref, *refs):
    small = 3 + vectors
    sources, refs = refs[: small + count], refs[small + count :]
    targets, (pack_ref, extra_ref, gain_mine_ref, gain_inv_ref) = refs[:count], refs[count : count + 4]
    scratch, sems = refs[count + 4 : -1], refs[-1]
    ids, chosen, gain_after = scratch[:3]
    targets = (*scratch, *targets)
    copies = [pltpu.make_async_copy(a, b, sems.at[n]) for n, (a, b) in enumerate(zip(sources, targets))]
    for copy in copies:
        copy.start()
    for copy in copies[:small]:
        copy.wait()
    for n, ref in enumerate(scratch[3:]):
        pack_ref[n : n + 1, : ref.shape[1]] = ref[...]
    me, seq = me_ref[0], seq_ref[0]
    gain_mine_ref[...] = gain_after[me]
    gain_inv_ref[...] = 1.0 / gain_after[...]
    top, steps, seqs = ids.shape
    for z in range(seq_count):
        target = (seq ^ z) * head_count + me
        weight = jnp.zeros((steps, seqs), F32)
        for n in range(top):
            weight = weight + jnp.where(ids[n] == target, chosen[n], 0.0)
        high = weight.astype(BF16).astype(F32)
        both = jnp.concatenate([high, weight - high], axis=0)
        rows, width = extra_ref.shape[1:]
        both = jnp.concatenate([both, jnp.zeros((rows - 2 * steps, seqs), F32)], axis=0)
        both = jnp.concatenate([both, jnp.zeros((rows, width - seqs), F32)], axis=1)
        extra_ref[z] = both.astype(BF16)
    for copy in copies[small:]:
        copy.wait()


def bring(me, seq, arrays, vectors, ids, chosen, gain_after, seq_count):
    head_count, _, width = gain_after.shape
    small = (ids, chosen, gain_after, *vectors)
    return call(
        functools.partial(bring_kernel, len(arrays), len(vectors), seq_count, head_count),
        "bring",
        [pltpu.VMEM(x.shape, x.dtype) for x in arrays]
        + [
            pltpu.VMEM((8, 128), F32),
            pltpu.VMEM((seq_count, 16, width), BF16),
            pltpu.VMEM((1, width), F32),
            pltpu.VMEM(gain_after.shape, F32),
        ],
        (me, seq),
        (),
        [pltpu.with_memory_space_constraint(x, pltpu.HBM) for x in (*small, *arrays)],
        [pltpu.VMEM(x.shape, x.dtype) for x in small]
        + [pltpu.SemaphoreType.DMA((len(small) + len(arrays),))],
    )


def front_kernel(
    steps,
    head_count,
    me_ref,
    *refs,
):
    x_refs = refs[:2]
    (
        gain_ref,
        small_ref,
        pack_ref,
        wq,
        wk,
        wv,
        wz,
        wo_hbm,
        states_hbm,
        own_ref,
        sib_ref,
        keys_ref,
        delta_ref,
        total_ref,
        wo,
        states,
        left,
        recalls,
        sems,
    ) = refs[2:]
    me = me_ref[0]
    _, rows, width = x_refs[0].shape
    seqs = rows // steps
    key_heads = wq.shape[1] // DK
    value_heads = wv.shape[1] // DV
    group = value_heads // key_heads
    pair = group * DV

    parts = sems.shape[0] - 1
    part = seqs // parts
    copies = []
    for n in range(parts):
        span = pl.ds(n * part, part)
        copies.append(pltpu.make_async_copy(states_hbm.at[span], states.at[span], sems.at[n]))
    copies.append(pltpu.make_async_copy(wo_hbm, wo, sems.at[parts]))
    for copy in copies:
        copy.start()

    squares = jnp.zeros((rows, 1), F32)
    for j in range(head_count):
        xj = x_refs[j % 2][j // 2].astype(F32)
        squares = squares + jnp.sum(xj * xj, axis=1, keepdims=True)
    inverse = lax.rsqrt(squares / (head_count * width) + EPS)
    normed = []
    spans = []
    for j in range(head_count):
        block = me ^ j
        normed.append((x_refs[j % 2][j // 2].astype(F32) * inverse * gain_ref[block]).astype(BF16))
        spans.append(pl.ds(pl.multiple_of(block * width, width), width))

    def project(w_ref):
        total = None
        for j in range(head_count):
            term = dot(normed[j], w_ref[spans[j], :])
            total = term if total is None else total + term
        return total

    small = None
    for j in range(head_count):
        term = lax.dot_general(
            normed[j],
            small_ref[me ^ j],
            (((1,), (1,)), ((), ())),
            preferred_element_type=F32,
        )
        small = term if small is None else small + term
    betas = 1.0 / (1.0 + jnp.exp(-small[:, :value_heads]))
    alphas = small[:, value_heads : 2 * value_heads] + pack_ref[1:2, :value_heads]
    softplus = jnp.maximum(alphas, 0.0) + jnp.log1p(jnp.exp(-jnp.abs(alphas)))
    decays = jnp.exp(-pack_ref[0:1, :value_heads] * softplus)

    def units(v):
        return v * lax.rsqrt(jnp.sum(v * v, axis=1, keepdims=True) + EPS)

    queries_all = silu(project(wq))
    keys_all = silu(project(wk))
    keys, queries = [], []
    for i in range(key_heads):
        k = units(keys_all[:, i * DK : (i + 1) * DK])
        q = units(queries_all[:, i * DK : (i + 1) * DK]) * DK ** (-0.5)
        keys_ref[i] = k
        keys.append([k[t * seqs : (t + 1) * seqs] for t in range(steps)])
        queries.append([q[t * seqs : (t + 1) * seqs] for t in range(steps)])
        for t in range(steps):
            for at, v in ((t, keys[i][t]), (steps + t, queries[i][t])):
                high = v.astype(BF16).astype(F32)
                left[i, pl.ds(at, seqs, stride=SLOTS), :] = high
                left[i, pl.ds(2 * steps + at, seqs, stride=SLOTS), :] = v - high
        for at in range(4 * steps, SLOTS):
            left[i, pl.ds(at, seqs, stride=SLOTS), :] = jnp.zeros((seqs, DK), F32)
    values_all = silu(project(wv))
    gates = silu(project(wz))

    def one(s, carry):
        base = pl.multiple_of(s * SLOTS, SLOTS)
        for i in range(key_heads):
            lhs = left[i, pl.ds(base, SLOTS), :].astype(BF16)
            rhs = jnp.concatenate([states[s, i * group + u] for u in range(group)], axis=1)
            high, low = split(rhs)
            answer = dot(jnp.concatenate([lhs, lhs], axis=1), jnp.concatenate([high, low], axis=0))
            for u in range(group):
                recalls[i * group + u, pl.ds(base, SLOTS), :] = answer[:, u * DV : (u + 1) * DV]
        return carry

    for n in range(parts):
        copies[n].wait()
        lax.fori_loop(n * part, (n + 1) * part, one, 0, unroll=4)

    def wide(columns, t, i):
        return jnp.concatenate(
            [
                jnp.broadcast_to(
                    columns[t * seqs : (t + 1) * seqs, i * group + u : i * group + u + 1],
                    (seqs, DV),
                )
                for u in range(group)
            ],
            axis=1,
        )

    mixed_rows = [[] for _ in range(steps)]
    for i in range(key_heads):
        decay = [wide(decays, t, i) for t in range(steps)]
        beta = [wide(betas, t, i) for t in range(steps)]

        def read(at):
            return jnp.concatenate(
                [
                    recalls[i * group + u, pl.ds(at, seqs, stride=SLOTS), :]
                    + recalls[i * group + u, pl.ds(2 * steps + at, seqs, stride=SLOTS), :]
                    for u in range(group)
                ],
                axis=1,
            )

        deltas = []
        running = None
        for t in range(steps):
            running = decay[t] if running is None else running * decay[t]
            recall = running * read(t)
            answer = running * read(steps + t)
            deltas = [d * decay[t] for d in deltas]
            for u, d in enumerate(deltas):
                recall = recall + d * jnp.sum(keys[i][t] * keys[i][u], axis=1, keepdims=True)
                answer = answer + d * jnp.sum(queries[i][t] * keys[i][u], axis=1, keepdims=True)
            value = values_all[t * seqs : (t + 1) * seqs, i * pair : (i + 1) * pair]
            delta = beta[t] * (value - recall)
            answer = answer + delta * jnp.sum(queries[i][t] * keys[i][t], axis=1, keepdims=True)
            deltas.append(delta)
            mixed_rows[t].append(answer)
        for t in range(steps):
            delta_ref[i, t] = deltas[t]
        total_ref[i] = running
    mixed = jnp.concatenate([jnp.concatenate(m, axis=1) for m in mixed_rows], axis=0)
    gated = []
    for h in range(value_heads):
        m = mixed[:, h * DV : (h + 1) * DV]
        m = m * lax.rsqrt(jnp.mean(m * m, axis=1, keepdims=True) + EPS)
        gated.append((m * pack_ref[2:3, :DV] * gates[:, h * DV : (h + 1) * DV]).astype(BF16))
    gated = jnp.concatenate(gated, axis=1)
    copies[parts].wait()
    for c in range(head_count):
        piece = dot(gated, wo[:, c * width : (c + 1) * width]).astype(BF16)
        away = me ^ c

        @pl.when(away % 2 == 0)
        def _():
            own_ref[away // 2] = piece

        @pl.when(away % 2 == 1)
        def _():
            sib_ref[away // 2] = piece


def front(me, xs, gain, small, pack, wq, wk, wv, wz, wo, states, steps):
    pairs, rows, width = xs[0].shape
    head_count = 2 * pairs
    seqs = rows // steps
    key_heads = wq.shape[1] // DK
    value_heads = wv.shape[1] // DV
    pair = value_heads // key_heads * DV
    return call(
        functools.partial(front_kernel, steps, head_count),
        "front",
        [
            pltpu.VMEM((head_count // 2, rows, width), BF16),
            pltpu.VMEM((head_count // 2, rows, width), BF16),
            pltpu.VMEM((key_heads, rows, DK), F32),
            pltpu.VMEM((key_heads, steps, seqs, pair), F32),
            pltpu.VMEM((key_heads, seqs, pair), F32),
        ],
        (me,),
        (*xs, gain, small, pack, wq, wk, wv, wz),
        [pltpu.with_memory_space_constraint(x, pltpu.HBM) for x in (wo, states)],
        [
            pltpu.VMEM(wo.shape, BF16),
            pltpu.VMEM(states.shape, F32),
            pltpu.VMEM((key_heads, seqs * SLOTS, DK), F32),
            pltpu.VMEM((value_heads, seqs * SLOTS, DV), F32),
            pltpu.SemaphoreType.DMA((9,)),
        ],
    )


def rows_kernel(pairs, *refs):
    merged_ref, received = refs[0], refs[1:pairs]
    mine_ref, gain_ref, extra_ref, _ = refs[pairs : pairs + 4]
    resid_ref, x_ref = refs[pairs + 4 : pairs + 6]
    messages = refs[pairs + 6 :]
    rows = mine_ref.shape[0]
    resid = mine_ref[...].astype(F32) + merged_ref[0].astype(F32)
    for ref in received:
        resid = resid + ref[...].astype(F32)
    resid_ref[...] = resid
    x = (resid * gain_ref[...]).astype(BF16)
    x_ref[...] = x
    for z, ref in enumerate(messages):
        ref[:rows, :] = x
        ref[rows:, :] = extra_ref[z + 1]


def make_rows(merged, received, mine, gain, extra, after):
    rows, width = mine.shape
    message = pltpu.VMEM((rows + extra.shape[1], width), BF16)
    return call(
        functools.partial(rows_kernel, merged.shape[0]),
        "rows",
        [
            pltpu.VMEM((rows, width), F32),
            pltpu.VMEM((rows, width), BF16),
            *([message] * (extra.shape[0] - 1)),
        ],
        (),
        (merged, *received, mine, gain, extra),
        after,
    )


def slab_kernel(a_ref, b_ref, *refs):
    out_ref = refs[-1]
    rows = out_ref.shape[1]
    out_ref[0] = a_ref[:rows, :]
    out_ref[1] = b_ref[:rows, :]


def slab_pair(a, b, rows, after):
    [out] = call(slab_kernel, "slab", [pltpu.VMEM((2, rows, a.shape[1]), BF16)], (), (a, b), after)
    return out


PER_BLOCK = DK // SLOTS


def update_kernel(steps, blocks, keys_ref, delta_ref, total_ref, states_ref, *refs):
    out_ref, done_ref, left, right, olds, news, old_sems, sems = refs[-8:]
    half = PER_BLOCK // 2
    loads, stores = [], []
    for n, block in enumerate(blocks):
        for part in range(2):
            whole = pl.ds(block * PER_BLOCK + part * half, half)
            here = pl.ds(part * half, half)
            at = 2 * n + part
            loads.append(
                pltpu.make_async_copy(states_ref.at[whole], olds.at[n, here], old_sems.at[at])
            )
            stores.append(pltpu.make_async_copy(news.at[n, here], out_ref.at[whole], sems.at[at]))
            loads[-1].start()
    key_heads, rows, _ = keys_ref.shape
    seqs = rows // steps
    group = olds.shape[2] // key_heads
    first, count = blocks[0] * PER_BLOCK, len(blocks) * PER_BLOCK
    for i in range(key_heads):
        for at in range(SLOTS):
            rows_at = pl.ds(at, count, stride=SLOTS)
            t = at % steps
            k = keys_ref[i, t * seqs + first : t * seqs + first + count, :]
            k_high = k.astype(BF16).astype(F32)
            k = k - k_high if at >= 2 * steps else k_high
            left[i, rows_at, :] = k if at < 3 * steps else jnp.zeros_like(k)
            for u in range(group):
                d = delta_ref[i, t, first : first + count, u * DV : (u + 1) * DV]
                d_high = d.astype(BF16).astype(F32)
                d = d - d_high if steps <= at < 2 * steps else d_high
                right[i * group + u, rows_at, :] = d if at < 3 * steps else jnp.zeros_like(d)
    slot_of = lax.broadcasted_iota(jnp.int32, (DK, DK), 1) // SLOTS
    for n, block in enumerate(blocks):
        span = slice(n * DK, (n + 1) * DK)
        lhs = [jnp.transpose(left[i, span, :]) for i in range(key_heads)]
        rhs = [
            jnp.concatenate(
                [right[i * group + u, span, :] for u in range(group)], axis=1
            ).astype(BF16)
            for i in range(key_heads)
        ]
        for m in range(PER_BLOCK):
            if m % half == 0:
                loads[2 * n + m // half].wait()
            s = block * PER_BLOCK + m
            for i in range(key_heads):
                masked = jnp.where(slot_of == m, lhs[i], 0.0).astype(BF16)
                change = dot(masked, rhs[i])
                for u in range(group):
                    columns = slice(u * DV, (u + 1) * DV)
                    h = i * group + u
                    total = total_ref[i, s : s + 1, columns]
                    news[n, m, h] = olds[n, m, h] * total + change[:, columns]
            if m % half == half - 1:
                stores[2 * n + m // half].start()
    for copy in stores:
        copy.wait()
    done_ref[...] = jnp.zeros_like(done_ref)


def update(keys, deltas, totals, states, blocks, after, before=None):
    key_heads, steps, seqs, pair = deltas.shape
    rows = len(blocks) * DK
    value_heads = states.shape[1]
    loose = after if before is None else (before, *after)
    buffers = pltpu.VMEM((len(blocks), PER_BLOCK, *states.shape[1:]), F32)
    return call(
        functools.partial(update_kernel, steps, blocks),
        "update",
        [jax.ShapeDtypeStruct(states.shape, F32), jax.ShapeDtypeStruct((8, 128), F32)],
        (),
        (keys, deltas, totals),
        (pltpu.with_memory_space_constraint(states, pltpu.HBM), *loose),
        [
            pltpu.VMEM((key_heads, rows, DK), F32),
            pltpu.VMEM((value_heads, rows, DV), F32),
            buffers,
            buffers,
            pltpu.SemaphoreType.DMA((2 * len(blocks),)),
            pltpu.SemaphoreType.DMA((2 * len(blocks),)),
        ],
        None if before is None else {4: 0},
        [ANY_SPEC, VMEM_SPEC],
    )


def blocks_of(pieces, order, odd, me):
    xs, places = [], []
    for ref, part in zip(pieces, order):
        _, zs, rows, width = ref.shape
        for n, place in enumerate(part):
            xs.append(ref[n].reshape(zs * rows, width))
            places.append(me ^ (2 * place + odd))
    return xs, places


def rows_squares(xs, places, gain_inv_ref):
    squares = None
    for x, place in zip(xs, places):
        plain = x.astype(F32) * gain_inv_ref[place]
        plain = plain * plain
        for c in range(0, x.shape[1], 128):
            part = plain[:, c : c + 128]
            squares = part if squares is None else squares + part
    return jnp.sum(squares, axis=1, keepdims=True)


def columns_sum(total, xs, places, w_ref, columns):
    for x, place in zip(xs, places):
        width = x.shape[1]
        term = dot(x, w_ref[0, pl.ds(pl.multiple_of(place * width, width), width), columns])
        total = term if total is None else total + term
    return total


def expert_first_kernel(order, me_ref, *refs):
    pieces, (gain_inv_ref, w_ref) = refs[: len(order)], refs[len(order) : len(order) + 2]
    pre_ref, sq_ref = refs[-2:]
    xs, places = blocks_of(pieces, order, 0, me_ref[0])
    for c in range(0, w_ref.shape[2], 256):
        columns = slice(c, c + 256)
        pre_ref[:, columns] = columns_sum(None, xs, places, w_ref, columns)
    sq_ref[...] = rows_squares(xs, places, gain_inv_ref)


def expert_first(me, pieces, gain_inv, w, order, after=()):
    total = pieces[0].shape[1] * pieces[0].shape[2]
    return call(
        functools.partial(expert_first_kernel, order),
        "expert_first",
        [pltpu.VMEM((total, w.shape[2]), F32), pltpu.VMEM((total, 1), F32)],
        (me,),
        (*pieces, gain_inv, w),
        after,
    )


def expert_rest_kernel(order, order_out, steps, whole, me_ref, *refs):
    pieces, refs = refs[: len(order)], refs[len(order) :]
    gain_inv_ref, w_ref, pre_ref, sq_ref, down_ref = refs[:5]
    own, sib, sq_out = refs[-3:]
    me = me_ref[0]
    features = down_ref.shape[2]
    hidden_width = down_ref.shape[1]
    count, zs, rows, width = own.shape
    xs, places = blocks_of(pieces, order, 1, me)
    squares = sq_ref[...] + rows_squares(xs, places, gain_inv_ref)
    sq_out[...] = squares
    inverse = lax.rsqrt(squares / features + EPS)
    hidden = []
    for c in range(0, hidden_width, 256):
        parts = []
        for at in (c, hidden_width + c):
            columns = slice(at, at + 256)
            parts.append(columns_sum(pre_ref[:, columns], xs, places, w_ref, columns) * inverse)
        hidden.append((silu(parts[0]) * parts[1]).astype(BF16))
    hidden = jnp.concatenate(hidden, axis=1)
    weight = []
    for z in range(zs):
        ref = refs[5 + z]
        extra = ref[0] if z == 0 and whole else ref[rows:, :]
        columns = jnp.transpose(extra.astype(F32))
        for t in range(steps):
            both = columns[:, t : t + 1] + columns[:, steps + t : steps + t + 1]
            weight.append(both[: rows // steps])
    weight = jnp.concatenate(weight, axis=0)
    for odd, ref in ((1, sib), (0, own)):
        for n in range(count):
            block = me ^ (2 * order_out[n] + odd)
            columns = pl.ds(pl.multiple_of(block * width, width), width)
            result = dot(hidden, down_ref[0, :, columns]) * weight
            ref[n] = result.astype(BF16).reshape(zs, rows, width)


def expert_rest(me, pieces, gain_inv, w, pre, sq, down, weights, order, order_out, steps, whole, after):
    count = len(order_out)
    shape = (count, *pieces[0].shape[1:])
    return call(
        functools.partial(expert_rest_kernel, order, order_out, steps, whole),
        "expert_rest",
        [pltpu.VMEM(shape, BF16), pltpu.VMEM(shape, BF16), pltpu.VMEM(sq.shape, F32)],
        (me,),
        (*pieces, gain_inv, w, pre, sq, down, *weights),
        after,
    )


def bit_reversed(count):
    bits = count.bit_length() - 1
    return [int(format(n, "b").zfill(bits)[::-1], 2) if bits else 0 for n in range(count)]


def add(a, b):
    return (a.astype(F32) + b.astype(F32)).astype(BF16)


def half_sum_kernel(a_ref, b_ref, *refs):
    keep_ref, send_ref = refs[-2:]
    half = a_ref.shape[0] // 2
    keep_ref[...] = add(a_ref[:half], b_ref[:half])
    send_ref[...] = add(a_ref[half:], b_ref[half:])


def half_sum(a, b, after=()):
    shape = (a.shape[0] // 2, *a.shape[1:])
    return call(
        half_sum_kernel,
        "half_sum",
        [pltpu.VMEM(shape, BF16), pltpu.VMEM(shape, BF16)],
        (),
        (a, b),
        after,
    )


def last_sum_kernel(a_ref, b_ref, *outs):
    for z, ref in enumerate(outs):
        ref[...] = add(a_ref[0, z], b_ref[0, z])


def last_sum(a, b):
    _, zs, rows, width = a.shape
    return call(last_sum_kernel, "last_sum", [pltpu.VMEM((rows, width), BF16)] * zs, (), (a, b))


def one_sum_kernel(a_ref, b_ref, *refs):
    refs[-1][...] = add(a_ref[...], b_ref[...])


def one_sum(a, b, after=()):
    [out] = call(one_sum_kernel, "one_sum", [pltpu.VMEM(a.shape, BF16)], (), (a, b), after)
    return out


def finish_kernel(count, *refs):
    total = refs[0][...]
    for ref in refs[1:count]:
        total = total + ref[...].astype(F32)
    refs[-1][...] = total.astype(BF16)


def finish(base, slab, received, after):
    arrays = (base, slab, *received)
    [out] = call(
        functools.partial(finish_kernel, len(arrays)),
        "finish",
        [jax.ShapeDtypeStruct(base.shape, BF16)],
        (),
        arrays,
        after,
    )
    return out


def shared_in_kernel(me_ref, x_ref, w_ref, *refs):
    refs = refs[-2:]
    chunks, _, width = refs[0].shape
    half = w_ref.shape[1] // 2
    part = half // 2
    pre = dot(x_ref[...], w_ref[...]).astype(BF16)
    odd = me_ref[0] % 2
    for core in range(2):
        for n in range(chunks):
            up, at = divmod(n * width, part)
            start = up * half + core * part + at
            piece = pre[:, start : start + width]

            @pl.when(odd == core)
            def _():
                refs[0][n] = piece

            @pl.when(odd != core)
            def _():
                refs[1][n] = piece


def shared_in(me, x, w, after):
    rows, width = x.shape
    shape = (w.shape[1] // 2 // width, rows, width)
    return call(
        shared_in_kernel, "shared_in", [pltpu.VMEM(shape, BF16)] * 2, (me,), (x, w), after
    )


def open_kernel(a_ref, b_ref, keep_ref, received_ref, *refs):
    out_ref = refs[-1]
    rows = out_ref.shape[2]
    out_ref[0, 0] = a_ref[:rows, :]
    out_ref[0, 1] = b_ref[:rows, :]
    out_ref[1] = add(keep_ref[...], received_ref[...])


def open_side(a, b, keep, received, after):
    shape = (2, *keep.shape)
    [out] = call(open_kernel, "open", [pltpu.VMEM(shape, BF16)], (), (a, b, keep, received), after)
    return out


def grow_kernel(mine_ref, received_ref, *refs):
    out_ref = refs[-1]
    count = mine_ref.shape[0] - 1
    out_ref[:count] = mine_ref[:count]
    out_ref[count : 2 * count] = received_ref[:count]
    out_ref[2 * count] = add(mine_ref[count], received_ref[count])


def grow(mine, received, after):
    shape = (2 * mine.shape[0] - 1, *mine.shape[1:])
    [out] = call(grow_kernel, "grow", [pltpu.VMEM(shape, BF16)], (), (mine, received), after)
    return out


def shared_hidden_kernel(features, a_ref, b_ref, sq_ref, *refs):
    out_ref = refs[-1]
    last, chunks, rows, width = a_ref.shape
    inverse = lax.rsqrt(sq_ref[:rows, :] / features + EPS)
    pre = [
        (a_ref[last - 1, n].astype(F32) + b_ref[last - 1, n].astype(F32)) * inverse
        for n in range(chunks)
    ]
    for n in range(chunks // 2):
        columns = slice(n * width, (n + 1) * width)
        out_ref[:, columns] = (silu(pre[n]) * pre[chunks // 2 + n]).astype(BF16)


def shared_hidden(features, a, b, sq, after):
    _, chunks, rows, width = a.shape
    [out] = call(
        functools.partial(shared_hidden_kernel, features),
        "shared_hidden",
        [pltpu.VMEM((rows, chunks // 2 * width), BF16)],
        (),
        (a, b, sq),
        after,
    )
    return out


def shared_out_kernel(me_ref, a_ref, b_ref, resid_ref, w_ref, out_ref):
    part = a_ref.shape[1]
    odd = me_ref[0] % 2
    total = resid_ref[...]
    for core, ref in ((odd, a_ref), (1 - odd, b_ref)):
        total = total + dot(ref[...], w_ref[pl.ds(pl.multiple_of(core * part, part), part), :])
    out_ref[...] = total


def shared_out(me, a, b, resid, w):
    [out] = call(
        shared_out_kernel, "shared_out", [pltpu.VMEM(resid.shape, F32)], (me,), (a, b, resid, w)
    )
    return out


def on_device(
    tokens,
    states,
    router_ids,
    router_weights,
    input_gain,
    w_query,
    w_key,
    w_value,
    w_zgate,
    w_beta,
    w_alpha,
    decay_scale,
    dt_bias,
    gated_gain,
    w_out,
    post_gain,
    w_shared_in,
    w_shared_out,
    w_expert_in,
    w_expert_out,
):
    seq_count = lax.axis_size("seq")
    head_count = lax.axis_size("head")
    head_index = lax.axis_index("head")
    seq_index = lax.axis_index("seq")
    me = head_index.astype(jnp.int32).reshape(1)
    seqs, steps, width = tokens.shape
    rows = seqs * steps
    features = head_count * width
    pairs = head_count // 2
    axes = [1 << n for n in range(1, head_count.bit_length() - 1)]

    mine = jnp.transpose(tokens, (1, 0, 2)).reshape(rows, width)
    value_heads = w_beta.shape[1]
    small = jnp.concatenate([w_beta, w_alpha], axis=1)
    small = jnp.transpose(small.reshape(head_count, width, 2 * value_heads), (0, 2, 1))
    small = jnp.pad(small, ((0, 0), (0, -2 * value_heads % 16), (0, 0)))

    others = [exchange(mine, "head", 2 * p) for p in range(1, pairs)]
    mine, w_query, w_key, w_value, w_shared_in, w_shared_out, gain, pack, extra, gain_mine, gain_inv = bring(
        me,
        seq_index.astype(jnp.int32).reshape(1),
        (
            mine,
            w_query,
            w_key,
            w_value,
            w_shared_in,
            w_shared_out,
            input_gain.reshape(head_count, 1, width),
        ),
        [v.reshape(1, -1) for v in (decay_scale, dt_bias, gated_gain)],
        jnp.transpose(router_ids, (2, 1, 0)),
        jnp.transpose(router_weights, (2, 1, 0)),
        post_gain.reshape(head_count, 1, width),
        seq_count,
    )
    own_tokens = stack((mine, *others))
    sib_tokens = exchange(own_tokens, "head", 1)
    [w_zgate] = load((w_zgate,), (own_tokens,))
    gathered = (own_tokens, sib_tokens)
    own, sib, keys, deltas, totals = front(
        me, gathered, gain, small, pack, w_query, w_key, w_value, w_zgate, w_out, states, steps
    )

    merged = one_sum(own, exchange(sib, "head", 1))
    received = [exchange(merged[p], "head", 2 * p) for p in range(1, pairs)]
    [w_in] = load((w_expert_in,), (merged,))
    resid, x, *messages = make_rows(merged, received, mine, gain_mine, extra, (w_in,))

    half = seq_count // 2
    messages = [exchange(m, "seq", z + 1) for z, m in enumerate(messages)]
    slabs = [x] + messages
    natural, reverse = list(range(pairs)), bit_reversed(pairs)
    blocks = tuple(range(seqs // PER_BLOCK))
    quarters = [blocks[len(blocks) * n // 4 : len(blocks) * (n + 1) // 4] for n in range(4)]
    shared_keep, sent = shared_in(me, x, w_shared_in, ())
    shared_received = exchange(sent, "head", 1)
    [w_down] = load((w_expert_out,), (shared_keep,))
    states_out, done = update(keys, deltas, totals, states, quarters[3], (w_down,))
    if half == 2:
        side = open_side(*slabs[:2], shared_keep, shared_received, (*slabs[2:], done))
    else:
        rows_only = jnp.stack([m[:rows] for m in slabs[:half]])
        side = jnp.stack([rows_only, add(shared_keep, shared_received)])
    if half == 2:
        other = slab_pair(*slabs[2:], rows, ())[None]
    else:
        other = jnp.stack([m[:rows] for m in slabs[half:]])[None]
    states_out, done = update(
        keys, deltas, totals, states, quarters[0] + quarters[1], (side, other), states_out
    )
    for bit in axes[:0:-1]:
        received = exchange(other, "head", bit)
        if other.shape[0] == 1:
            other = stack((other[0], received[0]), (done,))
        else:
            other = jnp.concatenate([other, received])
    for bit in axes[:-1]:
        side = grow(side, exchange(side, "head", bit), (done, other))
    sides = [[side, exchange(side, "head", axes[-1])]]
    sides.append([other, exchange(other, "head", axes[0])])
    siblings = [[exchange(piece, "head", 1) for piece in side] for side in sides]
    middle = pairs // 2
    orders = tuple((tuple(o[:middle]), tuple(o[middle:])) for o in (natural, reverse))

    firsts = []
    for side, order in zip(sides, orders):
        firsts.append(expert_first(me, side, gain_inv, w_in, order, (done,)))
        done = firsts[-1][1]
    owns, sibs, squares = [], [], []
    weights = (extra, *messages)
    for n, order_out in enumerate((reverse, natural)):
        own, sib, square = expert_rest(
            me,
            siblings[n],
            gain_inv,
            w_in,
            *firsts[n],
            w_down,
            weights[n * half : (n + 1) * half],
            orders[n],
            order_out,
            steps,
            n == 0,
            tuple(owns),
        )
        owns.append(own)
        sibs.append(sib)
        squares.append(square)
    received = [exchange(sib, "head", 1) for sib in sibs]
    tie = ()
    for n, bits in enumerate(zip(axes, axes[::-1])):
        for side, bit in enumerate(bits):
            owns[side], sent = half_sum(owns[side], received[side], tie)
            received[side] = exchange(sent, "head", bit)
        if n == 0:
            states_out, done = update(
                keys, deltas, totals, states, quarters[2], tuple(owns), states_out
            )
            hidden = shared_hidden(features, *sides[0], squares[0], tuple(owns))
            hidden_received = exchange(hidden, "head", 1)
            tie = (done, hidden_received)
    base = shared_out(me, hidden, hidden_received, resid, w_shared_out)
    slabs = []
    for side in range(2):
        slabs += last_sum(owns[side], received[side])
    received = [exchange(slabs[z], "seq", z) for z in range(1, seq_count)]
    result = finish(base, slabs[0], received, ())
    layer_out = jnp.transpose(result.reshape(steps, seqs, width), (1, 0, 2))
    return (layer_out, states_out)


def solution(mesh):
    in_specs = (
        P("seq", None, "head"),
        P("seq", "head", None, None),
        P("seq", None, None),
        P("seq", None, None),
        P(),
        P(None, "head"),
        P(None, "head"),
        P(None, "head"),
        P(None, "head"),
        P(None, "head"),
        P(None, "head"),
        P("head"),
        P("head"),
        P(),
        P("head", None),
        P(),
        P("head", None),
        P(None, "head"),
        P(("seq", "head"), None, None),
        P(("seq", "head"), None, None),
    )
    out_specs = (P("seq", None, "head"), P("seq", "head", None, None))
    return jax.shard_map(
        on_device, mesh=mesh, in_specs=in_specs, out_specs=out_specs, check_vma=False
    )
```

```python
import functools

import jax
import jax.numpy as jnp
from jax import lax
from jax.experimental import pallas as pl
from jax.experimental.pallas import tpu as pltpu
from jax.sharding import PartitionSpec as P

DK = 128
DV = 128
EPS = 1e-06
SLOTS = 16
F32 = jnp.float32
BF16 = jnp.bfloat16
VMEM_LIMIT = 24 * 1024 * 1024


def dot(a, b):
    return jnp.dot(a, b, preferred_element_type=F32)


def silu(v):
    return v / (1.0 + jnp.exp(-v))


def split(v):
    high = v.astype(BF16)
    low = (v - high.astype(F32)).astype(BF16)
    return high, low


def pin(x):
    return pltpu.with_memory_space_constraint(x, pltpu.VMEM)


VMEM_SPEC = pl.BlockSpec(memory_space=pltpu.VMEM)
SMEM_SPEC = pl.BlockSpec(memory_space=pltpu.SMEM)
ANY_SPEC = pl.BlockSpec(memory_space=pl.ANY)


def call(body, name, out_shapes, smem, pinned, loose=(), scratch=(), aliases=None, outs=None):
    return pl.pallas_call(
        body,
        out_shape=tuple(out_shapes),
        in_specs=[SMEM_SPEC] * len(smem) + [VMEM_SPEC] * len(pinned) + [ANY_SPEC] * len(loose),
        out_specs=tuple(outs or [VMEM_SPEC] * len(out_shapes)),
        scratch_shapes=list(scratch),
        input_output_aliases=aliases or {},
        compiler_params=pltpu.CompilerParams(vmem_limit_bytes=VMEM_LIMIT),
        name=name,
    )(*smem, *(pin(x) for x in pinned), *loose)


def exchange(x, axis, bit):
    size = lax.axis_size(axis)
    return lax.ppermute(x, axis, [(i, i ^ bit) for i in range(size)])


def stack_kernel(count, *refs):
    for n, ref in enumerate(refs[:count]):
        refs[-1][n] = ref[...]


def stack(arrays, after=()):
    shape = (len(arrays), *arrays[0].shape)
    body = functools.partial(stack_kernel, len(arrays))
    [out] = call(body, "stack", [pltpu.VMEM(shape, arrays[0].dtype)], (), arrays, after)
    return out


def load_kernel(count, *refs):
    sources, targets, sems = refs[:count], refs[-1 - count : -1], refs[-1]
    copies = [pltpu.make_async_copy(a, b, sems.at[n]) for n, (a, b) in enumerate(zip(sources, targets))]
    for copy in copies:
        copy.start()
    for copy in copies:
        copy.wait()


def load(arrays, after=()):
    return call(
        functools.partial(load_kernel, len(arrays)),
        "load",
        [pltpu.VMEM(x.shape, x.dtype) for x in arrays],
        (),
        (),
        (*(pltpu.with_memory_space_constraint(x, pltpu.HBM) for x in arrays), *after),
        [pltpu.SemaphoreType.DMA((len(arrays),))],
    )


def bring_kernel(count, vectors, seq_count, head_count, me_ref, seq_ref, *refs):
    small = 3 + vectors
    sources, refs = refs[: small + count], refs[small + count :]
    targets, (pack_ref, extra_ref, gain_mine_ref, gain_inv_ref) = refs[:count], refs[count : count + 4]
    scratch, sems = refs[count + 4 : -1], refs[-1]
    ids, chosen, gain_after = scratch[:3]
    targets = (*scratch, *targets)
    copies = [pltpu.make_async_copy(a, b, sems.at[n]) for n, (a, b) in enumerate(zip(sources, targets))]
    for copy in copies:
        copy.start()
    for copy in copies[:small]:
        copy.wait()
    for n, ref in enumerate(scratch[3:]):
        pack_ref[n : n + 1, : ref.shape[1]] = ref[...]
    me, seq = me_ref[0], seq_ref[0]
    gain_mine_ref[...] = gain_after[me]
    gain_inv_ref[...] = 1.0 / gain_after[...]
    top, steps, seqs = ids.shape
    for z in range(seq_count):
        target = (seq ^ z) * head_count + me
        weight = jnp.zeros((steps, seqs), F32)
        for n in range(top):
            weight = weight + jnp.where(ids[n] == target, chosen[n], 0.0)
        high = weight.astype(BF16).astype(F32)
        both = jnp.concatenate([high, weight - high], axis=0)
        rows, width = extra_ref.shape[1:]
        both = jnp.concatenate([both, jnp.zeros((rows - 2 * steps, seqs), F32)], axis=0)
        both = jnp.concatenate([both, jnp.zeros((rows, width - seqs), F32)], axis=1)
        extra_ref[z] = both.astype(BF16)
    for copy in copies[small:]:
        copy.wait()


def bring(me, seq, arrays, vectors, ids, chosen, gain_after, seq_count):
    head_count, _, width = gain_after.shape
    small = (ids, chosen, gain_after, *vectors)
    return call(
        functools.partial(bring_kernel, len(arrays), len(vectors), seq_count, head_count),
        "bring",
        [pltpu.VMEM(x.shape, x.dtype) for x in arrays]
        + [
            pltpu.VMEM((8, 128), F32),
            pltpu.VMEM((seq_count, 16, width), BF16),
            pltpu.VMEM((1, width), F32),
            pltpu.VMEM(gain_after.shape, F32),
        ],
        (me, seq),
        (),
        [pltpu.with_memory_space_constraint(x, pltpu.HBM) for x in (*small, *arrays)],
        [pltpu.VMEM(x.shape, x.dtype) for x in small]
        + [pltpu.SemaphoreType.DMA((len(small) + len(arrays),))],
    )


def front_kernel(
    steps,
    head_count,
    me_ref,
    *refs,
):
    x_refs = refs[:2]
    (
        gain_ref,
        small_ref,
        pack_ref,
        wq,
        wk,
        wv,
        wz,
        wo_hbm,
        states_hbm,
        own_ref,
        sib_ref,
        keys_ref,
        delta_ref,
        total_ref,
        wo,
        states,
        left,
        recalls,
        sems,
    ) = refs[2:]
    me = me_ref[0]
    _, rows, width = x_refs[0].shape
    seqs = rows // steps
    key_heads = wq.shape[1] // DK
    value_heads = wv.shape[1] // DV
    group = value_heads // key_heads
    pair = group * DV

    parts = sems.shape[0] - 1
    part = seqs // parts
    copies = []
    for n in range(parts):
        span = pl.ds(n * part, part)
        copies.append(pltpu.make_async_copy(states_hbm.at[span], states.at[span], sems.at[n]))
    copies.append(pltpu.make_async_copy(wo_hbm, wo, sems.at[parts]))
    for copy in copies:
        copy.start()

    squares = jnp.zeros((rows, 1), F32)
    for j in range(head_count):
        xj = x_refs[j % 2][j // 2].astype(F32)
        squares = squares + jnp.sum(xj * xj, axis=1, keepdims=True)
    inverse = lax.rsqrt(squares / (head_count * width) + EPS)
    normed = []
    spans = []
    for j in range(head_count):
        block = me ^ j
        normed.append((x_refs[j % 2][j // 2].astype(F32) * inverse * gain_ref[block]).astype(BF16))
        spans.append(pl.ds(pl.multiple_of(block * width, width), width))

    def project(w_ref):
        total = None
        for j in range(head_count):
            term = dot(normed[j], w_ref[spans[j], :])
            total = term if total is None else total + term
        return total

    small = None
    for j in range(head_count):
        term = lax.dot_general(
            normed[j],
            small_ref[me ^ j],
            (((1,), (1,)), ((), ())),
            preferred_element_type=F32,
        )
        small = term if small is None else small + term
    betas = 1.0 / (1.0 + jnp.exp(-small[:, :value_heads]))
    alphas = small[:, value_heads : 2 * value_heads] + pack_ref[1:2, :value_heads]
    softplus = jnp.maximum(alphas, 0.0) + jnp.log1p(jnp.exp(-jnp.abs(alphas)))
    decays = jnp.exp(-pack_ref[0:1, :value_heads] * softplus)

    def units(v):
        return v * lax.rsqrt(jnp.sum(v * v, axis=1, keepdims=True) + EPS)

    queries_all = silu(project(wq))
    keys_all = silu(project(wk))
    keys, queries = [], []
    for i in range(key_heads):
        k = units(keys_all[:, i * DK : (i + 1) * DK])
        q = units(queries_all[:, i * DK : (i + 1) * DK]) * DK ** (-0.5)
        keys_ref[i] = k
        keys.append([k[t * seqs : (t + 1) * seqs] for t in range(steps)])
        queries.append([q[t * seqs : (t + 1) * seqs] for t in range(steps)])
        for t in range(steps):
            for at, v in ((t, keys[i][t]), (steps + t, queries[i][t])):
                high = v.astype(BF16).astype(F32)
                left[i, pl.ds(at, seqs, stride=SLOTS), :] = high
                left[i, pl.ds(2 * steps + at, seqs, stride=SLOTS), :] = v - high
        for at in range(4 * steps, SLOTS):
            left[i, pl.ds(at, seqs, stride=SLOTS), :] = jnp.zeros((seqs, DK), F32)
    values_all = silu(project(wv))
    gates = silu(project(wz))

    def one(s, carry):
        base = pl.multiple_of(s * SLOTS, SLOTS)
        for i in range(key_heads):
            lhs = left[i, pl.ds(base, SLOTS), :].astype(BF16)
            rhs = jnp.concatenate([states[s, i * group + u] for u in range(group)], axis=1)
            high, low = split(rhs)
            answer = dot(jnp.concatenate([lhs, lhs], axis=1), jnp.concatenate([high, low], axis=0))
            for u in range(group):
                recalls[i * group + u, pl.ds(base, SLOTS), :] = answer[:, u * DV : (u + 1) * DV]
        return carry

    for n in range(parts):
        copies[n].wait()
        lax.fori_loop(n * part, (n + 1) * part, one, 0, unroll=4)

    def wide(columns, t, i):
        return jnp.concatenate(
            [
                jnp.broadcast_to(
                    columns[t * seqs : (t + 1) * seqs, i * group + u : i * group + u + 1],
                    (seqs, DV),
                )
                for u in range(group)
            ],
            axis=1,
        )

    mixed_rows = [[] for _ in range(steps)]
    for i in range(key_heads):
        decay = [wide(decays, t, i) for t in range(steps)]
        beta = [wide(betas, t, i) for t in range(steps)]

        def read(at):
            return jnp.concatenate(
                [
                    recalls[i * group + u, pl.ds(at, seqs, stride=SLOTS), :]
                    + recalls[i * group + u, pl.ds(2 * steps + at, seqs, stride=SLOTS), :]
                    for u in range(group)
                ],
                axis=1,
            )

        deltas = []
        running = None
        for t in range(steps):
            running = decay[t] if running is None else running * decay[t]
            recall = running * read(t)
            answer = running * read(steps + t)
            deltas = [d * decay[t] for d in deltas]
            for u, d in enumerate(deltas):
                recall = recall + d * jnp.sum(keys[i][t] * keys[i][u], axis=1, keepdims=True)
                answer = answer + d * jnp.sum(queries[i][t] * keys[i][u], axis=1, keepdims=True)
            value = values_all[t * seqs : (t + 1) * seqs, i * pair : (i + 1) * pair]
            delta = beta[t] * (value - recall)
            answer = answer + delta * jnp.sum(queries[i][t] * keys[i][t], axis=1, keepdims=True)
            deltas.append(delta)
            mixed_rows[t].append(answer)
        for t in range(steps):
            delta_ref[i, t] = deltas[t]
        total_ref[i] = running
    mixed = jnp.concatenate([jnp.concatenate(m, axis=1) for m in mixed_rows], axis=0)
    gated = []
    for h in range(value_heads):
        m = mixed[:, h * DV : (h + 1) * DV]
        m = m * lax.rsqrt(jnp.mean(m * m, axis=1, keepdims=True) + EPS)
        gated.append((m * pack_ref[2:3, :DV] * gates[:, h * DV : (h + 1) * DV]).astype(BF16))
    gated = jnp.concatenate(gated, axis=1)
    copies[parts].wait()
    for c in range(head_count):
        piece = dot(gated, wo[:, c * width : (c + 1) * width]).astype(BF16)
        away = me ^ c

        @pl.when(away % 2 == 0)
        def _():
            own_ref[away // 2] = piece

        @pl.when(away % 2 == 1)
        def _():
            sib_ref[away // 2] = piece


def front(me, xs, gain, small, pack, wq, wk, wv, wz, wo, states, steps):
    pairs, rows, width = xs[0].shape
    head_count = 2 * pairs
    seqs = rows // steps
    key_heads = wq.shape[1] // DK
    value_heads = wv.shape[1] // DV
    pair = value_heads // key_heads * DV
    return call(
        functools.partial(front_kernel, steps, head_count),
        "front",
        [
            pltpu.VMEM((head_count // 2, rows, width), BF16),
            pltpu.VMEM((head_count // 2, rows, width), BF16),
            pltpu.VMEM((key_heads, rows, DK), F32),
            pltpu.VMEM((key_heads, steps, seqs, pair), F32),
            pltpu.VMEM((key_heads, seqs, pair), F32),
        ],
        (me,),
        (*xs, gain, small, pack, wq, wk, wv, wz),
        [pltpu.with_memory_space_constraint(x, pltpu.HBM) for x in (wo, states)],
        [
            pltpu.VMEM(wo.shape, BF16),
            pltpu.VMEM(states.shape, F32),
            pltpu.VMEM((key_heads, seqs * SLOTS, DK), F32),
            pltpu.VMEM((value_heads, seqs * SLOTS, DV), F32),
            pltpu.SemaphoreType.DMA((9,)),
        ],
    )


def rows_kernel(pairs, me_ref, *refs):
    merged_ref, received = refs[0], refs[1:pairs]
    mine_ref, gain_ref, extra_ref, w_ref, _ = refs[pairs : pairs + 5]
    resid_ref, x_ref, keep_ref, send_ref = refs[pairs + 5 : pairs + 9]
    messages = refs[pairs + 9 :]
    rows = mine_ref.shape[0]
    resid = mine_ref[...].astype(F32) + merged_ref[...].astype(F32)
    for ref in received:
        resid = resid + ref[...].astype(F32)
    resid_ref[...] = resid
    x = (resid * gain_ref[...]).astype(BF16)
    x_ref[...] = x
    for z, ref in enumerate(messages):
        ref[:rows, :] = x
        ref[rows:, :] = extra_ref[z + 1]
    chunks, _, width = keep_ref.shape
    half = w_ref.shape[1] // 2
    part = half // 2
    pre = dot(x, w_ref[...]).astype(BF16)
    odd = me_ref[0] % 2
    for core in range(2):
        for n in range(chunks):
            up, at = divmod(n * width, part)
            start = up * half + core * part + at
            piece = pre[:, start : start + width]

            @pl.when(odd == core)
            def _():
                keep_ref[n] = piece

            @pl.when(odd != core)
            def _():
                send_ref[n] = piece


def make_rows(me, merged, received, mine, gain, extra, w, after):
    rows, width = mine.shape
    message = pltpu.VMEM((rows + extra.shape[1], width), BF16)
    shared = pltpu.VMEM((w.shape[1] // 2 // width, rows, width), BF16)
    return call(
        functools.partial(rows_kernel, 1 + len(received)),
        "rows",
        [
            pltpu.VMEM((rows, width), F32),
            pltpu.VMEM((rows, width), BF16),
            shared,
            shared,
            *([message] * (extra.shape[0] - 1)),
        ],
        (me,),
        (merged, *received, mine, gain, extra, w),
        after,
    )


def slab_kernel(a_ref, b_ref, *refs):
    out_ref = refs[-1]
    rows = out_ref.shape[1]
    out_ref[0] = a_ref[:rows, :]
    out_ref[1] = b_ref[:rows, :]


def slab_pair(a, b, rows, after):
    [out] = call(slab_kernel, "slab", [pltpu.VMEM((2, rows, a.shape[1]), BF16)], (), (a, b), after)
    return out


PER_BLOCK = DK // SLOTS


def update_kernel(steps, blocks, keys_ref, delta_ref, total_ref, states_ref, *refs):
    out_ref, done_ref, left, right, olds, news, old_sems, sems = refs[-8:]
    half = PER_BLOCK // 2
    loads, stores = [], []
    for n, block in enumerate(blocks):
        for part in range(2):
            whole = pl.ds(block * PER_BLOCK + part * half, half)
            here = pl.ds(part * half, half)
            at = 2 * n + part
            loads.append(
                pltpu.make_async_copy(states_ref.at[whole], olds.at[n, here], old_sems.at[at])
            )
            stores.append(pltpu.make_async_copy(news.at[n, here], out_ref.at[whole], sems.at[at]))
            loads[-1].start()
    key_heads, rows, _ = keys_ref.shape
    seqs = rows // steps
    group = olds.shape[2] // key_heads
    first, count = blocks[0] * PER_BLOCK, len(blocks) * PER_BLOCK
    for i in range(key_heads):
        for at in range(SLOTS):
            rows_at = pl.ds(at, count, stride=SLOTS)
            t = at % steps
            k = keys_ref[i, t * seqs + first : t * seqs + first + count, :]
            k_high = k.astype(BF16).astype(F32)
            k = k - k_high if at >= 2 * steps else k_high
            left[i, rows_at, :] = k if at < 3 * steps else jnp.zeros_like(k)
            for u in range(group):
                d = delta_ref[i, t, first : first + count, u * DV : (u + 1) * DV]
                d_high = d.astype(BF16).astype(F32)
                d = d - d_high if steps <= at < 2 * steps else d_high
                right[i * group + u, rows_at, :] = d if at < 3 * steps else jnp.zeros_like(d)
    slot_of = lax.broadcasted_iota(jnp.int32, (DK, DK), 1) // SLOTS
    for n, block in enumerate(blocks):
        span = slice(n * DK, (n + 1) * DK)
        lhs = [jnp.transpose(left[i, span, :]) for i in range(key_heads)]
        rhs = [
            jnp.concatenate(
                [right[i * group + u, span, :] for u in range(group)], axis=1
            ).astype(BF16)
            for i in range(key_heads)
        ]
        for m in range(PER_BLOCK):
            if m % half == 0:
                loads[2 * n + m // half].wait()
            s = block * PER_BLOCK + m
            for i in range(key_heads):
                masked = jnp.where(slot_of == m, lhs[i], 0.0).astype(BF16)
                change = dot(masked, rhs[i])
                for u in range(group):
                    columns = slice(u * DV, (u + 1) * DV)
                    h = i * group + u
                    total = total_ref[i, s : s + 1, columns]
                    news[n, m, h] = olds[n, m, h] * total + change[:, columns]
            if m % half == half - 1:
                stores[2 * n + m // half].start()
    for copy in stores:
        copy.wait()
    done_ref[...] = jnp.zeros_like(done_ref)


def update(keys, deltas, totals, states, blocks, after, before=None):
    key_heads, steps, seqs, pair = deltas.shape
    rows = len(blocks) * DK
    value_heads = states.shape[1]
    loose = after if before is None else (before, *after)
    buffers = pltpu.VMEM((len(blocks), PER_BLOCK, *states.shape[1:]), F32)
    return call(
        functools.partial(update_kernel, steps, blocks),
        "update",
        [jax.ShapeDtypeStruct(states.shape, F32), jax.ShapeDtypeStruct((8, 128), F32)],
        (),
        (keys, deltas, totals),
        (pltpu.with_memory_space_constraint(states, pltpu.HBM), *loose),
        [
            pltpu.VMEM((key_heads, rows, DK), F32),
            pltpu.VMEM((value_heads, rows, DV), F32),
            buffers,
            buffers,
            pltpu.SemaphoreType.DMA((2 * len(blocks),)),
            pltpu.SemaphoreType.DMA((2 * len(blocks),)),
        ],
        None if before is None else {4: 0},
        [ANY_SPEC, VMEM_SPEC],
    )


def blocks_of(pieces, order, odd, me):
    xs, places = [], []
    for ref, part in zip(pieces, order):
        _, zs, rows, width = ref.shape
        for n, place in enumerate(part):
            xs.append(ref[n].reshape(zs * rows, width))
            places.append(me ^ (2 * place + odd))
    return xs, places


def rows_squares(xs, places, gain_inv_ref):
    squares = None
    for x, place in zip(xs, places):
        plain = x.astype(F32) * gain_inv_ref[place]
        plain = plain * plain
        for c in range(0, x.shape[1], 128):
            part = plain[:, c : c + 128]
            squares = part if squares is None else squares + part
    return jnp.sum(squares, axis=1, keepdims=True)


def columns_sum(total, xs, places, w_ref, columns):
    for x, place in zip(xs, places):
        width = x.shape[1]
        term = dot(x, w_ref[0, pl.ds(pl.multiple_of(place * width, width), width), columns])
        total = term if total is None else total + term
    return total


def expert_first_kernel(order, me_ref, *refs):
    pieces, (gain_inv_ref, w_ref) = refs[: len(order)], refs[len(order) : len(order) + 2]
    pre_ref, sq_ref = refs[-2:]
    xs, places = blocks_of(pieces, order, 0, me_ref[0])
    for c in range(0, w_ref.shape[2], 256):
        columns = slice(c, c + 256)
        pre_ref[:, columns] = columns_sum(None, xs, places, w_ref, columns)
    sq_ref[...] = rows_squares(xs, places, gain_inv_ref)


def expert_first(me, pieces, gain_inv, w, order, after=()):
    total = pieces[0].shape[1] * pieces[0].shape[2]
    return call(
        functools.partial(expert_first_kernel, order),
        "expert_first",
        [pltpu.VMEM((total, w.shape[2]), F32), pltpu.VMEM((total, 1), F32)],
        (me,),
        (*pieces, gain_inv, w),
        after,
    )


def expert_rest_kernel(order, order_out, steps, whole, me_ref, *refs):
    pieces, refs = refs[: len(order)], refs[len(order) :]
    gain_inv_ref, w_ref, pre_ref, sq_ref, down_ref = refs[:5]
    own, sib, sq_out = refs[-3:]
    me = me_ref[0]
    features = down_ref.shape[2]
    hidden_width = down_ref.shape[1]
    count, zs, rows, width = own.shape
    xs, places = blocks_of(pieces, order, 1, me)
    squares = sq_ref[...] + rows_squares(xs, places, gain_inv_ref)
    sq_out[...] = squares
    inverse = lax.rsqrt(squares / features + EPS)
    hidden = []
    for c in range(0, hidden_width, 256):
        parts = []
        for at in (c, hidden_width + c):
            columns = slice(at, at + 256)
            parts.append(columns_sum(pre_ref[:, columns], xs, places, w_ref, columns) * inverse)
        hidden.append((silu(parts[0]) * parts[1]).astype(BF16))
    hidden = jnp.concatenate(hidden, axis=1)
    weight = []
    for z in range(zs):
        ref = refs[5 + z]
        extra = ref[0] if z == 0 and whole else ref[rows:, :]
        columns = jnp.transpose(extra.astype(F32))
        for t in range(steps):
            both = columns[:, t : t + 1] + columns[:, steps + t : steps + t + 1]
            weight.append(both[: rows // steps])
    weight = jnp.concatenate(weight, axis=0)
    for odd, ref in ((1, sib), (0, own)):
        for n in range(count):
            block = me ^ (2 * order_out[n] + odd)
            columns = pl.ds(pl.multiple_of(block * width, width), width)
            result = dot(hidden, down_ref[0, :, columns]) * weight
            ref[n] = result.astype(BF16).reshape(zs, rows, width)


def expert_rest(me, pieces, gain_inv, w, pre, sq, down, weights, order, order_out, steps, whole, after):
    count = len(order_out)
    shape = (count, *pieces[0].shape[1:])
    return call(
        functools.partial(expert_rest_kernel, order, order_out, steps, whole),
        "expert_rest",
        [pltpu.VMEM(shape, BF16), pltpu.VMEM(shape, BF16), pltpu.VMEM(sq.shape, F32)],
        (me,),
        (*pieces, gain_inv, w, pre, sq, down, *weights),
        after,
    )


def bit_reversed(count):
    bits = count.bit_length() - 1
    return [int(format(n, "b").zfill(bits)[::-1], 2) if bits else 0 for n in range(count)]


def add(a, b):
    return (a.astype(F32) + b.astype(F32)).astype(BF16)


def half_sum_kernel(a_ref, b_ref, *refs):
    keep_ref, send_ref = refs[-2:]
    half = a_ref.shape[0] // 2
    keep_ref[...] = add(a_ref[:half], b_ref[:half])
    send_ref[...] = add(a_ref[half:], b_ref[half:])


def half_sum(a, b, after=()):
    shape = (a.shape[0] // 2, *a.shape[1:])
    return call(
        half_sum_kernel,
        "half_sum",
        [pltpu.VMEM(shape, BF16), pltpu.VMEM(shape, BF16)],
        (),
        (a, b),
        after,
    )


def last_sum_kernel(a_ref, b_ref, *outs):
    for z, ref in enumerate(outs):
        ref[...] = add(a_ref[0, z], b_ref[0, z])


def last_sum(a, b):
    _, zs, rows, width = a.shape
    return call(last_sum_kernel, "last_sum", [pltpu.VMEM((rows, width), BF16)] * zs, (), (a, b))


def each_sum_kernel(a_ref, b_ref, *refs):
    for n, ref in enumerate(refs):
        ref[...] = add(a_ref[n], b_ref[n])


def each_sum(a, b):
    return call(each_sum_kernel, "each_sum", [pltpu.VMEM(a.shape[1:], BF16)] * a.shape[0], (), (a, b))


def finish_kernel(count, *refs):
    total = refs[0][...]
    for ref in refs[1:count]:
        total = total + ref[...].astype(F32)
    refs[-1][...] = total.astype(BF16)


def finish(base, slab, received, after):
    arrays = (base, slab, *received)
    [out] = call(
        functools.partial(finish_kernel, len(arrays)),
        "finish",
        [jax.ShapeDtypeStruct(base.shape, BF16)],
        (),
        arrays,
        after,
    )
    return out


def open_kernel(a_ref, b_ref, keep_ref, received_ref, *refs):
    out_ref = refs[-1]
    rows = out_ref.shape[2]
    out_ref[0, 0] = a_ref[:rows, :]
    out_ref[0, 1] = b_ref[:rows, :]
    out_ref[1] = add(keep_ref[...], received_ref[...])


def open_side(a, b, keep, received, after):
    shape = (2, *keep.shape)
    [out] = call(open_kernel, "open", [pltpu.VMEM(shape, BF16)], (), (a, b, keep, received), after)
    return out


def grow_kernel(mine_ref, received_ref, *refs):
    out_ref = refs[-1]
    count = mine_ref.shape[0] - 1
    out_ref[:count] = mine_ref[:count]
    out_ref[count : 2 * count] = received_ref[:count]
    out_ref[2 * count] = add(mine_ref[count], received_ref[count])


def grow(mine, received, after):
    shape = (2 * mine.shape[0] - 1, *mine.shape[1:])
    [out] = call(grow_kernel, "grow", [pltpu.VMEM(shape, BF16)], (), (mine, received), after)
    return out


def shared_hidden_kernel(features, a_ref, b_ref, sq_ref, *refs):
    out_ref = refs[-1]
    last, chunks, rows, width = a_ref.shape
    inverse = lax.rsqrt(sq_ref[:rows, :] / features + EPS)
    pre = [
        (a_ref[last - 1, n].astype(F32) + b_ref[last - 1, n].astype(F32)) * inverse
        for n in range(chunks)
    ]
    for n in range(chunks // 2):
        columns = slice(n * width, (n + 1) * width)
        out_ref[:, columns] = (silu(pre[n]) * pre[chunks // 2 + n]).astype(BF16)


def shared_hidden(features, a, b, sq, after):
    _, chunks, rows, width = a.shape
    [out] = call(
        functools.partial(shared_hidden_kernel, features),
        "shared_hidden",
        [pltpu.VMEM((rows, chunks // 2 * width), BF16)],
        (),
        (a, b, sq),
        after,
    )
    return out


def shared_out_kernel(me_ref, a_ref, b_ref, resid_ref, w_ref, out_ref):
    part = a_ref.shape[1]
    odd = me_ref[0] % 2
    total = resid_ref[...]
    for core, ref in ((odd, a_ref), (1 - odd, b_ref)):
        total = total + dot(ref[...], w_ref[pl.ds(pl.multiple_of(core * part, part), part), :])
    out_ref[...] = total


def shared_out(me, a, b, resid, w):
    [out] = call(
        shared_out_kernel, "shared_out", [pltpu.VMEM(resid.shape, F32)], (me,), (a, b, resid, w)
    )
    return out


def on_device(
    tokens,
    states,
    router_ids,
    router_weights,
    input_gain,
    w_query,
    w_key,
    w_value,
    w_zgate,
    w_beta,
    w_alpha,
    decay_scale,
    dt_bias,
    gated_gain,
    w_out,
    post_gain,
    w_shared_in,
    w_shared_out,
    w_expert_in,
    w_expert_out,
):
    seq_count = lax.axis_size("seq")
    head_count = lax.axis_size("head")
    head_index = lax.axis_index("head")
    seq_index = lax.axis_index("seq")
    me = head_index.astype(jnp.int32).reshape(1)
    seqs, steps, width = tokens.shape
    rows = seqs * steps
    features = head_count * width
    pairs = head_count // 2
    axes = [1 << n for n in range(1, head_count.bit_length() - 1)]

    mine = jnp.transpose(tokens, (1, 0, 2)).reshape(rows, width)
    value_heads = w_beta.shape[1]
    small = jnp.concatenate([w_beta, w_alpha], axis=1)
    small = jnp.transpose(small.reshape(head_count, width, 2 * value_heads), (0, 2, 1))
    small = jnp.pad(small, ((0, 0), (0, -2 * value_heads % 16), (0, 0)))

    others = [exchange(mine, "head", 2 * p) for p in range(1, pairs)]
    mine, w_query, w_key, w_value, w_shared_in, w_shared_out, gain, pack, extra, gain_mine, gain_inv = bring(
        me,
        seq_index.astype(jnp.int32).reshape(1),
        (
            mine,
            w_query,
            w_key,
            w_value,
            w_shared_in,
            w_shared_out,
            input_gain.reshape(head_count, 1, width),
        ),
        [v.reshape(1, -1) for v in (decay_scale, dt_bias, gated_gain)],
        jnp.transpose(router_ids, (2, 1, 0)),
        jnp.transpose(router_weights, (2, 1, 0)),
        post_gain.reshape(head_count, 1, width),
        seq_count,
    )
    own_tokens = stack((mine, *others))
    sib_tokens = exchange(own_tokens, "head", 1)
    [w_zgate] = load((w_zgate,), (own_tokens,))
    gathered = (own_tokens, sib_tokens)
    own, sib, keys, deltas, totals = front(
        me, gathered, gain, small, pack, w_query, w_key, w_value, w_zgate, w_out, states, steps
    )

    merged = each_sum(own, exchange(sib, "head", 1))
    received = [exchange(merged[p], "head", 2 * p) for p in range(1, pairs)]
    [w_in] = load((w_expert_in,), (merged[0],))
    resid, x, shared_keep, sent, *messages = make_rows(
        me, merged[0], received, mine, gain_mine, extra, w_shared_in, (w_in,)
    )

    half = seq_count // 2
    messages = [exchange(m, "seq", z + 1) for z, m in enumerate(messages)]
    slabs = [x] + messages
    natural, reverse = list(range(pairs)), bit_reversed(pairs)
    blocks = tuple(range(seqs // PER_BLOCK))
    quarters = [blocks[len(blocks) * n // 4 : len(blocks) * (n + 1) // 4] for n in range(4)]
    shared_received = exchange(sent, "head", 1)
    [w_down] = load((w_expert_out,), (shared_keep,))
    if half == 2:
        side = open_side(*slabs[:2], shared_keep, shared_received, (*slabs[2:], w_down))
    else:
        rows_only = jnp.stack([m[:rows] for m in slabs[:half]])
        side = jnp.stack([rows_only, add(shared_keep, shared_received)])
    if half == 2:
        other = slab_pair(*slabs[2:], rows, ())[None]
    else:
        other = jnp.stack([m[:rows] for m in slabs[half:]])[None]
    states_out, done = update(
        keys, deltas, totals, states, quarters[0] + quarters[1], (side, other)
    )
    for bit in axes[:0:-1]:
        received = exchange(other, "head", bit)
        if other.shape[0] == 1:
            other = stack((other[0], received[0]), (done,))
        else:
            other = jnp.concatenate([other, received])
    for bit in axes[:-1]:
        side = grow(side, exchange(side, "head", bit), (done, other))
    sides = [[side, exchange(side, "head", axes[-1])]]
    sides.append([other, exchange(other, "head", axes[0])])
    siblings = [[exchange(piece, "head", 1) for piece in side] for side in sides]
    middle = pairs // 2
    orders = tuple((tuple(o[:middle]), tuple(o[middle:])) for o in (natural, reverse))

    firsts = []
    for side, order in zip(sides, orders):
        firsts.append(expert_first(me, side, gain_inv, w_in, order, (done,)))
        done = firsts[-1][1]
    owns, sibs, squares = [], [], []
    weights = (extra, *messages)
    for n, order_out in enumerate((reverse, natural)):
        own, sib, square = expert_rest(
            me,
            siblings[n],
            gain_inv,
            w_in,
            *firsts[n],
            w_down,
            weights[n * half : (n + 1) * half],
            orders[n],
            order_out,
            steps,
            n == 0,
            tuple(owns),
        )
        owns.append(own)
        sibs.append(sib)
        squares.append(square)
    received = [exchange(sib, "head", 1) for sib in sibs]
    tie = ()
    for n, bits in enumerate(zip(axes, axes[::-1])):
        for side, bit in enumerate(bits):
            owns[side], sent = half_sum(owns[side], received[side], tie)
            received[side] = exchange(sent, "head", bit)
        if n == 0:
            states_out, done = update(
                keys, deltas, totals, states, quarters[2], tuple(owns), states_out
            )
            hidden = shared_hidden(features, *sides[0], squares[0], tuple(owns))
            hidden_received = exchange(hidden, "head", 1)
            tie = (done, hidden_received)
    base = shared_out(me, hidden, hidden_received, resid, w_shared_out)
    slabs = []
    for side in range(2):
        slabs += last_sum(owns[side], received[side])
    states_out, done = update(keys, deltas, totals, states, quarters[3], (slabs[-1],), states_out)
    received = [exchange(slabs[z], "seq", z) for z in range(1, seq_count)]
    result = finish(base, slabs[0], received, (done,))
    layer_out = jnp.transpose(result.reshape(steps, seqs, width), (1, 0, 2))
    return (layer_out, states_out)


def solution(mesh):
    in_specs = (
        P("seq", None, "head"),
        P("seq", "head", None, None),
        P("seq", None, None),
        P("seq", None, None),
        P(),
        P(None, "head"),
        P(None, "head"),
        P(None, "head"),
        P(None, "head"),
        P(None, "head"),
        P(None, "head"),
        P("head"),
        P("head"),
        P(),
        P("head", None),
        P(),
        P("head", None),
        P(None, "head"),
        P(("seq", "head"), None, None),
        P(("seq", "head"), None, None),
    )
    out_specs = (P("seq", None, "head"), P("seq", "head", None, None))
    return jax.shard_map(
        on_device, mesh=mesh, in_specs=in_specs, out_specs=out_specs, check_vma=False
    )
```

```python
import functools

import jax
import jax.numpy as jnp
from jax import lax
from jax.experimental import pallas as pl
from jax.experimental.pallas import tpu as pltpu
from jax.sharding import PartitionSpec as P

DK = 128
DV = 128
EPS = 1e-06
SLOTS = 16
F32 = jnp.float32
BF16 = jnp.bfloat16
VMEM_LIMIT = 24 * 1024 * 1024


def dot(a, b):
    return jnp.dot(a, b, preferred_element_type=F32)


def silu(v):
    return v / (1.0 + jnp.exp(-v))


def split(v):
    high = v.astype(BF16)
    low = (v - high.astype(F32)).astype(BF16)
    return high, low


def pin(x):
    return pltpu.with_memory_space_constraint(x, pltpu.VMEM)


VMEM_SPEC = pl.BlockSpec(memory_space=pltpu.VMEM)
SMEM_SPEC = pl.BlockSpec(memory_space=pltpu.SMEM)
ANY_SPEC = pl.BlockSpec(memory_space=pl.ANY)


def call(body, name, out_shapes, smem, pinned, loose=(), scratch=(), aliases=None, outs=None):
    return pl.pallas_call(
        body,
        out_shape=tuple(out_shapes),
        in_specs=[SMEM_SPEC] * len(smem) + [VMEM_SPEC] * len(pinned) + [ANY_SPEC] * len(loose),
        out_specs=tuple(outs or [VMEM_SPEC] * len(out_shapes)),
        scratch_shapes=list(scratch),
        input_output_aliases=aliases or {},
        compiler_params=pltpu.CompilerParams(vmem_limit_bytes=VMEM_LIMIT),
        name=name,
    )(*smem, *(pin(x) for x in pinned), *loose)


def exchange(x, axis, bit):
    size = lax.axis_size(axis)
    return lax.ppermute(x, axis, [(i, i ^ bit) for i in range(size)])


def stack_kernel(count, *refs):
    for n, ref in enumerate(refs[:count]):
        refs[-1][n] = ref[...]


def stack(arrays, after=()):
    shape = (len(arrays), *arrays[0].shape)
    body = functools.partial(stack_kernel, len(arrays))
    [out] = call(body, "stack", [pltpu.VMEM(shape, arrays[0].dtype)], (), arrays, after)
    return out


def load_kernel(count, *refs):
    sources, targets, sems = refs[:count], refs[-1 - count : -1], refs[-1]
    copies = [pltpu.make_async_copy(a, b, sems.at[n]) for n, (a, b) in enumerate(zip(sources, targets))]
    for copy in copies:
        copy.start()
    for copy in copies:
        copy.wait()


def load(arrays, after=()):
    return call(
        functools.partial(load_kernel, len(arrays)),
        "load",
        [pltpu.VMEM(x.shape, x.dtype) for x in arrays],
        (),
        (),
        (*(pltpu.with_memory_space_constraint(x, pltpu.HBM) for x in arrays), *after),
        [pltpu.SemaphoreType.DMA((len(arrays),))],
    )


def bring_kernel(count, vectors, seq_count, head_count, me_ref, seq_ref, *refs):
    small = 3 + vectors
    sources, refs = refs[: small + count], refs[small + count :]
    targets, (pack_ref, extra_ref, gain_mine_ref, gain_inv_ref) = refs[:count], refs[count : count + 4]
    scratch, sems = refs[count + 4 : -1], refs[-1]
    ids, chosen, gain_after = scratch[:3]
    targets = (*scratch, *targets)
    copies = [pltpu.make_async_copy(a, b, sems.at[n]) for n, (a, b) in enumerate(zip(sources, targets))]
    for copy in copies:
        copy.start()
    for copy in copies[:small]:
        copy.wait()
    for n, ref in enumerate(scratch[3:]):
        pack_ref[n : n + 1, : ref.shape[1]] = ref[...]
    me, seq = me_ref[0], seq_ref[0]
    gain_mine_ref[...] = gain_after[me]
    gain_inv_ref[...] = 1.0 / gain_after[...]
    top, steps, seqs = ids.shape
    for z in range(seq_count):
        target = (seq ^ z) * head_count + me
        weight = jnp.zeros((steps, seqs), F32)
        for n in range(top):
            weight = weight + jnp.where(ids[n] == target, chosen[n], 0.0)
        high = weight.astype(BF16).astype(F32)
        both = jnp.concatenate([high, weight - high], axis=0)
        rows, width = extra_ref.shape[1:]
        both = jnp.concatenate([both, jnp.zeros((rows - 2 * steps, seqs), F32)], axis=0)
        both = jnp.concatenate([both, jnp.zeros((rows, width - seqs), F32)], axis=1)
        extra_ref[z] = both.astype(BF16)
    for copy in copies[small:]:
        copy.wait()


def bring(me, seq, arrays, vectors, ids, chosen, gain_after, seq_count):
    head_count, _, width = gain_after.shape
    small = (ids, chosen, gain_after, *vectors)
    return call(
        functools.partial(bring_kernel, len(arrays), len(vectors), seq_count, head_count),
        "bring",
        [pltpu.VMEM(x.shape, x.dtype) for x in arrays]
        + [
            pltpu.VMEM((8, 128), F32),
            pltpu.VMEM((seq_count, 16, width), BF16),
            pltpu.VMEM((1, width), F32),
            pltpu.VMEM(gain_after.shape, F32),
        ],
        (me, seq),
        (),
        [pltpu.with_memory_space_constraint(x, pltpu.HBM) for x in (*small, *arrays)],
        [pltpu.VMEM(x.shape, x.dtype) for x in small]
        + [pltpu.SemaphoreType.DMA((len(small) + len(arrays),))],
    )


def front_kernel(
    steps,
    head_count,
    me_ref,
    *refs,
):
    x_refs = refs[:2]
    (
        gain_ref,
        small_ref,
        pack_ref,
        wq,
        wk,
        wv,
        wz,
        wo_hbm,
        states_hbm,
        own_ref,
        sib_ref,
        keys_ref,
        delta_ref,
        total_ref,
        wo,
        states,
        left,
        recalls,
        sems,
    ) = refs[2:]
    me = me_ref[0]
    _, rows, width = x_refs[0].shape
    seqs = rows // steps
    key_heads = wq.shape[1] // DK
    value_heads = wv.shape[1] // DV
    group = value_heads // key_heads
    pair = group * DV

    parts = sems.shape[0] - 1
    part = seqs // parts
    copies = []
    for n in range(parts):
        span = pl.ds(n * part, part)
        copies.append(pltpu.make_async_copy(states_hbm.at[span], states.at[span], sems.at[n]))
    copies.append(pltpu.make_async_copy(wo_hbm, wo, sems.at[parts]))
    for copy in copies:
        copy.start()

    squares = jnp.zeros((rows, 1), F32)
    for j in range(head_count):
        xj = x_refs[j % 2][j // 2].astype(F32)
        squares = squares + jnp.sum(xj * xj, axis=1, keepdims=True)
    inverse = lax.rsqrt(squares / (head_count * width) + EPS)
    normed = []
    spans = []
    for j in range(head_count):
        block = me ^ j
        normed.append((x_refs[j % 2][j // 2].astype(F32) * inverse * gain_ref[block]).astype(BF16))
        spans.append(pl.ds(pl.multiple_of(block * width, width), width))

    def project(w_ref):
        total = None
        for j in range(head_count):
            term = dot(normed[j], w_ref[spans[j], :])
            total = term if total is None else total + term
        return total

    small = None
    for j in range(head_count):
        term = lax.dot_general(
            normed[j],
            small_ref[me ^ j],
            (((1,), (1,)), ((), ())),
            preferred_element_type=F32,
        )
        small = term if small is None else small + term
    betas = 1.0 / (1.0 + jnp.exp(-small[:, :value_heads]))
    alphas = small[:, value_heads : 2 * value_heads] + pack_ref[1:2, :value_heads]
    softplus = jnp.maximum(alphas, 0.0) + jnp.log1p(jnp.exp(-jnp.abs(alphas)))
    decays = jnp.exp(-pack_ref[0:1, :value_heads] * softplus)

    def units(v):
        return v * lax.rsqrt(jnp.sum(v * v, axis=1, keepdims=True) + EPS)

    queries_all = silu(project(wq))
    keys_all = silu(project(wk))
    keys, queries = [], []
    for i in range(key_heads):
        k = units(keys_all[:, i * DK : (i + 1) * DK])
        q = units(queries_all[:, i * DK : (i + 1) * DK]) * DK ** (-0.5)
        keys_ref[i] = k
        keys.append([k[t * seqs : (t + 1) * seqs] for t in range(steps)])
        queries.append([q[t * seqs : (t + 1) * seqs] for t in range(steps)])
        for t in range(steps):
            for at, v in ((t, keys[i][t]), (steps + t, queries[i][t])):
                high = v.astype(BF16).astype(F32)
                left[i, pl.ds(at, seqs, stride=SLOTS), :] = high
                left[i, pl.ds(2 * steps + at, seqs, stride=SLOTS), :] = v - high
        for at in range(4 * steps, SLOTS):
            left[i, pl.ds(at, seqs, stride=SLOTS), :] = jnp.zeros((seqs, DK), F32)
    values_all = silu(project(wv))
    gates = silu(project(wz))

    def one(s, carry):
        base = pl.multiple_of(s * SLOTS, SLOTS)
        for i in range(key_heads):
            lhs = left[i, pl.ds(base, SLOTS), :].astype(BF16)
            rhs = jnp.concatenate([states[s, i * group + u] for u in range(group)], axis=1)
            high, low = split(rhs)
            answer = dot(jnp.concatenate([lhs, lhs], axis=1), jnp.concatenate([high, low], axis=0))
            for u in range(group):
                recalls[i * group + u, pl.ds(base, SLOTS), :] = answer[:, u * DV : (u + 1) * DV]
        return carry

    for n in range(parts):
        copies[n].wait()
        lax.fori_loop(n * part, (n + 1) * part, one, 0, unroll=4)

    def wide(columns, t, i):
        return jnp.concatenate(
            [
                jnp.broadcast_to(
                    columns[t * seqs : (t + 1) * seqs, i * group + u : i * group + u + 1],
                    (seqs, DV),
                )
                for u in range(group)
            ],
            axis=1,
        )

    mixed_rows = [[] for _ in range(steps)]
    for i in range(key_heads):
        decay = [wide(decays, t, i) for t in range(steps)]
        beta = [wide(betas, t, i) for t in range(steps)]

        def read(at):
            return jnp.concatenate(
                [
                    recalls[i * group + u, pl.ds(at, seqs, stride=SLOTS), :]
                    + recalls[i * group + u, pl.ds(2 * steps + at, seqs, stride=SLOTS), :]
                    for u in range(group)
                ],
                axis=1,
            )

        deltas = []
        running = None
        for t in range(steps):
            running = decay[t] if running is None else running * decay[t]
            recall = running * read(t)
            answer = running * read(steps + t)
            deltas = [d * decay[t] for d in deltas]
            for u, d in enumerate(deltas):
                recall = recall + d * jnp.sum(keys[i][t] * keys[i][u], axis=1, keepdims=True)
                answer = answer + d * jnp.sum(queries[i][t] * keys[i][u], axis=1, keepdims=True)
            value = values_all[t * seqs : (t + 1) * seqs, i * pair : (i + 1) * pair]
            delta = beta[t] * (value - recall)
            answer = answer + delta * jnp.sum(queries[i][t] * keys[i][t], axis=1, keepdims=True)
            deltas.append(delta)
            mixed_rows[t].append(answer)
        for t in range(steps):
            delta_ref[i, t] = deltas[t]
        total_ref[i] = running
    mixed = jnp.concatenate([jnp.concatenate(m, axis=1) for m in mixed_rows], axis=0)
    gated = []
    for h in range(value_heads):
        m = mixed[:, h * DV : (h + 1) * DV]
        m = m * lax.rsqrt(jnp.mean(m * m, axis=1, keepdims=True) + EPS)
        gated.append((m * pack_ref[2:3, :DV] * gates[:, h * DV : (h + 1) * DV]).astype(BF16))
    gated = jnp.concatenate(gated, axis=1)
    copies[parts].wait()
    for c in range(head_count):
        piece = dot(gated, wo[:, c * width : (c + 1) * width]).astype(BF16)
        away = me ^ c

        @pl.when(away % 2 == 0)
        def _():
            own_ref[away // 2] = piece

        @pl.when(away % 2 == 1)
        def _():
            sib_ref[away // 2] = piece


def front(me, xs, gain, small, pack, wq, wk, wv, wz, wo, states, steps):
    pairs, rows, width = xs[0].shape
    head_count = 2 * pairs
    seqs = rows // steps
    key_heads = wq.shape[1] // DK
    value_heads = wv.shape[1] // DV
    pair = value_heads // key_heads * DV
    return call(
        functools.partial(front_kernel, steps, head_count),
        "front",
        [
            pltpu.VMEM((head_count // 2, rows, width), BF16),
            pltpu.VMEM((head_count // 2, rows, width), BF16),
            pltpu.VMEM((key_heads, rows, DK), F32),
            pltpu.VMEM((key_heads, steps, seqs, pair), F32),
            pltpu.VMEM((key_heads, seqs, pair), F32),
        ],
        (me,),
        (*xs, gain, small, pack, wq, wk, wv, wz),
        [pltpu.with_memory_space_constraint(x, pltpu.HBM) for x in (wo, states)],
        [
            pltpu.VMEM(wo.shape, BF16),
            pltpu.VMEM(states.shape, F32),
            pltpu.VMEM((key_heads, seqs * SLOTS, DK), F32),
            pltpu.VMEM((value_heads, seqs * SLOTS, DV), F32),
            pltpu.SemaphoreType.DMA((9,)),
        ],
    )


def rows_kernel(pairs, me_ref, *refs):
    merged_ref, received = refs[0], refs[1:pairs]
    mine_ref, gain_ref, extra_ref, w_ref, _ = refs[pairs : pairs + 5]
    resid_ref, x_ref, keep_ref, send_ref = refs[pairs + 5 : pairs + 9]
    messages = refs[pairs + 9 :]
    rows = mine_ref.shape[0]
    resid = mine_ref[...].astype(F32) + merged_ref[...].astype(F32)
    for ref in received:
        resid = resid + ref[...].astype(F32)
    resid_ref[...] = resid
    x = (resid * gain_ref[...]).astype(BF16)
    x_ref[...] = x
    for z, ref in enumerate(messages):
        ref[:rows, :] = x
        ref[rows:, :] = extra_ref[z + 1]
    chunks, _, width = keep_ref.shape
    half = w_ref.shape[1] // 2
    part = half // 2
    pre = dot(x, w_ref[...]).astype(BF16)
    odd = me_ref[0] % 2
    for core in range(2):
        for n in range(chunks):
            up, at = divmod(n * width, part)
            start = up * half + core * part + at
            piece = pre[:, start : start + width]

            @pl.when(odd == core)
            def _():
                keep_ref[n] = piece

            @pl.when(odd != core)
            def _():
                send_ref[n] = piece


def make_rows(me, merged, received, mine, gain, extra, w, after):
    rows, width = mine.shape
    message = pltpu.VMEM((rows + extra.shape[1], width), BF16)
    shared = pltpu.VMEM((w.shape[1] // 2 // width, rows, width), BF16)
    return call(
        functools.partial(rows_kernel, 1 + len(received)),
        "rows",
        [
            pltpu.VMEM((rows, width), F32),
            pltpu.VMEM((rows, width), BF16),
            shared,
            shared,
            *([message] * (extra.shape[0] - 1)),
        ],
        (me,),
        (merged, *received, mine, gain, extra, w),
        after,
    )


def slab_kernel(a_ref, b_ref, *refs):
    out_ref = refs[-1]
    rows = out_ref.shape[1]
    out_ref[0] = a_ref[:rows, :]
    out_ref[1] = b_ref[:rows, :]


def slab_pair(a, b, rows, after):
    [out] = call(slab_kernel, "slab", [pltpu.VMEM((2, rows, a.shape[1]), BF16)], (), (a, b), after)
    return out


PER_BLOCK = DK // SLOTS


def update_kernel(steps, blocks, keys_ref, delta_ref, total_ref, states_ref, *refs):
    out_ref, done_ref, left, right, olds, news, old_sems, sems = refs[-8:]
    half = PER_BLOCK // 2
    loads, stores = [], []
    for n, block in enumerate(blocks):
        for part in range(2):
            whole = pl.ds(block * PER_BLOCK + part * half, half)
            here = pl.ds(part * half, half)
            at = 2 * n + part
            loads.append(
                pltpu.make_async_copy(states_ref.at[whole], olds.at[n, here], old_sems.at[at])
            )
            stores.append(pltpu.make_async_copy(news.at[n, here], out_ref.at[whole], sems.at[at]))
            loads[-1].start()
    key_heads, rows, _ = keys_ref.shape
    seqs = rows // steps
    group = olds.shape[2] // key_heads
    first, count = blocks[0] * PER_BLOCK, len(blocks) * PER_BLOCK
    for i in range(key_heads):
        for at in range(SLOTS):
            rows_at = pl.ds(at, count, stride=SLOTS)
            t = at % steps
            k = keys_ref[i, t * seqs + first : t * seqs + first + count, :]
            k_high = k.astype(BF16).astype(F32)
            k = k - k_high if at >= 2 * steps else k_high
            left[i, rows_at, :] = k if at < 3 * steps else jnp.zeros_like(k)
            for u in range(group):
                d = delta_ref[i, t, first : first + count, u * DV : (u + 1) * DV]
                d_high = d.astype(BF16).astype(F32)
                d = d - d_high if steps <= at < 2 * steps else d_high
                right[i * group + u, rows_at, :] = d if at < 3 * steps else jnp.zeros_like(d)
    slot_of = lax.broadcasted_iota(jnp.int32, (DK, DK), 1) // SLOTS
    for n, block in enumerate(blocks):
        span = slice(n * DK, (n + 1) * DK)
        lhs = [jnp.transpose(left[i, span, :]) for i in range(key_heads)]
        rhs = [
            jnp.concatenate(
                [right[i * group + u, span, :] for u in range(group)], axis=1
            ).astype(BF16)
            for i in range(key_heads)
        ]
        for m in range(PER_BLOCK):
            if m % half == 0:
                loads[2 * n + m // half].wait()
            s = block * PER_BLOCK + m
            for i in range(key_heads):
                masked = jnp.where(slot_of == m, lhs[i], 0.0).astype(BF16)
                change = dot(masked, rhs[i])
                for u in range(group):
                    columns = slice(u * DV, (u + 1) * DV)
                    h = i * group + u
                    total = total_ref[i, s : s + 1, columns]
                    news[n, m, h] = olds[n, m, h] * total + change[:, columns]
            if m % half == half - 1:
                stores[2 * n + m // half].start()
    for copy in stores:
        copy.wait()
    done_ref[...] = jnp.zeros_like(done_ref)


def update(keys, deltas, totals, states, blocks, after, before=None):
    key_heads, steps, seqs, pair = deltas.shape
    rows = len(blocks) * DK
    value_heads = states.shape[1]
    loose = after if before is None else (before, *after)
    buffers = pltpu.VMEM((len(blocks), PER_BLOCK, *states.shape[1:]), F32)
    return call(
        functools.partial(update_kernel, steps, blocks),
        "update",
        [jax.ShapeDtypeStruct(states.shape, F32), jax.ShapeDtypeStruct((8, 128), F32)],
        (),
        (keys, deltas, totals),
        (pltpu.with_memory_space_constraint(states, pltpu.HBM), *loose),
        [
            pltpu.VMEM((key_heads, rows, DK), F32),
            pltpu.VMEM((value_heads, rows, DV), F32),
            buffers,
            buffers,
            pltpu.SemaphoreType.DMA((2 * len(blocks),)),
            pltpu.SemaphoreType.DMA((2 * len(blocks),)),
        ],
        None if before is None else {4: 0},
        [ANY_SPEC, VMEM_SPEC],
    )


def blocks_of(pieces, order, odd, me):
    xs, places = [], []
    for ref, part in zip(pieces, order):
        _, zs, rows, width = ref.shape
        for n, place in enumerate(part):
            xs.append(ref[n].reshape(zs * rows, width))
            places.append(me ^ (2 * place + odd))
    return xs, places


def rows_squares(xs, places, gain_inv_ref):
    squares = None
    for x, place in zip(xs, places):
        plain = x.astype(F32) * gain_inv_ref[place]
        plain = plain * plain
        for c in range(0, x.shape[1], 128):
            part = plain[:, c : c + 128]
            squares = part if squares is None else squares + part
    return jnp.sum(squares, axis=1, keepdims=True)


def columns_sum(total, xs, places, w_ref, columns):
    for x, place in zip(xs, places):
        width = x.shape[1]
        term = dot(x, w_ref[0, pl.ds(pl.multiple_of(place * width, width), width), columns])
        total = term if total is None else total + term
    return total


def expert_first_kernel(order, me_ref, *refs):
    pieces, (gain_inv_ref, w_ref) = refs[: len(order)], refs[len(order) : len(order) + 2]
    pre_ref, sq_ref = refs[-2:]
    xs, places = blocks_of(pieces, order, 0, me_ref[0])
    for c in range(0, w_ref.shape[2], 256):
        columns = slice(c, c + 256)
        pre_ref[:, columns] = columns_sum(None, xs, places, w_ref, columns)
    sq_ref[...] = rows_squares(xs, places, gain_inv_ref)


def expert_first(me, pieces, gain_inv, w, order, after=()):
    total = pieces[0].shape[1] * pieces[0].shape[2]
    return call(
        functools.partial(expert_first_kernel, order),
        "expert_first",
        [pltpu.VMEM((total, w.shape[2]), F32), pltpu.VMEM((total, 1), F32)],
        (me,),
        (*pieces, gain_inv, w),
        after,
    )


def expert_rest_kernel(order, order_out, steps, whole, me_ref, *refs):
    pieces, refs = refs[: len(order)], refs[len(order) :]
    gain_inv_ref, w_ref, pre_ref, sq_ref, down_ref = refs[:5]
    own, sib, sq_out = refs[-3:]
    me = me_ref[0]
    features = down_ref.shape[2]
    hidden_width = down_ref.shape[1]
    count, zs, rows, width = own.shape
    xs, places = blocks_of(pieces, order, 1, me)
    squares = sq_ref[...] + rows_squares(xs, places, gain_inv_ref)
    sq_out[...] = squares
    inverse = lax.rsqrt(squares / features + EPS)
    hidden = []
    for c in range(0, hidden_width, 256):
        parts = []
        for at in (c, hidden_width + c):
            columns = slice(at, at + 256)
            parts.append(columns_sum(pre_ref[:, columns], xs, places, w_ref, columns) * inverse)
        hidden.append((silu(parts[0]) * parts[1]).astype(BF16))
    hidden = jnp.concatenate(hidden, axis=1)
    weight = []
    for z in range(zs):
        ref = refs[5 + z]
        extra = ref[0] if z == 0 and whole else ref[rows:, :]
        columns = jnp.transpose(extra.astype(F32))
        for t in range(steps):
            both = columns[:, t : t + 1] + columns[:, steps + t : steps + t + 1]
            weight.append(both[: rows // steps])
    weight = jnp.concatenate(weight, axis=0)
    for odd, ref in ((1, sib), (0, own)):
        for n in range(count):
            block = me ^ (2 * order_out[n] + odd)
            columns = pl.ds(pl.multiple_of(block * width, width), width)
            result = dot(hidden, down_ref[0, :, columns]) * weight
            ref[n] = result.astype(BF16).reshape(zs, rows, width)


def expert_rest(me, pieces, gain_inv, w, pre, sq, down, weights, order, order_out, steps, whole, after):
    count = len(order_out)
    shape = (count, *pieces[0].shape[1:])
    return call(
        functools.partial(expert_rest_kernel, order, order_out, steps, whole),
        "expert_rest",
        [pltpu.VMEM(shape, BF16), pltpu.VMEM(shape, BF16), pltpu.VMEM(sq.shape, F32)],
        (me,),
        (*pieces, gain_inv, w, pre, sq, down, *weights),
        after,
    )


def bit_reversed(count):
    bits = count.bit_length() - 1
    return [int(format(n, "b").zfill(bits)[::-1], 2) if bits else 0 for n in range(count)]


def add(a, b):
    return (a.astype(F32) + b.astype(F32)).astype(BF16)


def half_sum_kernel(a_ref, b_ref, *refs):
    keep_ref, send_ref = refs[-2:]
    half = a_ref.shape[0] // 2
    keep_ref[...] = add(a_ref[:half], b_ref[:half])
    send_ref[...] = add(a_ref[half:], b_ref[half:])


def half_sum(a, b, after=()):
    shape = (a.shape[0] // 2, *a.shape[1:])
    return call(
        half_sum_kernel,
        "half_sum",
        [pltpu.VMEM(shape, BF16), pltpu.VMEM(shape, BF16)],
        (),
        (a, b),
        after,
    )


def last_sum_kernel(a_ref, b_ref, *outs):
    for z, ref in enumerate(outs):
        ref[...] = add(a_ref[0, z], b_ref[0, z])


def last_sum(a, b):
    _, zs, rows, width = a.shape
    return call(last_sum_kernel, "last_sum", [pltpu.VMEM((rows, width), BF16)] * zs, (), (a, b))


def each_sum_kernel(a_ref, b_ref, *refs):
    for n, ref in enumerate(refs):
        ref[...] = add(a_ref[n], b_ref[n])


def each_sum(a, b):
    return call(each_sum_kernel, "each_sum", [pltpu.VMEM(a.shape[1:], BF16)] * a.shape[0], (), (a, b))


def finish_kernel(count, *refs):
    total = refs[0][...]
    for ref in refs[1:count]:
        total = total + ref[...].astype(F32)
    refs[-1][...] = total.astype(BF16)


def finish(base, slab, received, after):
    arrays = (base, slab, *received)
    [out] = call(
        functools.partial(finish_kernel, len(arrays)),
        "finish",
        [jax.ShapeDtypeStruct(base.shape, BF16)],
        (),
        arrays,
        after,
    )
    return out


def open_kernel(a_ref, b_ref, keep_ref, received_ref, *refs):
    out_ref = refs[-1]
    rows = out_ref.shape[2]
    out_ref[0, 0] = a_ref[:rows, :]
    out_ref[0, 1] = b_ref[:rows, :]
    out_ref[1] = add(keep_ref[...], received_ref[...])


def open_side(a, b, keep, received, after):
    shape = (2, *keep.shape)
    [out] = call(open_kernel, "open", [pltpu.VMEM(shape, BF16)], (), (a, b, keep, received), after)
    return out


def grow_kernel(mine_ref, received_ref, *refs):
    out_ref = refs[-1]
    count = mine_ref.shape[0] - 1
    out_ref[:count] = mine_ref[:count]
    out_ref[count : 2 * count] = received_ref[:count]
    out_ref[2 * count] = add(mine_ref[count], received_ref[count])


def grow(mine, received, after):
    shape = (2 * mine.shape[0] - 1, *mine.shape[1:])
    [out] = call(grow_kernel, "grow", [pltpu.VMEM(shape, BF16)], (), (mine, received), after)
    return out


def shared_hidden_kernel(features, a_ref, b_ref, sq_ref, *refs):
    out_ref = refs[-1]
    last, chunks, rows, width = a_ref.shape
    inverse = lax.rsqrt(sq_ref[:rows, :] / features + EPS)
    pre = [
        (a_ref[last - 1, n].astype(F32) + b_ref[last - 1, n].astype(F32)) * inverse
        for n in range(chunks)
    ]
    for n in range(chunks // 2):
        columns = slice(n * width, (n + 1) * width)
        out_ref[:, columns] = (silu(pre[n]) * pre[chunks // 2 + n]).astype(BF16)


def shared_hidden(features, a, b, sq, after):
    _, chunks, rows, width = a.shape
    [out] = call(
        functools.partial(shared_hidden_kernel, features),
        "shared_hidden",
        [pltpu.VMEM((rows, chunks // 2 * width), BF16)],
        (),
        (a, b, sq),
        after,
    )
    return out


def shared_out_kernel(me_ref, a_ref, b_ref, resid_ref, w_ref, out_ref):
    part = a_ref.shape[1]
    odd = me_ref[0] % 2
    total = resid_ref[...]
    for core, ref in ((odd, a_ref), (1 - odd, b_ref)):
        total = total + dot(ref[...], w_ref[pl.ds(pl.multiple_of(core * part, part), part), :])
    out_ref[...] = total


def shared_out(me, a, b, resid, w):
    [out] = call(
        shared_out_kernel, "shared_out", [pltpu.VMEM(resid.shape, F32)], (me,), (a, b, resid, w)
    )
    return out


def on_device(
    tokens,
    states,
    router_ids,
    router_weights,
    input_gain,
    w_query,
    w_key,
    w_value,
    w_zgate,
    w_beta,
    w_alpha,
    decay_scale,
    dt_bias,
    gated_gain,
    w_out,
    post_gain,
    w_shared_in,
    w_shared_out,
    w_expert_in,
    w_expert_out,
):
    seq_count = lax.axis_size("seq")
    head_count = lax.axis_size("head")
    head_index = lax.axis_index("head")
    seq_index = lax.axis_index("seq")
    me = head_index.astype(jnp.int32).reshape(1)
    seqs, steps, width = tokens.shape
    rows = seqs * steps
    features = head_count * width
    pairs = head_count // 2
    axes = [1 << n for n in range(1, head_count.bit_length() - 1)]

    mine = jnp.transpose(tokens, (1, 0, 2)).reshape(rows, width)
    value_heads = w_beta.shape[1]
    small = jnp.concatenate([w_beta, w_alpha], axis=1)
    small = jnp.transpose(small.reshape(head_count, width, 2 * value_heads), (0, 2, 1))
    small = jnp.pad(small, ((0, 0), (0, -2 * value_heads % 16), (0, 0)))

    others = [exchange(mine, "head", 2 * p) for p in range(1, pairs)]
    mine, w_query, w_key, w_value, w_shared_in, w_shared_out, gain, pack, extra, gain_mine, gain_inv = bring(
        me,
        seq_index.astype(jnp.int32).reshape(1),
        (
            mine,
            w_query,
            w_key,
            w_value,
            w_shared_in,
            w_shared_out,
            input_gain.reshape(head_count, 1, width),
        ),
        [v.reshape(1, -1) for v in (decay_scale, dt_bias, gated_gain)],
        jnp.transpose(router_ids, (2, 1, 0)),
        jnp.transpose(router_weights, (2, 1, 0)),
        post_gain.reshape(head_count, 1, width),
        seq_count,
    )
    own_tokens = stack((mine, *others))
    sib_tokens = exchange(own_tokens, "head", 1)
    [w_zgate] = load((w_zgate,), (own_tokens,))
    gathered = (own_tokens, sib_tokens)
    own, sib, keys, deltas, totals = front(
        me, gathered, gain, small, pack, w_query, w_key, w_value, w_zgate, w_out, states, steps
    )

    merged = each_sum(own, exchange(sib, "head", 1))
    received = [exchange(merged[p], "head", 2 * p) for p in range(1, pairs)]
    [w_in] = load((w_expert_in,), (merged[0],))
    resid, x, shared_keep, sent, *messages = make_rows(
        me, merged[0], received, mine, gain_mine, extra, w_shared_in, (w_in,)
    )

    half = seq_count // 2
    messages = [exchange(m, "seq", z + 1) for z, m in enumerate(messages)]
    slabs = [x] + messages
    natural, reverse = list(range(pairs)), bit_reversed(pairs)
    blocks = tuple(range(seqs // PER_BLOCK))
    quarters = [blocks[len(blocks) * n // 4 : len(blocks) * (n + 1) // 4] for n in range(4)]
    shared_received = exchange(sent, "head", 1)
    [w_down] = load((w_expert_out,), (shared_keep,))
    if half == 2:
        side = open_side(*slabs[:2], shared_keep, shared_received, (*slabs[2:], w_down))
    else:
        rows_only = jnp.stack([m[:rows] for m in slabs[:half]])
        side = jnp.stack([rows_only, add(shared_keep, shared_received)])
    if half == 2:
        other = slab_pair(*slabs[2:], rows, ())[None]
    else:
        other = jnp.stack([m[:rows] for m in slabs[half:]])[None]
    states_out, done = update(
        keys, deltas, totals, states, quarters[0] + quarters[1], (side, other)
    )
    for bit in axes[:0:-1]:
        received = exchange(other, "head", bit)
        if other.shape[0] == 1:
            other = stack((other[0], received[0]), (done,))
        else:
            other = jnp.concatenate([other, received])
    for bit in axes[:-1]:
        side = grow(side, exchange(side, "head", bit), (done, other))
    sides = [[side, exchange(side, "head", axes[-1])]]
    sides.append([other, exchange(other, "head", axes[0])])
    siblings = [[exchange(piece, "head", 1) for piece in side] for side in sides]
    middle = pairs // 2
    orders = tuple((tuple(o[:middle]), tuple(o[middle:])) for o in (natural, reverse))

    firsts = []
    for side, order in zip(sides, orders):
        firsts.append(expert_first(me, side, gain_inv, w_in, order, (done,)))
        done = firsts[-1][1]
    owns, sibs, squares = [], [], []
    weights = (extra, *messages)
    for n, order_out in enumerate((reverse, natural)):
        own, sib, square = expert_rest(
            me,
            siblings[n],
            gain_inv,
            w_in,
            *firsts[n],
            w_down,
            weights[n * half : (n + 1) * half],
            orders[n],
            order_out,
            steps,
            n == 0,
            tuple(owns),
        )
        owns.append(own)
        sibs.append(sib)
        squares.append(square)
    received = [exchange(sib, "head", 1) for sib in sibs]
    tie = ()
    for n, bits in enumerate(zip(axes, axes[::-1])):
        for side, bit in enumerate(bits):
            owns[side], sent = half_sum(owns[side], received[side], tie)
            received[side] = exchange(sent, "head", bit)
        if n == 0:
            states_out, done = update(
                keys, deltas, totals, states, quarters[2] + quarters[3], tuple(owns), states_out
            )
            hidden = shared_hidden(features, *sides[0], squares[0], tuple(owns))
            hidden_received = exchange(hidden, "head", 1)
            tie = (done, hidden_received)
    base = shared_out(me, hidden, hidden_received, resid, w_shared_out)
    slabs = []
    for side in range(2):
        slabs += last_sum(owns[side], received[side])
    received = [exchange(slabs[z], "seq", z) for z in range(1, seq_count)]
    result = finish(base, slabs[0], received, ())
    layer_out = jnp.transpose(result.reshape(steps, seqs, width), (1, 0, 2))
    return (layer_out, states_out)


def solution(mesh):
    in_specs = (
        P("seq", None, "head"),
        P("seq", "head", None, None),
        P("seq", None, None),
        P("seq", None, None),
        P(),
        P(None, "head"),
        P(None, "head"),
        P(None, "head"),
        P(None, "head"),
        P(None, "head"),
        P(None, "head"),
        P("head"),
        P("head"),
        P(),
        P("head", None),
        P(),
        P("head", None),
        P(None, "head"),
        P(("seq", "head"), None, None),
        P(("seq", "head"), None, None),
    )
    out_specs = (P("seq", None, "head"), P("seq", "head", None, None))
    return jax.shard_map(
        on_device, mesh=mesh, in_specs=in_specs, out_specs=out_specs, check_vma=False
    )
```
